32 devices in a mesh: img: 8 (over z, y), cls: 4 (over x, core).
Axes of the slice: x: 2, y: 2, z: 4, core: 2. Of those that a mesh axis runs over, the one named last changes fastest.
Arguments:
- patches: bfloat16 [16, 64, 18432], P('img', 'cls'), may hold values from -6 to 6
- boxes: int32 [16, 3, 4], P('img'), may hold values from 0 to 96, as said below
- match: int32 [16, 9, 6144], P('img'), may hold values from -2 to 15, as said below
- gt_labels: int32 [16, 16], P('img'), may hold values from 0 to 79
- gt_deltas: float32 [16, 16, 4], P('img'), may hold values from -4 to 4
- ema_old: float32 [], replicated, may hold values from 9830.4 to 39321.6
- shared_params: float32 [1378304], P(('img', 'cls'))
- shared_m: float32 [1378304], P(('img', 'cls')), may hold values from -0.0048828125 to 0.0048828125
- shared_v: float32 [1378304], P(('img', 'cls')), may hold values from 5.086263e-08 to 8.138021e-07
- class_params: float32 [2304, 720], P('img', 'cls'), may hold values from -0.125 to 0.125
- class_m: float32 [2304, 720], P('img', 'cls'), may hold values from -0.00048828125 to 0.00048828125
- class_v: float32 [2304, 720], P('img', 'cls'), may hold values from 5.086263e-10 to 8.138021e-09
Outputs:
- loss: float32 [], replicated
- ema: float32 [], replicated
- shared_new: float32 [1378304], P(('img', 'cls'))
- shared_m_new: float32 [1378304], P(('img', 'cls'))
- shared_v_new: float32 [1378304], P(('img', 'cls'))
- class_new: float32 [2304, 720], P('img', 'cls')
- class_m_new: float32 [2304, 720], P('img', 'cls')
- class_v_new: float32 [2304, 720], P('img', 'cls')
The draws below stay inside these ranges and needn't reach their ends.
Inputs may be any that keep to these rules, and one draw needn't show every extreme that they name: `boxes`: crops of a canvas are disjoint; crop 0 covers every row of its canvas. `match`: -1 marks background, -2 an ignored anchor, other values the index of the matched ground-truth box.
All inputs are finite; a program needn't handle non-finite values.
Results may differ from the reference program's by a relative error of at most 0.011.
The reference program's roundings to bfloat16 on the way count: a program that leaves them out, or rounds other values in their place, can miss the bound.
Values may be sent and summed in bfloat16 or wider, within the bound.
A program may use at most 320 MiB of HBM per device.

```python
import math
import jax
import jax.numpy as jnp
from jax import lax

C = 256
CLASSES = 80
ANCH = 9
PATCH = 192
CLS_OUT = 720
BOX_OUT = 36
HC = 64
WC = 96
GT = 16
STEP = 5
CANVASES = 16
P_SHARED = 1378304


def draw_boxes(key, part):
    key = jax.random.fold_in(key, 1)
    streams = jax.random.split(key, 3)
    margin_top = min(4, HC // 8, WC // 8) + 1
    cut_col = jax.random.randint(streams[0], (CANVASES,), WC // 4, 3 * WC // 4 + 1)
    cut_row = jax.random.randint(streams[1], (CANVASES,), HC // 4, 3 * HC // 4 + 1)
    margin = jax.random.randint(streams[2], (CANVASES, 7), 0, margin_top)
    first = jnp.stack([jnp.zeros_like(cut_col), margin[:, 0], jnp.full_like(cut_col, HC), cut_col], -1)
    second = jnp.stack([margin[:, 1], cut_col + margin[:, 2], cut_row, WC - margin[:, 3]], -1)
    third = jnp.stack([cut_row + margin[:, 4], cut_col + margin[:, 5], HC - margin[:, 6], WC - margin[:, 3]], -1)
    return jnp.stack([first, second, third], 1).astype(jnp.int32)


def draw_match(key, part):
    key = jax.random.fold_in(key, 2)
    streams = jax.random.split(key, 2)
    shape = (CANVASES, ANCH, HC * WC)
    roll = jax.random.randint(streams[0], shape, 0, 1000)
    which = jax.random.randint(streams[1], shape, 0, GT)
    last = max(CANVASES - 1, 1)
    canvas = lax.broadcasted_iota(jnp.int32, shape, 0)
    row_index = lax.broadcasted_iota(jnp.int32, shape, 2) // WC
    limit = 10 * (last + 2 * canvas) * (HC + 2 * row_index) // (last * HC)
    return jnp.where(roll < limit, which, jnp.where(roll < limit + 50, -2, -1)).astype(jnp.int32)


def draw_shared_params(key, part):
    key = jax.random.fold_in(key, 3)
    position = lax.iota(jnp.int32, P_SHARED)
    lengths = [PATCH * C, C, C * C, C, 18 * C * C, 2 * C, 9 * C * BOX_OUT]
    spreads = [PATCH ** (-0.5), 0.3, C ** (-0.5), 0.3, (9 * C) ** (-0.5), 0.3, (9 * C) ** (-0.5)]
    spread_all = jnp.zeros((P_SHARED,), jnp.float32)
    offset = 0
    for length, spread in zip(lengths, spreads):
        spread_all = jnp.where((position >= offset) & (position < offset + length), spread, spread_all)
        offset = offset + length
    noise = jax.random.normal(key, (P_SHARED,), jnp.float32)
    return noise * spread_all


def touch_ends(drawn, rng, smallest, top_value):
    shape = drawn.shape
    place = [jax.random.randint(jax.random.fold_in(rng, axis), (), 0, shape[axis]) for axis in range(len(shape))]
    drawn = drawn.at[tuple(place)].set(smallest)
    longest = shape.index(max(shape))
    place[longest] = (place[longest] + 1) % shape[longest]
    return drawn.at[tuple(place)].set(top_value)


def levels(stream_key, shape, cuts, least, largest):
    def one(axis_at, parts):
        heights = jax.random.uniform(jax.random.fold_in(jax.random.fold_in(stream_key, 6), axis_at), (parts,), jnp.float32, least / len(cuts), largest / len(cuts))
        return jnp.repeat(jnp.exp(heights), shape[axis_at] // parts).reshape((-1,) + (1,) * (len(shape) - axis_at - 1))

    factor_of = one(*cuts[0])
    for cut in cuts[1:]:
        factor_of = factor_of * one(*cut)
    return factor_of


def centred(own_key, dims, scale, bound, cuts=(), held_as=jnp.bfloat16):
    gain = levels(own_key, dims, cuts, -0.22, 0.18) if cuts else 1.0
    values = jax.random.normal(own_key, dims, jnp.float32) * scale * gain
    return jnp.minimum(jnp.maximum(values, -bound), bound).astype(held_as)


def setup_inputs(seed: int = 0) -> dict:
    keys = jax.random.split(jax.random.key(seed), 13)
    return {
        "patches": centred(keys[0], (CANVASES, HC, WC * PATCH), 1.0, 6.0, ((0, 8), (1, 4))),
        "boxes": draw_boxes(jax.random.fold_in(keys[12], 71), 0),
        "match": draw_match(jax.random.fold_in(keys[12], 71), 0),
        "gt_labels": touch_ends(jax.random.randint(keys[3], (CANVASES, GT), 0, CLASSES), jax.random.fold_in(keys[3], 1), 0, CLASSES - 1).astype(jnp.int32),
        "gt_deltas": centred(keys[4], (CANVASES, GT, 4), 1.0, 4.0, ((0, 8),), jnp.float32),
        "ema_old": jnp.clip(jax.random.uniform(keys[5], (), jnp.float32, 9830.4, 39321.6), 9830.4, 39321.6),
        "shared_params": draw_shared_params(jax.random.fold_in(keys[12], 71), 0),
        "shared_m": centred(keys[7], (P_SHARED,), (0.1 * (CANVASES * HC * WC) ** -0.5), 0.0048828125, ((0, 32),), jnp.float32),
        "shared_v": jnp.clip(jnp.exp(math.log(8.138021030390519e-07) - 2.7725887 * jax.random.uniform(keys[8], (P_SHARED,), jnp.float32) ** levels(keys[8], (P_SHARED,), ((0, 32),), -0.2, 0.2)), 5.086263143994074e-08, 8.138021030390519e-07),
        "class_params": centred(keys[9], (9 * C, CLS_OUT), (9 * C) ** -0.5, 0.125, ((0, 8), (1, 4)), jnp.float32),
        "class_m": centred(keys[10], (9 * C, CLS_OUT), (0.01 * (CANVASES * HC * WC) ** -0.5), 0.00048828125, ((0, 8), (1, 4)), jnp.float32),
        "class_v": jnp.clip(jnp.exp(math.log(8.138020923809108e-09) - 2.7725887 * jax.random.uniform(keys[11], (9 * C, CLS_OUT), jnp.float32) ** levels(keys[11], (9 * C, CLS_OUT), ((0, 8), (1, 4)), -0.2, 0.2)), 5.086263077380693e-10, 8.138020923809108e-09),
    }


PRECISE = lax.Precision.HIGHEST
PRIOR = -4.59511985013459
ALPHA = 0.25
HUBER = 1.0 / 9.0
EMA_KEEP = 0.9
RATE = 0.01
MOMENT_ONE = 0.5
MOMENT_TWO = 0.5
DECAY = 0.05
EPSILON = 1e-08

@jax.custom_vjp
def low(v):
    return lax.optimization_barrier(v.astype(jnp.bfloat16)).astype(jnp.float32)

@jax.custom_vjp
def low_back(v):
    return v

def low_keep(v):
    return (low(v), None)

def low_pass(kept, grad):
    return (grad,)

def back_keep(v):
    return (v, None)

def back_low(kept, grad):
    return (low(grad),)
low.defvjp(low_keep, low_pass)
low_back.defvjp(back_keep, back_low)

def crop_map(boxes, row_count, col_count):
    row_index = jnp.arange(row_count, dtype=jnp.int32)[:, None, None]
    col_index = jnp.arange(col_count, dtype=jnp.int32)[None, :, None]
    edges = boxes[..., None, None, :, :]
    inside = (row_index >= edges[..., 0]) & (row_index < edges[..., 2]) & (col_index >= edges[..., 1]) & (col_index < edges[..., 3])
    number = jnp.arange(boxes.shape[-2], dtype=jnp.int32)
    return lax.optimization_barrier(jnp.max(jnp.where(inside, number, -1), axis=-1)).astype(jnp.int32)

def unpack(flat_values):
    lengths = [PATCH * C, C, C * C, C, 18 * C * C, 2 * C, 9 * C * BOX_OUT]
    pieces = []
    offset = 0
    for length in lengths:
        pieces.append(flat_values[offset:offset + length])
        offset = offset + length
    return (pieces[0].reshape(PATCH, C), pieces[1], pieces[2].reshape(C, C), pieces[3], pieces[4].reshape(2, 9, C, C), pieces[5].reshape(2, C), pieces[6].reshape(9, C, BOX_OUT))

def targets(crop_ids, match, labels, deltas):
    valid = (crop_ids >= 0)[..., None]
    positive = (match >= 0) & valid
    counted = (match != -2) & valid
    onehot = match[..., None] == jnp.arange(GT, dtype=jnp.int32)
    matched_label = lax.optimization_barrier(jnp.sum(jnp.where(onehot, labels[..., None, None, None, :], 0), axis=-1)).astype(jnp.int32)
    matched_label = jnp.where(positive, matched_label, -1)
    box_target = jnp.einsum('...rwag,...gk->...rwak', onehot.astype(jnp.float32), deltas, precision=PRECISE)
    return (positive, counted, matched_label, box_target.reshape(box_target.shape[:-2] + (4 * ANCH,)))

def focal_sum(logit_in, target, weighting):
    prob = jax.nn.sigmoid(logit_in)
    cross = jax.nn.softplus(logit_in) - target * logit_in
    miss = prob + target - 2.0 * prob * target
    balance = ALPHA * target + (1.0 - ALPHA) * (1.0 - target)
    return jnp.sum(weighting * balance * miss * miss * cross)

def huber_sum(differ, weighting):
    magnitude = jnp.abs(differ)
    return jnp.sum(weighting * jnp.where(magnitude < HUBER, 0.5 * differ * differ / HUBER, magnitude - 0.5 * HUBER))

def masked_conv(inputs, taps, crop_ids):
    row_count, col_count = crop_ids.shape
    padded = jnp.pad(inputs, ((1, 1), (1, 1), (0, 0)))
    padded_ids = jnp.pad(crop_ids, 1, constant_values=-1)
    summed = jnp.zeros((row_count, col_count, taps.shape[-1]), jnp.float32)
    for row_tap in range(3):
        for col_tap in range(3):
            same = (padded_ids[row_tap:row_tap + row_count, col_tap:col_tap + col_count] == crop_ids) & (crop_ids >= 0)
            masked_in = jnp.where(same[..., None], padded[row_tap:row_tap + row_count, col_tap:col_tap + col_count], 0.0)
            summed = summed + jnp.einsum('rwc,co->rwo', masked_in, taps[row_tap * 3 + col_tap], precision=PRECISE)
    return summed

def canvas_sums(weights, canvas_data):
    stem_w, stem_b, lat_w, lat_b, tower_w, tower_b, box_w, class_w = weights
    patch, crop_ids, match, labels, deltas = canvas_data
    stem_pre = low_back(jnp.einsum('rwp,pc->rwc', patch, stem_w, precision=PRECISE) + stem_b)
    stem_out = low(jax.nn.gelu(stem_pre))
    feature = low(low_back(jnp.einsum('rwc,cd->rwd', stem_out, lat_w, precision=PRECISE) + lat_b))
    class_pre = low_back(masked_conv(feature, tower_w[0], crop_ids) + tower_b[0])
    box_pre = low_back(masked_conv(feature, tower_w[1], crop_ids) + tower_b[1])
    class_tower = low(jax.nn.gelu(class_pre))
    box_tower = low(jax.nn.gelu(box_pre))
    logits = low_back(masked_conv(class_tower, class_w, crop_ids) + PRIOR)
    predicted = low_back(masked_conv(box_tower, box_w, crop_ids))
    positive, counted, matched_label, box_target = targets(crop_ids, match, labels, deltas)
    class_target = (matched_label[..., None] == jnp.arange(CLASSES, dtype=jnp.int32)).astype(jnp.float32).reshape(logits.shape)
    class_weight = jnp.broadcast_to(counted[..., None], counted.shape + (CLASSES,)).astype(jnp.float32).reshape(logits.shape)
    box_weight = jnp.repeat(positive, 4, axis=-1).astype(jnp.float32)
    return (focal_sum(logits, class_target, class_weight), huber_sum(predicted - box_target, box_weight))

def adamw_update(weight, first, second, grad):
    first_new = MOMENT_ONE * first + (1.0 - MOMENT_ONE) * grad
    second_new = MOMENT_TWO * second + (1.0 - MOMENT_TWO) * grad * grad
    first_hat = first_new / (1.0 - MOMENT_ONE ** STEP)
    second_hat = second_new / (1.0 - MOMENT_TWO ** STEP)
    weight_new = weight - RATE * (first_hat / (jnp.sqrt(second_hat) + EPSILON) + DECAY * weight)
    return (weight_new, first_new, second_new)

def reference(patches, boxes, match, gt_labels, gt_deltas, ema_old, shared_params, shared_m, shared_v, class_params, class_m, class_v):
    crop_ids = crop_map(boxes, HC, WC)
    match_cells = jnp.transpose(match.reshape(CANVASES, ANCH, HC, WC), (0, 2, 3, 1))
    positives = jnp.sum(((match_cells >= 0) & (crop_ids[..., None] >= 0)).astype(jnp.int32)).astype(jnp.float32)
    ema_new = EMA_KEEP * ema_old + (1.0 - EMA_KEEP) * jnp.maximum(positives, 1.0)
    box_norm = jnp.maximum(positives, 1.0)
    patch_values = patches.astype(jnp.float32).reshape(CANVASES, HC, WC, PATCH)

    def loss_fn(flat_values, class_values):
        weights = unpack(low(flat_values)) + (low(class_values).reshape(9, C, CLS_OUT),)

        def advance(running, canvas_data):
            focal_part, huber_part = jax.checkpoint(canvas_sums)(weights, canvas_data)
            return ((running[0] + focal_part, running[1] + huber_part), None)
        start = (jnp.zeros((), jnp.float32), jnp.zeros((), jnp.float32))
        (focal_total, huber_total), _ = lax.scan(advance, start, (patch_values, crop_ids, match_cells, gt_labels, gt_deltas))
        return focal_total / ema_new + huber_total / box_norm
    loss_value, pull = jax.vjp(loss_fn, shared_params, class_params)
    shared_grad, class_grad = pull(jnp.ones((), jnp.float32))
    shared_new, shared_m_new, shared_v_new = adamw_update(shared_params, shared_m, shared_v, shared_grad)
    class_new, class_m_new, class_v_new = adamw_update(class_params, class_m, class_v, class_grad)
    return (loss_value, ema_new, shared_new, shared_m_new, shared_v_new, class_new, class_m_new, class_v_new)
```

```python
import functools

import jax
import jax.numpy as jnp
from jax import lax
from jax.experimental import pallas as pl
from jax.experimental.pallas import tpu as pltpu
from jax.sharding import PartitionSpec as P

C = 256
CLASSES = 80
ANCH = 9
PATCH = 192
BOX_OUT = 36
CLS_OUT = ANCH * CLASSES
STEP = 5
GT = 16
HALO = 4
SLOT = 16
BOX_ROWS = 4 * SLOT
LANE = 128
WIDE = 768

PRIOR = -4.59511985013459
ALPHA = 0.25
HUBER = 1.0 / 9.0
EMA_KEEP = 0.9
RATE = 0.01
MOMENT_ONE = 0.5
MOMENT_TWO = 0.5
DECAY = 0.05
EPSILON = 1e-08

BF = jnp.bfloat16
F32 = jnp.float32
TAPS = [(di, dj) for di in (-1, 0, 1) for dj in (-1, 0, 1)]
NN = (((1,), (0,)), ((), ()))
NT = (((1,), (1,)), ((), ()))
TN = (((0,), (0,)), ((), ()))
K0 = 0.7978845608028654
K1 = 0.044715


def mm(a, b, dims=NN):
    return lax.dot_general(a, b, dims, preferred_element_type=F32)


def gelu(x):
    return 0.5 * x * (1.0 + jnp.tanh(K0 * (x + K1 * x * x * x)))


def gelu_slope(x):
    square = x * x
    th = jnp.tanh(K0 * (x + K1 * x * square))
    return 0.5 * (1.0 + th) + (0.5 * K0) * x * (1.0 - th * th) * (1.0 + 3.0 * K1 * square)


def columns_of(x, pairs, width):
    return [x[:, width * k : width * (k + 1)] for k in range(pairs)]


def stem_kernel(pairs, cols, rows, x_ref, h_ref, w_ref, b_ref, lw_ref, lb_ref, pre_ref, so_ref, f_ref, t_ref):
    step = pl.program_id(0)
    canvases = x_ref.shape[0]
    own_rows = canvases * rows
    total = (rows + 2 * HALO) * cols

    @pl.when(step == 0)
    def _():
        for c in range(canvases):
            for n in range(2):
                t_ref[c, n, 0:8, :] = jnp.zeros((8, LANE), F32)
                t_ref[c, n, 8 + total : 16 + total, :] = jnp.zeros((8, LANE), F32)

    x = x_ref[...].reshape(own_rows, x_ref.shape[2])
    own = columns_of(x, pairs, 2 * PATCH)
    rim = columns_of(h_ref[...], pairs, 2 * PATCH)
    pre = mm(jnp.concatenate(own + rim, axis=0), w_ref[...]) + b_ref[...]
    count = pairs * own_rows
    pre_ref[...] = pre[:count]
    out = gelu(pre).astype(BF)
    so_ref[...] = out[:count]
    for half in range(2):
        feat = mm(out[:, half * C : half * C + C], lw_ref[...]) + lb_ref[...]
        for k in range(pairs):
            j = step * 2 * pairs + 2 * k + half
            for c in range(canvases):
                at = k * own_rows + c * rows
                rim_at = count + k * 2 * HALO * canvases + c * 2 * HALO
                for n in range(2):
                    side = slice(n * LANE, n * LANE + LANE)
                    place = pl.ds(8 + HALO * cols + j, rows, stride=cols)
                    t_ref[c, n, place, :] = feat[at : at + rows, side]
                    place = pl.ds(8 + j, HALO, stride=cols)
                    t_ref[c, n, place, :] = feat[rim_at : rim_at + HALO, side]
                    place = pl.ds(8 + (HALO + rows) * cols + j, HALO, stride=cols)
                    t_ref[c, n, place, :] = feat[rim_at + HALO : rim_at + 2 * HALO, side]

    @pl.when(step == pl.num_programs(0) - 1)
    def _():
        piece = 4 * cols

        def move(i, carry):
            base = pl.multiple_of(i * piece, 16)
            for c in range(canvases):
                for n in range(2):
                    value = t_ref[c, n, pl.ds(base, piece + 16), :]
                    for k in range(3):
                        moved = value[7 + k : 7 + k + piece].astype(BF)
                        f_ref[c, k, pl.ds(base, piece), n * LANE : n * LANE + LANE] = moved
            return carry

        lax.fori_loop(0, total // piece, move, 0)


def stem_back_kernel(pairs, cols, rows, x_ref, fg_ref, so_ref, pre_ref, lw_ref, sw_out, sb_out, lw_out, lb_out):
    step = pl.program_id(0)
    canvases = x_ref.shape[0]

    @pl.when(step == 0)
    def _():
        sw_out[...] = jnp.zeros_like(sw_out)
        sb_out[...] = jnp.zeros_like(sb_out)
        lw_out[...] = jnp.zeros_like(lw_out)
        lb_out[...] = jnp.zeros_like(lb_out)

    x = x_ref[...].reshape(canvases * rows, x_ref.shape[2])
    own = jnp.concatenate(columns_of(x, pairs, 2 * PATCH), axis=0)
    low = []
    for half in range(2):
        parts = []
        for k in range(pairs):
            j = step * 2 * pairs + 2 * k + half
            for c in range(canvases):
                place = pl.ds(j, rows, stride=cols)
                parts.append(jnp.concatenate([fg_ref[c, n, place, :] for n in range(2)], axis=1))
        grad32 = jnp.concatenate(parts, axis=0)
        grad = grad32.astype(BF)
        cut = slice(half * C, half * C + C)
        lw_out[...] += mm(so_ref[:, cut], grad, TN)
        lb_out[...] += jnp.sum(grad32, axis=0, keepdims=True)
        back = mm(grad, lw_ref[...], NT) * gelu_slope(pre_ref[:, cut])
        back = back.astype(BF)
        sb_out[...] += jnp.sum(back.astype(F32), axis=0, keepdims=True)
        low.append(back)
    both = mm(own, jnp.concatenate(low, axis=1), TN)
    sw_out[...] += both[:PATCH, :C] + both[PATCH:, C:]


def head_kernel(
    cols, rows, scal_ref, f_ref, mk_ref, lab_ref, btt_ref, e_ref, wt_ref, tb_ref, wct_ref, wb_ref,
    dwc_ref, dwt_ref, dwb_ref, db_ref, fg_ref, sums_ref,
    mx_ref, x_ref, pre_ref, bt_ref, lgt_ref, lgs_ref, lg_ref, g_ref,
):
    own = rows * cols
    edge = HALO * cols
    total = own + 2 * edge
    shift = [cols * di + dj for di, dj in TAPS]

    @pl.when(pl.program_id(0) == 0)
    def _():
        dwc_ref[...] = jnp.zeros_like(dwc_ref)
        dwt_ref[...] = jnp.zeros_like(dwt_ref)
        dwb_ref[...] = jnp.zeros_like(dwb_ref)
        db_ref[...] = jnp.zeros_like(db_ref)
        sums_ref[...] = jnp.zeros_like(sums_ref)
        lg_ref[CLS_OUT:, :] = jnp.zeros((WIDE - CLS_OUT, 256), F32)

    def spread(i, carry):
        at = pl.multiple_of(i * 384, 128)
        wide = mm(mk_ref[0, :, pl.ds(at, 384)], e_ref[...], TN).astype(BF)
        for t in range(9):
            mx_ref[t, pl.ds(at, 384), :] = wide[:, t * LANE : (t + 1) * LANE]
        return carry

    lax.fori_loop(0, total // 384, spread, 0)

    def twice(mask):
        return jnp.concatenate([mask, mask], axis=1)

    def build(source, at, count, row):
        for t, (di, dj) in enumerate(TAPS):
            value = source[dj + 1, pl.ds(at + cols * di, count), :]
            x_ref[pl.ds(row, count), t * C : (t + 1) * C] = value * twice(mx_ref[t, pl.ds(at, count), :])

    first_tower = cols
    tower_rows = total - 2 * cols
    first_logit = edge - 256
    logit_cells = own + 512
    first_g = edge - 128
    g_cells = own + 256

    def heads(ct32_ref, ct_ref):
        zero = jnp.zeros((cols + 8, C), F32)
        ct32_ref[0 : cols + 8, :] = zero
        ct32_ref[8 + total - cols : 16 + total, :] = zero
        zero = jnp.zeros((cols, C), BF)
        bt_ref[0:cols, :] = zero
        bt_ref[total - cols : total, :] = zero
        piece = tower_rows // 3

        def tower(i, carry):
            row = pl.multiple_of(i * piece, 16)
            at = pl.multiple_of(first_tower + i * piece, 16)
            build(f_ref.at[0], at, piece, row)
            pre = mm(x_ref[pl.ds(row, piece), :], wt_ref[...]) + tb_ref[...]
            pre_ref[pl.ds(row, piece), :] = pre
            out = gelu(pre)
            ct32_ref[pl.ds(pl.multiple_of(8 + at, 8), piece), :] = out[:, :C]
            bt_ref[pl.ds(at, piece), :] = out[:, C:].astype(BF)
            return carry

        lax.fori_loop(0, 3, tower, 0)

        def move(i, carry):
            base = pl.multiple_of(i * edge, 16)
            value = ct32_ref[pl.ds(base, edge + 16), :]
            for k in range(3):
                ct_ref[k, pl.ds(base, edge), :] = value[7 + k : 7 + k + edge].astype(BF)
            return carry

        lax.fori_loop(0, total // edge, move, 0)
        inv_ema = scal_ref[0]
        number = lax.broadcasted_iota(jnp.int32, (CLASSES, 256), 0).astype(F32)
        lane = lax.broadcasted_iota(jnp.int32, (8, 256), 1)

        def logits(q, carry):
            row = pl.multiple_of(q * 256, 128)
            at = pl.multiple_of(first_logit + q * 256, 128)
            build(ct_ref, at, 256, row)
            lg_ref[0:CLS_OUT, :] = mm(wct_ref[...], x_ref[pl.ds(row, 256), :], NT) + PRIOR
            place = lane + at
            mine = ((place >= edge) & (place < edge + own)).astype(F32)

            def focal(a, total_focal):
                here = pl.multiple_of(a * CLASSES, 16)
                value = lg_ref[pl.ds(here, CLASSES), :]
                label = jnp.broadcast_to(lab_ref[0, pl.ds(a, 1), pl.ds(at, 256)], (CLASSES, 256))
                hit = label == number
                side = jnp.where(hit, -value, value)
                small = jnp.exp(-jnp.abs(side))
                ratio = 1.0 / (1.0 + small)
                tiny = small * (1.0 - small * (0.5 - small * (1.0 / 3.0)))
                cross = jnp.maximum(side, 0.0) + jnp.where(small < 0.01, tiny, jnp.log(1.0 + small))
                prob = jnp.where(side >= 0.0, ratio, small * ratio)
                square = prob * prob
                weight = jnp.where(hit, ALPHA, 1.0 - ALPHA)
                weight = jnp.where(label > -1.5, weight, 0.0)
                loss = weight * square * cross
                pull = weight * square * (2.0 * (1.0 - prob) * cross + prob) * inv_ema
                pull = jnp.where(hit, -pull, pull)
                lg_ref[pl.ds(here, CLASSES), :] = pull
                lgt_ref[pl.ds(here, CLASSES), pl.ds(row, 256)] = pull.astype(BF)
                return total_focal + jnp.sum(loss.reshape(CLASSES // 8, 8, 256), axis=0)

            sums_ref[0:8, :] += lax.fori_loop(0, ANCH, focal, jnp.zeros((8, 256), F32)) * mine
            lgs_ref[pl.ds(row, 256), :] = lg_ref[...].T.astype(BF)
            return carry

        lax.fori_loop(0, logit_cells // 256, logits, 0)

        def class_weights(i, carry):
            at = pl.multiple_of(i * 256, 128)
            dwc_ref[:, pl.ds(at, 256)] += mm(lgt_ref[:, 256 : 256 + own], x_ref[256 : 256 + own, pl.ds(at, 256)])
            return carry

        lax.fori_loop(0, 9, class_weights, 0)

    pl.run_scoped(heads, pltpu.VMEM((total + 16, C), F32), pltpu.VMEM((3, total, C), BF))

    def boxes(y_ref, gg_ref, xg_ref):
        inv_norm = scal_ref[1]

        def outer(i, carry):
            at = pl.multiple_of(i * 768, 128)
            y_ref[:, pl.ds(at, 768)] = mm(wb_ref[...], bt_ref[pl.ds(at, 768), :], NT)
            return carry

        lax.fori_loop(0, total // 768, outer, 0)
        lane = lax.broadcasted_iota(jnp.int32, (SLOT, total), 1)
        mine = (lane >= edge) & (lane < edge + own)

        def guess(m, carry):
            acc = jnp.zeros((SLOT, total), F32)
            for t in range(9):
                value = y_ref[pl.ds(pl.multiple_of(t * BOX_ROWS + m * SLOT, 8), SLOT), :]
                moved = pltpu.roll(value, (-shift[t]) % total, 1)
                acc += moved * mk_ref[0, t : t + 1, :].astype(F32)
            differ = acc - btt_ref[0, m]
            positive = lab_ref[0] >= 0.0
            size = jnp.abs(differ)
            loss = jnp.where(size < HUBER, 0.5 * differ * differ / HUBER, size - 0.5 * HUBER)
            loss = jnp.where(positive & mine, loss, 0.0)
            part = loss[:, 0:256]
            for k in range(1, total // 256):
                part += loss[:, k * 256 : (k + 1) * 256]
            sums_ref[8:16, :] += part[0:8] + part[8:16]
            pull = jnp.minimum(jnp.maximum(differ / HUBER, -1.0), 1.0) * inv_norm
            pull = jnp.where(positive, pull, 0.0)
            gg_ref[pl.ds(pl.multiple_of(m * SLOT, 8), SLOT), :] = pull
            return carry

        lax.fori_loop(0, 4, guess, 0)
        for t in range(9):
            moved = pltpu.roll(gg_ref[...], shift[t] % total, 1)
            xg_ref[t * BOX_ROWS : (t + 1) * BOX_ROWS, :] = (moved * mk_ref[0, 8 - t : 9 - t, :].astype(F32)).astype(BF)
        dwb_ref[...] += mm(xg_ref[:, edge : edge + own], bt_ref[edge : edge + own, :])

        def into(q, carry):
            row = pl.multiple_of(q * 256, 128)
            grad = mm(xg_ref[:, pl.ds(pl.multiple_of(first_g + row, 128), 256)], wb_ref[...], TN)
            pre = pre_ref[pl.ds(pl.multiple_of(first_g - first_tower + row, 16), 256), C:]
            g_ref[pl.ds(row, 256), C:] = (grad * gelu_slope(pre)).astype(BF)
            return carry

        lax.fori_loop(0, g_cells // 256, into, 0)

    pl.run_scoped(
        boxes,
        pltpu.VMEM((9 * BOX_ROWS, total), F32),
        pltpu.VMEM((BOX_ROWS, total), F32),
        pltpu.VMEM((9 * BOX_ROWS, total), BF),
    )

    def class_back(z_ref):
        z_ref[:, 0:8, :] = jnp.zeros((3, 8, C), F32)
        z_ref[:, 8 + g_cells : 16 + g_cells, :] = jnp.zeros((3, 8, C), F32)
        piece = g_cells // 4

        def multiply(i, carry):
            row = pl.multiple_of(i * piece, 16)
            for k in range(3):
                acc = jnp.zeros((piece, C), F32)
                for r in range(3):
                    t = r * 3 + k
                    source = row + first_g - cols * (r - 1)
                    mask = mx_ref[t, pl.ds(pl.multiple_of(source, 16), piece), :]
                    value = lgs_ref[pl.ds(pl.multiple_of(source - first_logit, 16), piece), :]
                    value = value * jnp.concatenate([mask] * (WIDE // LANE), axis=1)
                    acc += mm(value[:, :CLS_OUT], wct_ref[:, t * C : t * C + C])
                z_ref[k, pl.ds(pl.multiple_of(8 + row, 8), piece), :] = acc
            return carry

        lax.fori_loop(0, 4, multiply, 0)

        def collect(q, carry):
            row = pl.multiple_of(q * 256, 128)
            grad = z_ref[1, pl.ds(pl.multiple_of(8 + row, 8), 256), :]
            grad += z_ref[0, pl.ds(row, 272), :][9:265] + z_ref[2, pl.ds(row, 272), :][7:263]
            pre = pre_ref[pl.ds(pl.multiple_of(first_g - first_tower + row, 16), 256), :C]
            g_ref[pl.ds(row, 256), :C] = (grad * gelu_slope(pre)).astype(BF)
            return carry

        lax.fori_loop(0, g_cells // 256, collect, 0)

    pl.run_scoped(class_back, pltpu.VMEM((3, g_cells + 16, C), F32))

    def tower_back(z_ref, gt_ref):
        def flip(q, carry):
            row = pl.multiple_of(q * 256, 128)
            part = g_ref[pl.ds(pl.multiple_of(edge - first_g + row, 16), 256), :].astype(F32)
            gt_ref[:, pl.ds(row, 256)] = part.T.astype(BF)
            db_ref[...] += jnp.sum(part, axis=0, keepdims=True)
            build(f_ref.at[0], pl.multiple_of(edge + row, 16), 256, row)
            return carry

        lax.fori_loop(0, own // 256, flip, 0)

        def tower_weights(i, carry):
            at = pl.multiple_of(i * 256, 128)
            dwt_ref[:, pl.ds(at, 256)] += mm(gt_ref[...], x_ref[0:own, pl.ds(at, 256)])
            return carry

        lax.fori_loop(0, 9, tower_weights, 0)
        first_z = edge - 16
        piece = (own + 32) // 2

        def multiply(i, carry):
            row = pl.multiple_of(i * piece, 16)
            for k in range(3):
                acc = jnp.zeros((piece, C), F32)
                for r in range(3):
                    t = r * 3 + k
                    source = row + first_z - cols * (r - 1)
                    mask = mx_ref[t, pl.ds(pl.multiple_of(source, 16), piece), :]
                    value = g_ref[pl.ds(pl.multiple_of(source - first_g, 16), piece), :]
                    value = value * jnp.concatenate([mask] * (2 * C // LANE), axis=1)
                    acc += mm(value, wt_ref[t * C : t * C + C, :], NT)
                z_ref[k, pl.ds(row, piece), :] = acc
            return carry

        lax.fori_loop(0, 2, multiply, 0)

        def collect(q, carry):
            row = pl.multiple_of(q * 256, 128)
            base = pl.multiple_of(row + 8, 8)
            grad = z_ref[1, pl.ds(pl.multiple_of(16 + row, 8), 256), :]
            grad += z_ref[0, pl.ds(base, 272), :][9:265] + z_ref[2, pl.ds(base, 272), :][7:263]
            grad = grad.astype(BF).astype(F32)
            for n in range(2):
                fg_ref[0, n, pl.ds(row, 256), :] = grad[:, n * LANE : n * LANE + LANE]
            return carry

        lax.fori_loop(0, own // 256, collect, 0)

    pl.run_scoped(
        tower_back,
        pltpu.VMEM((3, own + 32, C), F32),
        pltpu.VMEM((2 * C, own), BF),
    )


def whole(shape):
    return pl.BlockSpec(shape, lambda *_: (0,) * len(shape))


def shape_of(shape, dtype=F32):
    return jax.ShapeDtypeStruct(shape, dtype)


VMEM_LIMIT = 63 * 1024 * 1024


def stem_forward(patches, rim, stem_w, stem_b, lat_w, lat_b):
    canvases, rows, width = patches.shape
    cols = width // PATCH
    pairs = 8
    steps = cols // (2 * pairs)
    chunk = 2 * pairs * PATCH
    zero = jnp.zeros((PATCH, C), BF)
    w2 = jnp.concatenate(
        [jnp.concatenate([stem_w, zero], axis=1), jnp.concatenate([zero, stem_w], axis=1)], axis=0
    )
    b2 = jnp.concatenate([stem_b, stem_b]).astype(F32)[None]
    count = pairs * canvases * rows
    total = (rows + 2 * HALO) * cols
    return pl.pallas_call(
        functools.partial(stem_kernel, pairs, cols, rows),
        grid=(steps,),
        in_specs=[
            pl.BlockSpec((canvases, rows, chunk), lambda s: (0, 0, s)),
            pl.BlockSpec((2 * HALO * canvases, chunk), lambda s: (0, s)),
            whole((2 * PATCH, 2 * C)),
            whole((1, 2 * C)),
            whole((C, C)),
            whole((1, C)),
        ],
        out_specs=[
            pl.BlockSpec((count, 2 * C), lambda s: (s, 0)),
            pl.BlockSpec((count, 2 * C), lambda s: (s, 0)),
            whole((canvases, 3, total, C)),
        ],
        out_shape=[
            shape_of((steps * count, 2 * C)),
            shape_of((steps * count, 2 * C), BF),
            shape_of((canvases, 3, total, C), BF),
        ],
        scratch_shapes=[pltpu.VMEM((canvases, 2, total + 16, LANE), F32)],
        compiler_params=pltpu.CompilerParams(vmem_limit_bytes=VMEM_LIMIT),
        name="stem",
    )(patches, rim, w2, b2, lat_w, lat_b.astype(F32)[None])


def stem_backward(patches, feature_grad, stem_out, stem_pre, lat_w):
    canvases, rows, width = patches.shape
    cols = width // PATCH
    pairs = 8
    steps = cols // (2 * pairs)
    chunk = 2 * pairs * PATCH
    count = pairs * canvases * rows
    return pl.pallas_call(
        functools.partial(stem_back_kernel, pairs, cols, rows),
        grid=(steps,),
        in_specs=[
            pl.BlockSpec((canvases, rows, chunk), lambda s: (0, 0, s)),
            whole((canvases, 2, rows * cols, LANE)),
            pl.BlockSpec((count, 2 * C), lambda s: (s, 0)),
            pl.BlockSpec((count, 2 * C), lambda s: (s, 0)),
            whole((C, C)),
        ],
        out_specs=[whole((PATCH, C)), whole((1, C)), whole((C, C)), whole((1, C))],
        out_shape=[shape_of((PATCH, C)), shape_of((1, C)), shape_of((C, C)), shape_of((1, C))],
        compiler_params=pltpu.CompilerParams(vmem_limit_bytes=VMEM_LIMIT),
        name="stem_back",
    )(patches, feature_grad, stem_out, stem_pre, lat_w)


def heads_call(rows, cols, scal, feats, masks, labels, box_target, wt, tb, wct, wb):
    canvases = feats.shape[0]
    own = rows * cols
    total = own + 2 * HALO * cols
    spread = jnp.repeat(jnp.eye(SLOT, 9, dtype=BF), LANE, axis=1)

    def per(shape):
        return pl.BlockSpec((1,) + shape, lambda c: (c,) + (0,) * len(shape))

    return pl.pallas_call(
        functools.partial(head_kernel, cols, rows),
        grid=(canvases,),
        in_specs=[
            pl.BlockSpec(memory_space=pltpu.SMEM),
            pl.BlockSpec((1, 3, total, C), lambda c: (c, 0, 0, 0), pipeline_mode=pl.Buffered(1)),
            per((SLOT, total)),
            per((SLOT, total)),
            per((4, SLOT, total)),
            whole(spread.shape),
            whole(wt.shape),
            whole(tb.shape),
            whole(wct.shape),
            whole(wb.shape),
        ],
        out_specs=[
            whole((CLS_OUT, 9 * C)),
            whole((2 * C, 9 * C)),
            whole((9 * BOX_ROWS, C)),
            whole((1, 2 * C)),
            per((2, own, LANE)),
            whole((16, 256)),
        ],
        out_shape=[
            shape_of((CLS_OUT, 9 * C)),
            shape_of((2 * C, 9 * C)),
            shape_of((9 * BOX_ROWS, C)),
            shape_of((1, 2 * C)),
            shape_of((canvases, 2, own, LANE)),
            shape_of((16, 256)),
        ],
        scratch_shapes=[
            pltpu.VMEM((9, total, LANE), BF),
            pltpu.VMEM((total - 2 * cols, 9 * C), BF),
            pltpu.VMEM((total - 2 * cols, 2 * C), F32),
            pltpu.VMEM((total, C), BF),
            pltpu.VMEM((CLS_OUT, own + 512), BF),
            pltpu.VMEM((own + 512, WIDE), BF),
            pltpu.VMEM((WIDE, 256), F32),
            pltpu.VMEM((own + 256, 2 * C), BF),
        ],
        compiler_params=pltpu.CompilerParams(vmem_limit_bytes=VMEM_LIMIT),
        name="heads",
    )(scal, feats, masks, labels, box_target, spread, wt, tb, wct, wb)


def unpack(flat_values):
    lengths = [PATCH * C, C, C * C, C, 18 * C * C, 2 * C, 9 * C * BOX_OUT]
    pieces = []
    offset = 0
    for length in lengths:
        pieces.append(flat_values[offset : offset + length])
        offset = offset + length
    return (
        pieces[0].reshape(PATCH, C),
        pieces[1],
        pieces[2].reshape(C, C),
        pieces[3],
        pieces[4].reshape(2, 9, C, C),
        pieces[5].reshape(2, C),
        pieces[6].reshape(9, C, BOX_OUT),
    )


def adamw_update(weight, first, second, grad):
    first_new = MOMENT_ONE * first + (1.0 - MOMENT_ONE) * grad
    second_new = MOMENT_TWO * second + (1.0 - MOMENT_TWO) * grad * grad
    first_hat = first_new / (1.0 - MOMENT_ONE**STEP)
    second_hat = second_new / (1.0 - MOMENT_TWO**STEP)
    weight_new = weight - RATE * (first_hat / (jnp.sqrt(second_hat) + EPSILON) + DECAY * weight)
    return (weight_new, first_new, second_new)


def cell_data(boxes, match, gt_labels, gt_deltas, first_row, rows, cols):
    full_rows = match.shape[2] // cols
    total = (rows + 2 * HALO) * cols
    place = jnp.arange(total, dtype=jnp.int32)[None]
    row = place // cols + (first_row - HALO)
    col = place % cols

    def crop(r, j):
        found = jnp.full((boxes.shape[0], total), -1, jnp.int32)
        for k in range(boxes.shape[1]):
            edge = boxes[:, k, :, None]
            inside = (r >= edge[:, 0]) & (r < edge[:, 2]) & (j >= edge[:, 1]) & (j < edge[:, 3])
            found = jnp.where(inside, k, found)
        return jnp.where((r >= 0) & (r < full_rows) & (j >= 0) & (j < cols), found, -1)

    centre = crop(row, col)
    valid = centre >= 0
    masks = jnp.stack([(crop(row + di, col + dj) == centre) & valid for di, dj in TAPS], axis=1)
    masks = jnp.pad(masks.astype(BF), ((0, 0), (0, SLOT - 9), (0, 0)))
    edge = HALO * cols
    near = jnp.pad(match, ((0, 0), (0, 0), (edge, edge)), constant_values=-2)
    near = lax.dynamic_slice_in_dim(near, first_row * cols, total, 2)
    near = jnp.where(valid[:, None], near, -2)
    near = jnp.pad(near, ((0, 0), (0, SLOT - 9), (0, 0)), constant_values=-2)
    labels = near
    targets = jnp.zeros((near.shape[0], 4) + near.shape[1:], F32)
    for g in range(gt_labels.shape[1]):
        labels = jnp.where(near == g, gt_labels[:, g, None, None], labels)
        targets = jnp.where((near == g)[:, None], gt_deltas[:, g, :, None, None], targets)
    return masks, labels.astype(F32), targets


def local(patches, boxes, match, gt_labels, gt_deltas, ema_old, shared_params, shared_m, shared_v, class_params, class_m, class_v):
    cls_rank = lax.axis_index("cls")
    cls_parts = lax.axis_size("cls")
    canvases, rows, width = patches.shape
    cols = width // PATCH
    own = rows * cols
    edge = HALO * cols
    masks, labels, targets = cell_data(boxes, match, gt_labels, gt_deltas, cls_rank * rows, rows, cols)
    count = jnp.sum((labels[:, :, edge : edge + own] >= 0.0).astype(F32))
    positives = lax.psum(count, ("img", "cls"))
    norm = jnp.maximum(positives, 1.0)
    ema_new = EMA_KEEP * ema_old + (1.0 - EMA_KEEP) * norm

    all_weights = lax.all_gather(shared_params.astype(BF), ("img", "cls"), axis=0, tiled=True)
    class_w = lax.all_gather(class_params.astype(BF), ("img", "cls"), axis=0)
    class_w = class_w.reshape(-1, cls_parts, *class_params.shape).transpose(0, 2, 1, 3).reshape(9, C, CLS_OUT)
    down = lax.ppermute(patches[:, rows - HALO :], "cls", [(i, i + 1) for i in range(cls_parts - 1)])
    up = lax.ppermute(patches[:, :HALO], "cls", [(i + 1, i) for i in range(cls_parts - 1)])
    rim = jnp.concatenate([down, up], axis=1).reshape(canvases * 2 * HALO, width)

    stem_w, stem_b, lat_w, lat_b, tower_w, tower_b, box_w = unpack(all_weights)
    stem_pre, stem_out, feats = stem_forward(patches, rim, stem_w, stem_b, lat_w, lat_b)
    wt = jnp.concatenate([tower_w[0].reshape(9 * C, C), tower_w[1].reshape(9 * C, C)], axis=1)
    tb = tower_b.reshape(1, 2 * C).astype(F32)
    wct = class_w.transpose(2, 0, 1).reshape(CLS_OUT, 9 * C)
    wb = jnp.pad(box_w.reshape(9, C, ANCH, 4).transpose(0, 3, 2, 1), ((0, 0), (0, 0), (0, SLOT - ANCH), (0, 0)))
    wb = wb.reshape(9 * BOX_ROWS, C)
    scal = jnp.stack([1.0 / ema_new, 1.0 / norm])
    dwc, dwt, dwb, db, feature_grad, sums = heads_call(
        rows, cols, scal, feats, masks, labels, targets, wt, tb, wct, wb
    )
    stem_g, stem_bg, lat_g, lat_bg = stem_backward(patches, feature_grad, stem_out, stem_pre, lat_w)
    focal, huber = lax.psum((jnp.sum(sums[0:8]), jnp.sum(sums[8:16])), ("img", "cls"))
    loss = focal / ema_new + huber / norm

    tower_g = dwt.reshape(2, C, 9 * C).transpose(0, 2, 1)
    box_g = dwb.reshape(9, 4, SLOT, C)[:, :, :ANCH].transpose(0, 3, 2, 1)
    flat = jnp.concatenate(
        [stem_g.reshape(-1), stem_bg.reshape(-1), lat_g.reshape(-1), lat_bg.reshape(-1), tower_g.reshape(-1), db.reshape(-1), box_g.reshape(-1)]
    )
    shared_grad = lax.psum_scatter(flat, ("img", "cls"), scatter_dimension=0, tiled=True)
    class_sum = lax.psum_scatter(dwc.T, "img", scatter_dimension=0, tiled=True)
    class_grad = lax.psum_scatter(class_sum, "cls", scatter_dimension=1, tiled=True)
    return (
        loss,
        ema_new,
        *adamw_update(shared_params, shared_m, shared_v, shared_grad),
        *adamw_update(class_params, class_m, class_v, class_grad),
    )


def solution(mesh):
    spread = P(("img", "cls"))
    block = P("img", "cls")
    return jax.shard_map(
        local,
        mesh=mesh,
        in_specs=(
            P("img", "cls", None),
            P("img", None, None),
            P("img", None, None),
            P("img", None),
            P("img", None, None),
            P(),
            spread,
            spread,
            spread,
            block,
            block,
            block,
        ),
        out_specs=(P(), P(), spread, spread, spread, block, block, block),
        check_vma=False,
    )
```

```python
import functools

import jax
import jax.numpy as jnp
from jax import lax
from jax.experimental import pallas as pl
from jax.experimental.pallas import tpu as pltpu
from jax.sharding import PartitionSpec as P

C = 256
CLASSES = 80
ANCH = 9
PATCH = 192
BOX_OUT = 36
CLS_OUT = ANCH * CLASSES
STEP = 5
GT = 16
HALO = 4
SLOT = 16
BOX_ROWS = 4 * SLOT
LANE = 128
WIDE = 768
GROUP = 16

PRIOR = -4.59511985013459
ALPHA = 0.25
HUBER = 1.0 / 9.0
EMA_KEEP = 0.9
RATE = 0.01
MOMENT_ONE = 0.5
MOMENT_TWO = 0.5
DECAY = 0.05
EPSILON = 1e-08

LENGTHS = [PATCH * C, C, C * C, C, 18 * C * C, 2 * C, 9 * C * BOX_OUT]
TOWER_AT = sum(LENGTHS[:4]) // C
LEAD = -TOWER_AT % 16
TOWER_ROW = TOWER_AT + LEAD
TAIL_ROW = TOWER_ROW + 18 * C
FULL_ROWS = -(-(LEAD + sum(LENGTHS) // C) // 16) * 16
HALF = 384
MESH = pl.DeviceIdType.MESH

BF = jnp.bfloat16
F32 = jnp.float32
TAPS = [(di, dj) for di in (-1, 0, 1) for dj in (-1, 0, 1)]
NN = (((1,), (0,)), ((), ()))
NT = (((1,), (1,)), ((), ()))
TN = (((0,), (0,)), ((), ()))
K0 = 0.7978845608028654
K1 = 0.044715


def mm(a, b, dims=NN):
    return lax.dot_general(a, b, dims, preferred_element_type=F32)


def gelu(x):
    return 0.5 * x * (1.0 + jnp.tanh(K0 * (x + K1 * x * x * x)))


def gelu_slope(x):
    square = x * x
    th = jnp.tanh(K0 * (x + K1 * x * square))
    return 0.5 * (1.0 + th) + (0.5 * K0) * x * (1.0 - th * th) * (1.0 + 3.0 * K1 * square)


def columns_of(x, pairs, width):
    return [x[:, width * k : width * (k + 1)] for k in range(pairs)]


def stem_kernel(pairs, cols, rows, x_ref, h_ref, head_ref, pre_ref, so_ref, f_ref, lw_ref, t_ref, w_ref, b_ref, lb_ref):
    step = pl.program_id(0)
    canvases = x_ref.shape[0]
    own_rows = canvases * rows
    total = (rows + 2 * HALO) * cols

    @pl.when(step == 0)
    def _():
        head = head_ref[...].astype(F32)
        w_ref[...] = jnp.zeros_like(w_ref)
        stem_w = head[LEAD : LEAD + PATCH].astype(BF)
        w_ref[:PATCH, :C] = stem_w
        w_ref[PATCH:, C:] = stem_w
        bias = head[LEAD + PATCH : LEAD + PATCH + 1]
        b_ref[...] = jnp.concatenate([bias, bias], axis=1)
        lw_ref[...] = head[LEAD + PATCH + 1 : TOWER_ROW - 1].astype(BF)
        lb_ref[...] = head[TOWER_ROW - 1 : TOWER_ROW]
        for c in range(canvases):
            for n in range(2):
                t_ref[c, n, 0:8, :] = jnp.zeros((8, LANE), F32)
                t_ref[c, n, 8 + total : 16 + total, :] = jnp.zeros((8, LANE), F32)

    x = x_ref[...].reshape(own_rows, x_ref.shape[2])
    own = columns_of(x, pairs, 2 * PATCH)
    rim = columns_of(h_ref[...], pairs, 2 * PATCH)
    pre = mm(jnp.concatenate(own + rim, axis=0), w_ref[...]) + b_ref[...]
    count = pairs * own_rows
    pre_ref[...] = pre[:count]
    out = gelu(pre).astype(BF)
    so_ref[...] = out[:count]
    for half in range(2):
        feat = mm(out[:, half * C : half * C + C], lw_ref[...]) + lb_ref[...]
        for k in range(pairs):
            j = step * 2 * pairs + 2 * k + half
            for c in range(canvases):
                at = k * own_rows + c * rows
                rim_at = count + k * 2 * HALO * canvases + c * 2 * HALO
                for n in range(2):
                    side = slice(n * LANE, n * LANE + LANE)
                    place = pl.ds(8 + HALO * cols + j, rows, stride=cols)
                    t_ref[c, n, place, :] = feat[at : at + rows, side]
                    place = pl.ds(8 + j, HALO, stride=cols)
                    t_ref[c, n, place, :] = feat[rim_at : rim_at + HALO, side]
                    place = pl.ds(8 + (HALO + rows) * cols + j, HALO, stride=cols)
                    t_ref[c, n, place, :] = feat[rim_at + HALO : rim_at + 2 * HALO, side]

    @pl.when(step == pl.num_programs(0) - 1)
    def _():
        piece = 4 * cols

        def move(i, carry):
            base = pl.multiple_of(i * piece, 16)
            for c in range(canvases):
                for n in range(2):
                    value = t_ref[c, n, pl.ds(base, piece + 16), :]
                    for k in range(3):
                        moved = value[7 + k : 7 + k + piece].astype(BF)
                        f_ref[c, k, pl.ds(base, piece), n * LANE : n * LANE + LANE] = moved
            return carry

        lax.fori_loop(0, total // piece, move, 0)


def stem_back_kernel(pairs, cols, rows, x_ref, fg_ref, so_ref, pre_ref, lw_ref, head_ref, sw_out, sb_out, lw_out, lb_out, h_ref):
    step = pl.program_id(0)
    canvases = x_ref.shape[0]

    @pl.when(step == 0)
    def _():
        sw_out[...] = jnp.zeros_like(sw_out)
        sb_out[...] = jnp.zeros_like(sb_out)
        lw_out[...] = jnp.zeros_like(lw_out)
        lb_out[...] = jnp.zeros_like(lb_out)

    x = x_ref[...].reshape(canvases * rows, x_ref.shape[2])
    own = jnp.concatenate(columns_of(x, pairs, 2 * PATCH), axis=0)
    low = []
    for half in range(2):
        parts = []
        for k in range(pairs):
            j = step * 2 * pairs + 2 * k + half
            for c in range(canvases):
                place = pl.ds(j, rows, stride=cols)
                parts.append(jnp.concatenate([fg_ref[c, n, place, :] for n in range(2)], axis=1))
        grad32 = jnp.concatenate(parts, axis=0)
        grad = grad32.astype(BF)
        cut = slice(half * C, half * C + C)
        lw_out[...] += mm(so_ref[:, cut], grad, TN)
        lb_out[...] += jnp.sum(grad32, axis=0, keepdims=True)
        back = mm(grad, lw_ref[...], NT) * gelu_slope(pre_ref[:, cut])
        back = back.astype(BF)
        sb_out[...] += jnp.sum(back.astype(F32), axis=0, keepdims=True)
        low.append(back)
    both = mm(own, jnp.concatenate(low, axis=1), TN)
    sw_out[...] += both[:PATCH, :C] + both[PATCH:, C:]

    @pl.when(step == pl.num_programs(0) - 1)
    def _():
        at = LEAD + PATCH
        h_ref[0:LEAD, :] = jnp.zeros((LEAD, C), F32)
        h_ref[LEAD:at, :] = sw_out[...]
        h_ref[at : at + 1, :] = sb_out[...]
        h_ref[at + 1 : TOWER_ROW - 1, :] = lw_out[...]
        h_ref[TOWER_ROW - 1 :, :] = lb_out[...]
        head_ref[...] = h_ref[...].astype(BF)


def pipeline(count, build, work, finish, flush, bufs, outs):
    build(0, bufs[0])

    def step(s, k):
        finish(s - 1, outs[1 - k])
        build(jnp.minimum(s + 1, count - 1), bufs[1 - k])
        work(s, bufs[k], outs[k])
        flush(jnp.maximum(s - 1, 0))

    def pair(i, carry):
        step(2 * i, 0)
        step(2 * i + 1, 1)
        return carry

    lax.fori_loop(0, count // 2, pair, 0)
    finish(count - 1, outs[1])
    flush(count - 1)


def aligned(value, multiple):
    return value if isinstance(value, int) else pl.multiple_of(value, multiple)


def many(mask, count):
    return jnp.concatenate([mask] * count, axis=1)


def weight_sums(canvas, cols, edge, own, grad, source, mx_ref, sum_ref):
    def go(x_ref):
        def triple(n, carry):
            at = pl.multiple_of(edge + cols * (n - 1), 16)
            for k in range(3):
                mask = mx_ref[n * 3 + k, edge : edge + own, :]
                x_ref[:, k * C : k * C + C] = source[k, pl.ds(at, own), :] * many(mask, 2)
            side = pl.ds(pl.multiple_of(n * 3 * C, C), 3 * C)
            sum_ref[:, side] = jnp.where(canvas > 0, sum_ref[:, side], 0.0) + mm(grad(), x_ref[...])
            return carry

        lax.fori_loop(0, 3, triple, 0)

    pl.run_scoped(go, pltpu.VMEM((own, 3 * C), BF))


def head_kernel(
    cols, rows, scal_ref, f_ref, mk_ref, lab_ref, btt_ref, e_ref, full_ref, tb_ref, wct_ref, wb_ref,
    dwc_ref, dwt_ref, dwb_ref, db_ref, fg_ref, sums_ref,
    mx_ref, pre_ref, bt_ref, lgt_ref, lgs_ref, g_ref, wt_ref,
):
    own = rows * cols
    edge = HALO * cols
    total = own + 2 * edge
    shift = [cols * di + dj for di, dj in TAPS]

    @pl.when(pl.program_id(0) == 0)
    def _():
        dwb_ref[...] = jnp.zeros_like(dwb_ref)
        db_ref[...] = jnp.zeros_like(db_ref)
        sums_ref[...] = jnp.zeros_like(sums_ref)
        for n in range(2):
            here = TOWER_ROW + n * 9 * C
            wt_ref[:, n * C : n * C + C] = full_ref[here : here + 9 * C, :]

    def spread(i, carry):
        at = pl.multiple_of(i * 384, 128)
        wide = mm(mk_ref[0, :, pl.ds(at, 384)], e_ref[...], TN).astype(BF)
        for t in range(9):
            mx_ref[t, pl.ds(at, 384), :] = wide[:, t * LANE : (t + 1) * LANE]
        return carry

    lax.fori_loop(0, total // 384, spread, 0)

    def twice(mask):
        return jnp.concatenate([mask, mask], axis=1)

    def build(source, at, count, x_ref):
        for t, (di, dj) in enumerate(TAPS):
            value = source[dj + 1, pl.ds(pl.multiple_of(at + cols * di, 16), count), :]
            x_ref[:, t * C : (t + 1) * C] = value * twice(mx_ref[t, pl.ds(at, count), :])

    first_tower = cols
    tower_rows = total - 2 * cols
    first_logit = edge - 256
    logit_cells = own + 512
    first_g = edge - 128
    g_cells = own + 256

    def heads(ct32_ref, ct_ref):
        zero = jnp.zeros((cols + 8, C), F32)
        ct32_ref[0 : cols + 8, :] = zero
        ct32_ref[8 + total - cols : 16 + total, :] = zero
        zero = jnp.zeros((cols, C), BF)
        bt_ref[0:cols, :] = zero
        bt_ref[total - cols : total, :] = zero
        piece = tower_rows // 3

        def towers(x_ref):
            def tower(i, carry):
                row = pl.multiple_of(i * piece, 16)
                at = pl.multiple_of(first_tower + i * piece, 16)
                build(f_ref.at[0], at, piece, x_ref)
                pre = mm(x_ref[...], wt_ref[...]) + tb_ref[...]
                pre_ref[pl.ds(row, piece), :] = pre
                out = gelu(pre)
                ct32_ref[pl.ds(pl.multiple_of(8 + at, 8), piece), :] = out[:, :C]
                bt_ref[pl.ds(at, piece), :] = out[:, C:].astype(BF)
                return carry

            lax.fori_loop(0, 3, tower, 0)

        pl.run_scoped(towers, pltpu.VMEM((piece, 9 * C), BF))

        def move(i, carry):
            base = pl.multiple_of(i * edge, 16)
            value = ct32_ref[pl.ds(base, edge + 16), :]
            for k in range(3):
                ct_ref[k, pl.ds(base, edge), :] = value[7 + k : 7 + k + edge].astype(BF)
            return carry

        lax.fori_loop(0, total // edge, move, 0)
        def logits(xa_ref, xb_ref, la_ref, lb_ref, st_ref, tt_ref):
            inv_ema = scal_ref[0]
            number = lax.broadcasted_iota(jnp.int32, (GROUP, 256), 0).astype(F32)
            lane = lax.broadcasted_iota(jnp.int32, (8, 256), 1)
            plan = column_plan()

            def ready(q, x_ref):
                build(ct_ref, pl.multiple_of(first_logit + q * 256, 128), 256, x_ref)

            def work(q, x_ref, l_ref):
                l_ref[...] = mm(wct_ref[...], x_ref[...], NT)

            def focal(q, l_ref):
                at = pl.multiple_of(first_logit + jnp.maximum(q, 0) * 256, 128)
                spot = lane + at
                mine = (spot >= edge) & (spot < edge + own) & (lane + q >= 0)
                lines = [lab_ref[0, a : a + 1, pl.ds(at, 256)] for a in range(ANCH)]
                rest = [jnp.where(line > -1.5, 1.0 - ALPHA, 0.0) for line in lines]
                pulls = [line * inv_ema for line in rest]
                total_focal = jnp.zeros((8, 256), F32)
                for first in range(0, WIDE, GROUP):
                    value = l_ref[first : first + GROUP, :] + PRIOR
                    key = None
                    for begin, count, anchor, klass in plan:
                        if begin >= first + GROUP or begin + count <= first:
                            continue
                        if anchor < 0:
                            parts = [jnp.full((GROUP, 256), n, F32) for n in (-2.0, 0.0, 0.0)]
                        else:
                            parts = [lines[anchor] - float(klass - (begin - first)), rest[anchor], pulls[anchor]]
                            parts = [jnp.broadcast_to(part, (GROUP, 256)) for part in parts]
                        if key is None:
                            key, other, pull_other = parts
                        else:
                            later = number >= float(begin - first)
                            key = jnp.where(later, parts[0], key)
                            other = jnp.where(later, parts[1], other)
                            pull_other = jnp.where(later, parts[2], pull_other)
                    hit = key == number
                    side = jnp.where(hit, -value, value)
                    small = jnp.exp(-jnp.abs(side))
                    whole_one = 1.0 + small
                    ratio = pltpu.reciprocal(whole_one, approx=True)
                    ratio = ratio * (2.0 - whole_one * ratio)
                    part = small * ratio
                    up = side >= 0.0
                    prob = jnp.where(up, ratio, part)
                    miss = jnp.where(up, part, ratio)
                    tiny = small * (1.0 - 0.5 * small)
                    cross = jnp.maximum(side, 0.0) + jnp.where(small < 0.001, tiny, jnp.log(whole_one))
                    square = prob * prob
                    value = square * cross * jnp.where(hit, ALPHA, other)
                    pull = square * (2.0 * miss * cross + prob) * jnp.where(hit, -ALPHA * inv_ema, pull_other)
                    l_ref[first : first + GROUP, :] = pull
                    st_ref[first : first + GROUP, :] = pull.astype(BF)
                    total_focal += jnp.sum(value.reshape(GROUP // 8, 8, 256), axis=0)
                sums_ref[0:8, :] += jnp.where(mine, total_focal, 0.0)
                tt_ref[...] = l_ref[...].T.astype(BF)

            def flush(q):
                row = pl.multiple_of(q * 256, 128)
                lgt_ref[:, pl.ds(row, 256)] = st_ref[...]
                lgs_ref[pl.ds(row, 256), :] = tt_ref[...]

            pipeline(logit_cells // 256, ready, work, focal, flush, (xa_ref, xb_ref), (la_ref, lb_ref))

        pl.run_scoped(
            logits,
            pltpu.VMEM((256, 9 * C), BF),
            pltpu.VMEM((256, 9 * C), BF),
            pltpu.VMEM((WIDE, 256), F32),
            pltpu.VMEM((WIDE, 256), F32),
            pltpu.VMEM((WIDE, 256), BF),
            pltpu.VMEM((256, WIDE), BF),
        )
        weight_sums(pl.program_id(0), cols, edge, own, lambda: lgt_ref[:, 256 : 256 + own], ct_ref, mx_ref, dwc_ref)

    pl.run_scoped(heads, pltpu.VMEM((total + 16, C), F32), pltpu.VMEM((3, total, C), BF))

    def box_forward(gg_ref, y_ref):
        inv_norm = scal_ref[1]

        def outer(i, carry):
            at = pl.multiple_of(i * 768, 128)
            y_ref[:, pl.ds(at, 768)] = mm(wb_ref[...], bt_ref[pl.ds(at, 768), :], NT)
            return carry

        lax.fori_loop(0, total // 768, outer, 0)
        lane = lax.broadcasted_iota(jnp.int32, (SLOT, total), 1)
        mine = (lane >= edge) & (lane < edge + own)

        def guess(m, carry):
            acc = jnp.zeros((SLOT, total), F32)
            for t in range(9):
                value = y_ref[pl.ds(pl.multiple_of(t * BOX_ROWS + m * SLOT, 8), SLOT), :]
                moved = pltpu.roll(value, (-shift[t]) % total, 1)
                acc += moved * mk_ref[0, t : t + 1, :].astype(F32)
            differ = acc - btt_ref[0, m]
            positive = lab_ref[0] >= 0.0
            size = jnp.abs(differ)
            loss = jnp.where(size < HUBER, 0.5 * differ * differ / HUBER, size - 0.5 * HUBER)
            loss = jnp.where(positive & mine, loss, 0.0)
            part = loss[:, 0:256]
            for k in range(1, total // 256):
                part += loss[:, k * 256 : (k + 1) * 256]
            sums_ref[8:16, :] += part[0:8] + part[8:16]
            pull = jnp.minimum(jnp.maximum(differ / HUBER, -1.0), 1.0) * inv_norm
            pull = jnp.where(positive, pull, 0.0)
            gg_ref[pl.ds(pl.multiple_of(m * SLOT, 8), SLOT), :] = pull
            return carry

        lax.fori_loop(0, 4, guess, 0)

    def box_back(gg_ref, xg_ref):
        for t in range(9):
            moved = pltpu.roll(gg_ref[...], shift[t] % total, 1)
            xg_ref[t * BOX_ROWS : (t + 1) * BOX_ROWS, :] = (moved * mk_ref[0, 8 - t : 9 - t, :].astype(F32)).astype(BF)
        dwb_ref[...] += mm(xg_ref[:, edge : edge + own], bt_ref[edge : edge + own, :])

        def into(q, carry):
            row = pl.multiple_of(q * 256, 128)
            grad = mm(xg_ref[:, pl.ds(pl.multiple_of(first_g + row, 128), 256)], wb_ref[...], TN)
            pre = pre_ref[pl.ds(pl.multiple_of(first_g - first_tower + row, 16), 256), C:]
            g_ref[pl.ds(row, 256), C:] = (grad * gelu_slope(pre)).astype(BF)
            return carry

        lax.fori_loop(0, g_cells // 256, into, 0)

    def boxes(gg_ref):
        pl.run_scoped(functools.partial(box_forward, gg_ref), pltpu.VMEM((9 * BOX_ROWS, total), F32))
        pl.run_scoped(functools.partial(box_back, gg_ref), pltpu.VMEM((9 * BOX_ROWS, total), BF))

    pl.run_scoped(boxes, pltpu.VMEM((BOX_ROWS, total), F32))

    def class_back(z_ref):
        z_ref[:, 0:8, :] = jnp.zeros((3, 8, C), F32)
        z_ref[:, 8 + g_cells : 16 + g_cells, :] = jnp.zeros((3, 8, C), F32)
        piece = g_cells // 4

        def multiply(i, carry):
            row = pl.multiple_of(i * piece, 16)
            for k in range(3):
                acc = jnp.zeros((piece, C), F32)
                for r in range(3):
                    t = r * 3 + k
                    source = row + first_g - cols * (r - 1)
                    mask = mx_ref[t, pl.ds(pl.multiple_of(source, 16), piece), :]
                    value = lgs_ref[pl.ds(pl.multiple_of(source - first_logit, 16), piece), :]
                    value = value * jnp.concatenate([mask] * (WIDE // LANE), axis=1)
                    acc += mm(value, wct_ref[:, t * C : t * C + C])
                z_ref[k, pl.ds(pl.multiple_of(8 + row, 8), piece), :] = acc
            return carry

        lax.fori_loop(0, 4, multiply, 0)

        def collect(q, carry):
            row = pl.multiple_of(q * 256, 128)
            grad = z_ref[1, pl.ds(pl.multiple_of(8 + row, 8), 256), :]
            grad += z_ref[0, pl.ds(row, 272), :][9:265] + z_ref[2, pl.ds(row, 272), :][7:263]
            pre = pre_ref[pl.ds(pl.multiple_of(first_g - first_tower + row, 16), 256), :C]
            g_ref[pl.ds(row, 256), :C] = (grad * gelu_slope(pre)).astype(BF)
            return carry

        lax.fori_loop(0, g_cells // 256, collect, 0)

    pl.run_scoped(class_back, pltpu.VMEM((3, g_cells + 16, C), F32))

    def tower_back(z_ref, gt_ref):
        def flip(q, carry):
            row = pl.multiple_of(q * 256, 128)
            part = g_ref[pl.ds(pl.multiple_of(edge - first_g + row, 16), 256), :].astype(F32)
            gt_ref[:, pl.ds(row, 256)] = part.T.astype(BF)
            db_ref[...] += jnp.sum(part, axis=0, keepdims=True)
            return carry

        lax.fori_loop(0, own // 256, flip, 0)
        weight_sums(pl.program_id(0), cols, edge, own, lambda: gt_ref[...], f_ref.at[0], mx_ref, dwt_ref)
        first_z = edge - 16
        piece = (own + 32) // 2

        def multiply(i, carry):
            row = pl.multiple_of(i * piece, 16)
            for k in range(3):
                acc = jnp.zeros((piece, C), F32)
                for r in range(3):
                    t = r * 3 + k
                    source = row + first_z - cols * (r - 1)
                    mask = mx_ref[t, pl.ds(pl.multiple_of(source, 16), piece), :]
                    value = g_ref[pl.ds(pl.multiple_of(source - first_g, 16), piece), :]
                    value = value * jnp.concatenate([mask] * (2 * C // LANE), axis=1)
                    acc += mm(value, wt_ref[t * C : t * C + C, :], NT)
                z_ref[k, pl.ds(row, piece), :] = acc
            return carry

        lax.fori_loop(0, 2, multiply, 0)

        def collect(q, carry):
            row = pl.multiple_of(q * 256, 128)
            base = pl.multiple_of(row + 8, 8)
            grad = z_ref[1, pl.ds(pl.multiple_of(16 + row, 8), 256), :]
            grad += z_ref[0, pl.ds(base, 272), :][9:265] + z_ref[2, pl.ds(base, 272), :][7:263]
            grad = grad.astype(BF).astype(F32)
            for n in range(2):
                fg_ref[0, n, pl.ds(row, 256), :] = grad[:, n * LANE : n * LANE + LANE]
            return carry

        lax.fori_loop(0, own // 256, collect, 0)

    pl.run_scoped(
        tower_back,
        pltpu.VMEM((3, own + 32, C), F32),
        pltpu.VMEM((2 * C, own), BF),
    )


def whole(shape):
    return pl.BlockSpec(shape, lambda *_: (0,) * len(shape))


def shape_of(shape, dtype=F32):
    return jax.ShapeDtypeStruct(shape, dtype)


VM = pl.BlockSpec(memory_space=pltpu.VMEM)
VMEM_LIMIT = 63 * 1024 * 1024


def stem_forward(patches, rim, head):
    canvases, rows, width = patches.shape
    cols = width // PATCH
    pairs = 8
    steps = cols // (2 * pairs)
    chunk = 2 * pairs * PATCH
    count = pairs * canvases * rows
    total = (rows + 2 * HALO) * cols
    return pl.pallas_call(
        functools.partial(stem_kernel, pairs, cols, rows),
        grid=(steps,),
        in_specs=[
            pl.BlockSpec((canvases, rows, chunk), lambda s: (0, 0, s)),
            pl.BlockSpec((2 * HALO * canvases, chunk), lambda s: (0, s)),
            whole(head.shape),
        ],
        out_specs=[
            pl.BlockSpec((count, 2 * C), lambda s: (s, 0)),
            pl.BlockSpec((count, 2 * C), lambda s: (s, 0)),
            whole((canvases, 3, total, C)),
            whole((C, C)),
        ],
        out_shape=[
            shape_of((steps * count, 2 * C)),
            shape_of((steps * count, 2 * C), BF),
            shape_of((canvases, 3, total, C), BF),
            shape_of((C, C), BF),
        ],
        scratch_shapes=[
            pltpu.VMEM((canvases, 2, total + 16, LANE), F32),
            pltpu.VMEM((2 * PATCH, 2 * C), BF),
            pltpu.VMEM((1, 2 * C), F32),
            pltpu.VMEM((1, C), F32),
        ],
        compiler_params=pltpu.CompilerParams(vmem_limit_bytes=VMEM_LIMIT),
        name="stem",
    )(patches, rim, head)


def stem_backward(patches, feature_grad, stem_out, stem_pre, lat_w):
    canvases, rows, width = patches.shape
    cols = width // PATCH
    pairs = 8
    steps = cols // (2 * pairs)
    chunk = 2 * pairs * PATCH
    count = pairs * canvases * rows
    return pl.pallas_call(
        functools.partial(stem_back_kernel, pairs, cols, rows),
        grid=(steps,),
        in_specs=[
            pl.BlockSpec((canvases, rows, chunk), lambda s: (0, 0, s)),
            whole((canvases, 2, rows * cols, LANE)),
            pl.BlockSpec((count, 2 * C), lambda s: (s, 0)),
            pl.BlockSpec((count, 2 * C), lambda s: (s, 0)),
            whole((C, C)),
        ],
        out_specs=whole((TOWER_ROW, C)),
        out_shape=shape_of((TOWER_ROW, C), BF),
        scratch_shapes=[
            pltpu.VMEM((PATCH, C), F32),
            pltpu.VMEM((1, C), F32),
            pltpu.VMEM((C, C), F32),
            pltpu.VMEM((1, C), F32),
            pltpu.VMEM((TOWER_ROW, C), F32),
        ],
        compiler_params=pltpu.CompilerParams(vmem_limit_bytes=VMEM_LIMIT),
        name="stem_back",
    )(patches, feature_grad, stem_out, stem_pre, lat_w)


BOX_CUTS = [(BOX_OUT * n // C, BOX_OUT * n % C) for n in range(64)]


def box_in_kernel(tail_ref, o_ref, t_ref, d_ref, u_ref):
    tail = tail_ref[...].astype(F32)
    count = tail.shape[0]
    lane = lax.broadcasted_iota(jnp.int32, (40, LANE), 1)
    for n in range(2):
        t_ref[n, 0:count, :] = tail[:, n * LANE : n * LANE + LANE]
        t_ref[n, count:, :] = jnp.zeros((t_ref.shape[1] - count, LANE), F32)
    lines = []
    for r in range(9):
        lines.append(jnp.concatenate([t_ref[n, pl.ds(2 + r, 40, stride=9), :] for n in range(2)], axis=1))
    for s, (r, at) in enumerate(BOX_CUTS):
        wide = jnp.concatenate([lines[r], lines[min(r + 1, 8)]], axis=1)
        d_ref[pl.ds(s, 40, stride=64), :] = jnp.where(lane < BOX_OUT, wide[:, at : at + LANE], 0.0)
    for t in range(9):
        turned = d_ref[t * C : t * C + C, :].T
        for n in range(2):
            u_ref[n] = turned[:, n * LANE : n * LANE + LANE]
        for m in range(4):
            here = t * BOX_ROWS + m * SLOT
            parts = [u_ref[n, pl.ds(m, SLOT, stride=4), :] for n in range(2)]
            o_ref[here : here + SLOT, :] = jnp.concatenate(parts, axis=1).astype(BF)


def box_out_kernel(w_ref, b_ref, o_ref, t_ref, d_ref, u_ref):
    u_ref[...] = jnp.zeros_like(u_ref)
    d_ref[9 * C :, :] = jnp.zeros((d_ref.shape[0] - 9 * C, LANE), F32)
    for t in range(9):
        for m in range(4):
            here = t * BOX_ROWS + m * SLOT
            for n in range(2):
                u_ref[n, pl.ds(m, SLOT, stride=4), :] = w_ref[here : here + SLOT, n * LANE : n * LANE + LANE]
        d_ref[t * C : t * C + C, :] = jnp.concatenate([u_ref[0], u_ref[1]], axis=1).T
    lines = [jnp.zeros((40, 2 * C), F32) for _ in range(9)]
    zero = jnp.zeros((40, 2 * C - LANE), F32)
    for s, (r, at) in enumerate(BOX_CUTS):
        wide = jnp.concatenate([d_ref[pl.ds(s, 40, stride=64), :], zero], axis=1)
        lines[r] = lines[r] + (pltpu.roll(wide, at, 1) if at else wide)
    t_ref[...] = jnp.zeros_like(t_ref)
    for r in range(9):
        line = lines[r][:, :C]
        if r:
            line = line + lines[r - 1][:, C:]
        for n in range(2):
            t_ref[n, pl.ds(2 + r, 40, stride=9), :] = line[:, n * LANE : n * LANE + LANE]
    for n in range(2):
        for k in range(2):
            at = k * C + n * LANE
            t_ref[n, k : k + 1, :] = b_ref[:, at : at + LANE]
    rows = o_ref.shape[0]
    o_ref[...] = jnp.concatenate([t_ref[0, 0:rows, :], t_ref[1, 0:rows, :]], axis=1).astype(BF)


def box_call(kernel, shape, kind, name, *args):
    return pl.pallas_call(
        kernel,
        in_specs=[VM] * len(args),
        out_specs=VM,
        out_shape=shape_of(shape, kind),
        scratch_shapes=[
            pltpu.VMEM((2, 368, LANE), F32),
            pltpu.VMEM((40 * 64, LANE), F32),
            pltpu.VMEM((2, LANE, LANE), F32),
        ],
        compiler_params=pltpu.CompilerParams(vmem_limit_bytes=VMEM_LIMIT),
        name=name,
    )(*args)


def heads_call(rows, cols, scal, feats, masks, labels, box_target, full, tb, wct, wb):
    canvases = feats.shape[0]
    own = rows * cols
    total = own + 2 * HALO * cols
    spread = jnp.repeat(jnp.eye(SLOT, 9, dtype=BF), LANE, axis=1)

    def per(shape):
        return pl.BlockSpec((1,) + shape, lambda c: (c,) + (0,) * len(shape))

    return pl.pallas_call(
        functools.partial(head_kernel, cols, rows),
        grid=(canvases,),
        in_specs=[
            pl.BlockSpec(memory_space=pltpu.SMEM),
            pl.BlockSpec((1, 3, total, C), lambda c: (c, 0, 0, 0), pipeline_mode=pl.Buffered(1)),
            per((SLOT, total)),
            per((SLOT, total)),
            per((4, SLOT, total)),
            whole(spread.shape),
            whole(full.shape),
            whole(tb.shape),
            whole(wct.shape),
            whole(wb.shape),
        ],
        out_specs=[
            whole((WIDE, 9 * C)),
            whole((2 * C, 9 * C)),
            whole((9 * BOX_ROWS, C)),
            whole((1, 2 * C)),
            per((2, own, LANE)),
            whole((16, 256)),
        ],
        out_shape=[
            shape_of((WIDE, 9 * C)),
            shape_of((2 * C, 9 * C)),
            shape_of((9 * BOX_ROWS, C)),
            shape_of((1, 2 * C)),
            shape_of((canvases, 2, own, LANE)),
            shape_of((16, 256)),
        ],
        scratch_shapes=[
            pltpu.VMEM((9, total, LANE), BF),
            pltpu.VMEM((total - 2 * cols, 2 * C), F32),
            pltpu.VMEM((total, C), BF),
            pltpu.VMEM((WIDE, own + 512), BF),
            pltpu.VMEM((own + 512, WIDE), BF),
            pltpu.VMEM((own + 256, 2 * C), BF),
            pltpu.VMEM((9 * C, 2 * C), BF),
        ],
        compiler_params=pltpu.CompilerParams(vmem_limit_bytes=VMEM_LIMIT),
        name="heads",
    )(scal, feats, masks, labels, box_target, spread, full, tb, wct, wb)


def place():
    img = lax.axis_index("img")
    cls = lax.axis_index("cls")
    return img // 2, img % 2, cls // 2, cls % 2


def target(z, y, x, c):
    return (z * 2 + y, x * 2 + c)


def owner(z, y, x, c):
    return ((z * 2 + y) * 2 + x) * 2 + c


def enter(peers):
    barrier = pltpu.get_barrier_semaphore()
    for peer in peers:
        pl.semaphore_signal(barrier, inc=1, device_id=peer, device_id_type=MESH)
    pl.semaphore_wait(barrier, len(peers))


class Mail:
    def __init__(self, send_sems, recv_sems):
        self.send_sems, self.recv_sems, self.used, self.sent = send_sems, recv_sems, 0, []

    def push(self, source, landing, peer):
        copy = pltpu.make_async_remote_copy(
            src_ref=source,
            dst_ref=landing,
            send_sem=self.send_sems.at[self.used],
            recv_sem=self.recv_sems.at[self.used],
            device_id=peer,
            device_id_type=MESH,
        )
        self.used += 1
        copy.start()
        self.sent.append(copy)
        return copy

    def close(self):
        for copy in self.sent:
            copy.wait_send()


def window_row(index, shard):
    return pl.multiple_of((index * shard + LEAD * C) // (16 * C) * 16, 16)


def gather_kernel(shard, s_ref, k_ref, n_ref, full_ref, head_ref, count_ref, first_ref, last_ref, sh_ref, kx_ref, send_sems, recv_sems):
    z, y, x, c = place()
    block = k_ref.shape[0]
    win = s_ref.shape[0]
    others = [(k, j) for k in range(4) for j in range(2) if k or j]
    ring = [((z + k) % 4, (y + j) % 2) for k, j in others]
    enter([target(zz, yy, x, c) for zz, yy in ring] + [target(z, y, 1 - x, c), target(z, y, x, 1 - c)])
    mail = Mail(send_sems, recv_sems)
    me = owner(z, y, x, c)

    def rows(zz, yy):
        return pl.ds(pl.multiple_of((zz * 2 + yy) * block, 16), block)

    def lanes(cc):
        return pl.ds(pl.multiple_of(cc * HALF, LANE), HALF)

    got_kx = mail.push(k_ref, kx_ref, target(z, y, 1 - x, c))
    counts = [mail.push(n_ref, count_ref.at[z * 2 + y], target(zz, yy, x, c)) for zz, yy in ring]
    slot = sh_ref.at[me]
    got_z = [mail.push(s_ref, slot, target((z + k) % 4, y, x, c)) for k in range(1, 4)]
    got_y = [mail.push(s_ref, slot, target(z, 1 - y, x, c))]
    got_x = [mail.push(s_ref, slot, target(z, y, 1 - x, c))]
    got_c = [mail.push(s_ref, slot, target(z, y, x, 1 - c))]
    count_ref[z * 2 + y] = n_ref[...]
    sh_ref[me] = s_ref[...]

    got_kx.wait_recv()
    mine = head_ref.at[rows(z, y), lanes(c)]
    head_ref[rows(z, y), lanes(c)] = k_ref[...] + kx_ref[...]
    got_kz = [mail.push(mine, mine, target((z + k) % 4, y, x, c)) for k in range(1, 4)]
    got_ky = [mail.push(mine, mine, target(z, 1 - y, x, c))]
    got_kc = [mail.push(mine, mine, target(z, y, x, 1 - c))]

    for k in range(1, 4):
        got_z[k - 1].wait_recv()
        slot = sh_ref.at[owner((z + 4 - k) % 4, y, x, c)]
        got_y.append(mail.push(slot, slot, target(z, 1 - y, x, c)))
        got_x.append(mail.push(slot, slot, target(z, y, 1 - x, c)))
        got_c.append(mail.push(slot, slot, target(z, y, x, 1 - c)))
    for k in range(1, 4):
        got_kz[k - 1].wait_recv()
        part = head_ref.at[rows((z + 4 - k) % 4, y), lanes(c)]
        got_ky.append(mail.push(part, part, target(z, 1 - y, x, c)))
        got_kc.append(mail.push(part, part, target(z, y, x, 1 - c)))
    for k in range(4):
        got_y[k].wait_recv()
        slot = sh_ref.at[owner((z + 4 - k) % 4, 1 - y, x, c)]
        got_x.append(mail.push(slot, slot, target(z, y, 1 - x, c)))
        got_c.append(mail.push(slot, slot, target(z, y, x, 1 - c)))
    for k in range(4):
        got_ky[k].wait_recv()
        part = head_ref.at[rows((z + 4 - k) % 4, 1 - y), lanes(c)]
        got_kc.append(mail.push(part, part, target(z, y, x, 1 - c)))
    for k in range(8):
        got_x[k].wait_recv()
        slot = sh_ref.at[owner((z + 4 - k % 4) % 4, (y + k // 4) % 2, 1 - x, c)]
        got_c.append(mail.push(slot, slot, target(z, y, x, 1 - c)))
    for copy in got_c + got_kc + counts:
        copy.wait_recv()
    full_ref[...] = jnp.zeros_like(full_ref)

    def merge(d, carry):
        full_ref[pl.ds(window_row(d, shard), win), :] += sh_ref[d]
        return carry

    lax.fori_loop(0, 32, merge, 0)
    first_ref[...] = full_ref[0:TOWER_ROW, :]
    last_ref[...] = full_ref[TAIL_ROW:FULL_ROWS, :]
    mail.close()


def scatter_kernel(
    shard, head_ref, tower_ref, tail_ref, k_ref, n_ref, s_out, k_out, n_out,
    full_ref, sc_ref, sx_ref, sy_ref, sz_ref, kc_ref, ky_ref, kz_ref, kx_ref, mine_ref, peer_ref, far_ref, nz_ref, send_sems, recv_sems,
):
    z, y, x, c = place()
    block = kx_ref.shape[1]
    win = s_out.shape[0]
    enter([target((z + k) % 4, y, x, c) for k in range(1, 4)] + [target(z, 1 - y, x, c), target(z, y, 1 - x, c), target(z, y, x, 1 - c)])
    mail = Mail(send_sems, recv_sems)

    def rows(zz, yy):
        return pl.ds(pl.multiple_of((zz * 2 + yy) * block, 16), block)

    def lanes(cc):
        return pl.ds(pl.multiple_of(cc * HALF, LANE), HALF)

    def window(zz, yy, xx, cc):
        return pl.ds(window_row(owner(zz, yy, xx, cc), shard), win)

    mine_ref[0] = n_ref[...]
    sum_c = mail.push(mine_ref.at[0], peer_ref.at[0], target(z, y, x, 1 - c))
    spots = [(j, k) for j in (1, 0) for k in (1, 2, 3, 0)]
    got_kc = []
    for n, (j, k) in enumerate(spots):
        part = k_ref.at[rows((z + k) % 4, (y + j) % 2), lanes(1 - c)]
        got_kc.append(mail.push(part, kc_ref.at[n], target(z, y, x, 1 - c)))
    full_ref[0:TOWER_ROW, :] = head_ref[...]
    full_ref[TOWER_ROW:TAIL_ROW, :] = tower_ref[...]
    full_ref[TAIL_ROW:FULL_ROWS, :] = tail_ref[...]
    got_c = []
    for i in (1, 0):
        for n, (j, k) in enumerate(spots):
            part = full_ref.at[window((z + k) % 4, (y + j) % 2, (x + i) % 2, 1 - c), :]
            got_c.append(mail.push(part, sc_ref.at[(1 - i) * 8 + n], target(z, y, x, 1 - c)))

    sum_c.wait_recv()
    mine_ref[1] = mine_ref[0] + peer_ref[0]
    sum_x = mail.push(mine_ref.at[1], peer_ref.at[1], target(z, y, 1 - x, c))

    got_ky = []
    for n, (j, k) in enumerate(spots):
        got_kc[n].wait_recv()
        kc_ref[n] = kc_ref[n] + k_ref[rows((z + k) % 4, (y + j) % 2), lanes(c)]
        if j == 1:
            got_ky.append(mail.push(kc_ref.at[n], ky_ref.at[n], target(z, 1 - y, x, c)))
    got_x = []
    for n, (j, k) in enumerate(spots):
        got_c[n].wait_recv()
        sc_ref[n] = sc_ref[n] + full_ref[window((z + k) % 4, (y + j) % 2, 1 - x, c), :]
        got_x.append(mail.push(sc_ref.at[n], sx_ref.at[n], target(z, y, 1 - x, c)))

    sum_x.wait_recv()
    mine_ref[2] = mine_ref[1] + peer_ref[1]
    sum_y = mail.push(mine_ref.at[2], peer_ref.at[2], target(z, 1 - y, x, c))

    got_kz = []
    for n in range(4):
        got_ky[n].wait_recv()
        kc_ref[4 + n] = kc_ref[4 + n] + ky_ref[n]
        if n < 3:
            got_kz.append(mail.push(kc_ref.at[4 + n], kz_ref.at[n], target((z + n + 1) % 4, y, x, c)))
    got_y = []
    for n, (j, k) in enumerate(spots):
        got_c[8 + n].wait_recv()
        got_x[n].wait_recv()
        total = sc_ref[8 + n].astype(F32) + full_ref[window((z + k) % 4, (y + j) % 2, x, c), :].astype(F32)
        sc_ref[8 + n] = (total + sx_ref[n].astype(F32)).astype(BF)
        if j == 1:
            got_y.append(mail.push(sc_ref.at[8 + n], sy_ref.at[n], target(z, 1 - y, x, c)))

    sum_y.wait_recv()
    mine_ref[3] = mine_ref[2] + peer_ref[2]
    nz_ref[z] = mine_ref[3]
    sum_z = [mail.push(mine_ref.at[3], nz_ref.at[z], target((z + k) % 4, y, x, c)) for k in range(1, 4)]

    total = kc_ref[7].astype(F32)
    for n in range(3):
        got_kz[n].wait_recv()
        total += kz_ref[n].astype(F32)
    kx_ref[0] = total.astype(BF)
    got_kx = mail.push(kx_ref.at[0], kx_ref.at[1], target(z, y, 1 - x, c))
    got_z = []
    for n in range(4):
        got_y[n].wait_recv()
        sc_ref[12 + n] = sc_ref[12 + n] + sy_ref[n]
        if n < 3:
            got_z.append(mail.push(sc_ref.at[12 + n], sz_ref.at[n], target((z + n + 1) % 4, y, x, c)))
    total = sc_ref[15].astype(F32)
    for n in range(3):
        got_z[n].wait_recv()
        total += sz_ref[n].astype(F32)
    s_out[...] = total
    for copy in sum_z:
        copy.wait_recv()
    n_out[...] = (nz_ref[0] + nz_ref[1]) + (nz_ref[2] + nz_ref[3])
    got_kx.wait_recv()
    k_out[...] = kx_ref[0].astype(F32) + kx_ref[1].astype(F32)
    mail.close()


def fast_mesh(img_parts, cls_parts, class_rows):
    return img_parts == 8 and cls_parts == 4 and class_rows % 16 == 0


def flat_place(index, shard):
    return (index * shard + LEAD * C) % (16 * C)


def gather_all(shared_params, class_params, count):
    img, cls = lax.axis_index("img"), lax.axis_index("cls")
    img_parts, cls_parts = lax.axis_size("img"), lax.axis_size("cls")
    shard = shared_params.shape[0]
    block, part = class_params.shape
    if not fast_mesh(img_parts, cls_parts, block):
        flat = lax.all_gather(shared_params.astype(BF), ("img", "cls"), axis=0, tiled=True)
        full = jnp.pad(flat, (LEAD * C, FULL_ROWS * C - LEAD * C - flat.shape[0])).reshape(FULL_ROWS, C)
        head = lax.all_gather(class_params.astype(BF), ("img", "cls"), axis=0)
        head = head.reshape(img_parts, cls_parts, block, part).transpose(0, 2, 1, 3).reshape(-1, CLS_OUT)
        pieces = []
        for half in range(2):
            pieces += [head[:, 180 * half : 180 * half + 180], head[:, 360 + 180 * half : 540 + 180 * half]]
            pieces.append(jnp.zeros((head.shape[0], HALF - 360), BF))
        return full, full[:TOWER_ROW], full[TAIL_ROW:], jnp.concatenate(pieces, axis=1), lax.psum(count, "img")
    rows = -(-(shard + 16 * C) // (16 * C)) * 16
    window = lax.dynamic_update_slice(
        jnp.zeros((rows * C,), BF), shared_params.astype(BF), (flat_place(img * cls_parts + cls, shard),)
    ).reshape(rows, C)
    wide = jnp.pad(class_params.astype(BF), ((0, 0), (part, HALF - part)))
    wide = lax.dynamic_slice_in_dim(
        jnp.pad(wide, ((0, 0), (0, part))), jnp.where(cls // 2 == 0, part, 0), HALF, 1
    )
    number = jnp.broadcast_to(count, (8, LANE))
    full, head, counts, first, last = pl.pallas_call(
        functools.partial(gather_kernel, shard),
        in_specs=[VM, VM, VM],
        out_specs=[VM] * 5,
        out_shape=[
            shape_of((FULL_ROWS, C), BF),
            shape_of((img_parts * block, 2 * HALF), BF),
            shape_of((img_parts, 8, LANE)),
            shape_of((TOWER_ROW, C), BF),
            shape_of((FULL_ROWS - TAIL_ROW, C), BF),
        ],
        scratch_shapes=[
            pltpu.VMEM((img_parts * cls_parts, rows, C), BF),
            pltpu.VMEM((block, HALF), BF),
            pltpu.SemaphoreType.DMA((54,)),
            pltpu.SemaphoreType.DMA((54,)),
        ],
        compiler_params=pltpu.CompilerParams(collective_id=0, has_side_effects=True, vmem_limit_bytes=VMEM_LIMIT),
        name="gather",
    )(window, wide, number)
    return full, first, last, head, jnp.sum(counts[:, 0, 0])


def scatter_all(head, tower, tail, class_grad, sums, shard, block, part):
    img, cls = lax.axis_index("img"), lax.axis_index("cls")
    img_parts, cls_parts = lax.axis_size("img"), lax.axis_size("cls")
    if not fast_mesh(img_parts, cls_parts, block):
        flat = jnp.concatenate([head, tower, tail], axis=0).reshape(-1)
        flat = flat[LEAD * C : LEAD * C + shard * img_parts * cls_parts].astype(F32)
        shared = lax.psum_scatter(flat, ("img", "cls"), scatter_dimension=0, tiled=True)
        pieces = [class_grad[:, at : at + 180] for at in (0, HALF, 180, HALF + 180)]
        whole_grad = lax.psum_scatter(
            jnp.concatenate(pieces, axis=1).astype(F32), "img", scatter_dimension=0, tiled=True
        )
        return shared, lax.psum_scatter(whole_grad, "cls", scatter_dimension=1, tiled=True), lax.psum(sums, ("img", "cls"))
    rows = -(-(shard + 16 * C) // (16 * C)) * 16
    window, wide, sums = pl.pallas_call(
        functools.partial(scatter_kernel, shard),
        in_specs=[VM] * 5,
        out_specs=[VM] * 3,
        out_shape=[shape_of((rows, C)), shape_of((block, HALF)), shape_of(sums.shape)],
        scratch_shapes=[
            pltpu.VMEM((FULL_ROWS, C), BF),
            pltpu.VMEM((16, rows, C), BF),
            pltpu.VMEM((8, rows, C), BF),
            pltpu.VMEM((4, rows, C), BF),
            pltpu.VMEM((3, rows, C), BF),
            pltpu.VMEM((8, block, HALF), BF),
            pltpu.VMEM((4, block, HALF), BF),
            pltpu.VMEM((3, block, HALF), BF),
            pltpu.VMEM((2, block, HALF), BF),
            pltpu.VMEM((4,) + sums.shape, F32),
            pltpu.VMEM((3,) + sums.shape, F32),
            pltpu.VMEM((8, LANE), F32),
            pltpu.VMEM((4,) + sums.shape, F32),
            pltpu.SemaphoreType.DMA((53,)),
            pltpu.SemaphoreType.DMA((53,)),
        ],
        compiler_params=pltpu.CompilerParams(collective_id=1, has_side_effects=True, vmem_limit_bytes=VMEM_LIMIT),
        name="scatter",
    )(head, tower, tail, class_grad, sums)
    flat = lax.dynamic_slice_in_dim(window.reshape(-1), flat_place(img * cls_parts + cls, shard), shard)
    grad = lax.dynamic_slice_in_dim(wide, jnp.where(cls // 2 == 0, 0, part), part, 1)
    return flat, grad, sums


def turn_kernel(k_ref, o_ref):
    o_ref[...] = k_ref[...].T


def turn(head):
    return pl.pallas_call(
        turn_kernel,
        grid=(9,),
        in_specs=[pl.BlockSpec((C, 2 * HALF), lambda t: (t, 0))],
        out_specs=pl.BlockSpec((2 * HALF, C), lambda t: (0, t)),
        out_shape=shape_of((2 * HALF, 9 * C), BF),
        name="turn",
    )(head)


def turn_back_kernel(k_ref, t_ref, ko_ref, to_ref):
    ko_ref[...] = k_ref[...].astype(BF).T
    for n in range(2):
        to_ref[n] = t_ref[n * C : n * C + C, :].astype(BF).T


def turn_back(class_grad, tower_grad):
    return pl.pallas_call(
        turn_back_kernel,
        grid=(9,),
        in_specs=[pl.BlockSpec((2 * HALF, C), lambda t: (0, t)), pl.BlockSpec((2 * C, C), lambda t: (0, t))],
        out_specs=[pl.BlockSpec((C, 2 * HALF), lambda t: (t, 0)), pl.BlockSpec((2, C, C), lambda t: (0, t, 0))],
        out_shape=[shape_of((9 * C, 2 * HALF), BF), shape_of((2, 9 * C, C), BF)],
        name="turn_back",
    )(class_grad, tower_grad)


def column_plan():
    plan = []
    for half in range(2):
        for group in range(2):
            column, row, end = 360 * group + 180 * half, HALF * half + 180 * group, 360 * group + 180 * half + 180
            while column < end:
                count = min(end, (column // CLASSES + 1) * CLASSES) - column
                plan.append((row, count, column // CLASSES, column % CLASSES))
                column, row = column + count, row + count
        plan.append((HALF * half + 360, HALF - 360, -1, 0))
    return plan


def adamw_update(weight, first, second, grad):
    first_new = MOMENT_ONE * first + (1.0 - MOMENT_ONE) * grad
    second_new = MOMENT_TWO * second + (1.0 - MOMENT_TWO) * grad * grad
    first_hat = first_new / (1.0 - MOMENT_ONE**STEP)
    second_hat = second_new / (1.0 - MOMENT_TWO**STEP)
    weight_new = weight - RATE * (first_hat / (jnp.sqrt(second_hat) + EPSILON) + DECAY * weight)
    return (weight_new, first_new, second_new)


def valid_positives(boxes, match, full_rows, cols):
    place = jnp.arange(full_rows * cols, dtype=jnp.int32)
    row, col = place // cols, place % cols
    inside = jnp.zeros((boxes.shape[0], full_rows * cols), bool)
    for k in range(boxes.shape[1]):
        edge = boxes[:, k, :, None]
        inside |= (row >= edge[:, 0]) & (row < edge[:, 2]) & (col >= edge[:, 1]) & (col < edge[:, 3])
    return ((match >= 0) & inside[:, None]).astype(F32)


def cell_data(boxes, match, gt_labels, gt_deltas, first_row, rows, cols):
    full_rows = match.shape[2] // cols
    total = (rows + 2 * HALO) * cols
    place = jnp.arange(total, dtype=jnp.int32)[None]
    row = place // cols + (first_row - HALO)
    col = place % cols

    def crop(r, j):
        found = jnp.full((boxes.shape[0], total), -1, jnp.int32)
        for k in range(boxes.shape[1]):
            edge = boxes[:, k, :, None]
            inside = (r >= edge[:, 0]) & (r < edge[:, 2]) & (j >= edge[:, 1]) & (j < edge[:, 3])
            found = jnp.where(inside, k, found)
        return jnp.where((r >= 0) & (r < full_rows) & (j >= 0) & (j < cols), found, -1)

    centre = crop(row, col)
    valid = centre >= 0
    masks = jnp.stack([(crop(row + di, col + dj) == centre) & valid for di, dj in TAPS], axis=1)
    masks = jnp.pad(masks.astype(BF), ((0, 0), (0, SLOT - 9), (0, 0)))
    edge = HALO * cols
    near = jnp.pad(match, ((0, 0), (0, 0), (edge, edge)), constant_values=-2)
    near = lax.dynamic_slice_in_dim(near, first_row * cols, total, 2)
    near = jnp.where(valid[:, None], near, -2)
    near = jnp.pad(near, ((0, 0), (0, SLOT - 9), (0, 0)), constant_values=-2)
    labels = near
    targets = jnp.zeros((near.shape[0], 4) + near.shape[1:], F32)
    for g in range(gt_labels.shape[1]):
        labels = jnp.where(near == g, gt_labels[:, g, None, None], labels)
        targets = jnp.where((near == g)[:, None], gt_deltas[:, g, :, None, None], targets)
    return masks, labels.astype(F32), targets


def local(patches, boxes, match, gt_labels, gt_deltas, ema_old, shared_params, shared_m, shared_v, class_params, class_m, class_v):
    cls_rank = lax.axis_index("cls")
    cls_parts = lax.axis_size("cls")
    canvases, rows, width = patches.shape
    cols = width // PATCH
    masks, labels, targets = cell_data(boxes, match, gt_labels, gt_deltas, cls_rank * rows, rows, cols)
    full_rows = match.shape[2] // cols
    count = jnp.sum(valid_positives(boxes, match, full_rows, cols))
    full, first, last, head, positives = gather_all(shared_params, class_params, count)
    norm = jnp.maximum(positives, 1.0)
    ema_new = EMA_KEEP * ema_old + (1.0 - EMA_KEEP) * norm
    down = lax.ppermute(patches[:, rows - HALO :], "cls", [(i, i + 1) for i in range(cls_parts - 1)])
    up = lax.ppermute(patches[:, :HALO], "cls", [(i + 1, i) for i in range(cls_parts - 1)])
    rim = jnp.concatenate([down, up], axis=1).reshape(canvases * 2 * HALO, width)
    tb = last[0:2].reshape(1, 2 * C).astype(F32)
    wb = box_call(box_in_kernel, (9 * BOX_ROWS, C), BF, "box_in", last)
    stem_pre, stem_out, feats, lat_w = stem_forward(patches, rim, first)
    scal = jnp.stack([1.0 / ema_new, 1.0 / norm])
    dwc, dwt, dwb, db, feature_grad, sums = heads_call(
        rows, cols, scal, feats, masks, labels, targets, full, tb, turn(head), wb
    )
    first_grad = stem_backward(patches, feature_grad, stem_out, stem_pre, lat_w)
    class_turned, tower_turned = turn_back(dwc, dwt)
    last_grad = box_call(box_out_kernel, last.shape, BF, "box_out", dwb, db)
    shared_grad, class_grad, sums = scatter_all(
        first_grad, tower_turned.reshape(18 * C, C), last_grad, class_turned, sums, shared_params.shape[0], *class_params.shape
    )
    loss = jnp.sum(sums[0:8]) / ema_new + jnp.sum(sums[8:16]) / norm
    return (
        loss,
        ema_new,
        *adamw_update(shared_params, shared_m, shared_v, shared_grad),
        *adamw_update(class_params, class_m, class_v, class_grad),
    )


def solution(mesh):
    spread = P(("img", "cls"))
    block = P("img", "cls")
    return jax.shard_map(
        local,
        mesh=mesh,
        in_specs=(
            P("img", "cls", None),
            P("img", None, None),
            P("img", None, None),
            P("img", None),
            P("img", None, None),
            P(),
            spread,
            spread,
            spread,
            block,
            block,
            block,
        ),
        out_specs=(P(), P(), spread, spread, spread, block, block, block),
        check_vma=False,
    )
```

```python
import functools

import jax
import jax.numpy as jnp
from jax import lax
from jax.experimental import pallas as pl
from jax.experimental.pallas import tpu as pltpu
from jax.sharding import PartitionSpec as P

C = 256
CLASSES = 80
ANCH = 9
PATCH = 192
BOX_OUT = 36
CLS_OUT = ANCH * CLASSES
STEP = 5
GT = 16
HALO = 4
SLOT = 16
BOX_ROWS = 4 * SLOT
LANE = 128
WIDE = 768
GROUP = 16

PRIOR = -4.59511985013459
ALPHA = 0.25
HUBER = 1.0 / 9.0
EMA_KEEP = 0.9
RATE = 0.01
MOMENT_ONE = 0.5
MOMENT_TWO = 0.5
DECAY = 0.05
EPSILON = 1e-08

LENGTHS = [PATCH * C, C, C * C, C, 18 * C * C, 2 * C, 9 * C * BOX_OUT]
TOWER_AT = sum(LENGTHS[:4]) // C
LEAD = -TOWER_AT % 16
TOWER_ROW = TOWER_AT + LEAD
TAIL_ROW = TOWER_ROW + 18 * C
FULL_ROWS = -(-(LEAD + sum(LENGTHS) // C) // 16) * 16
HALF = 384
MESH = pl.DeviceIdType.MESH

BF = jnp.bfloat16
F32 = jnp.float32
TAPS = [(di, dj) for di in (-1, 0, 1) for dj in (-1, 0, 1)]
NN = (((1,), (0,)), ((), ()))
NT = (((1,), (1,)), ((), ()))
TN = (((0,), (0,)), ((), ()))
K0 = 0.7978845608028654
K1 = 0.044715


def mm(a, b, dims=NN):
    return lax.dot_general(a, b, dims, preferred_element_type=F32)


def gelu(x):
    return 0.5 * x * (1.0 + jnp.tanh(K0 * (x + K1 * x * x * x)))


def gelu_slope(x):
    square = x * x
    th = jnp.tanh(K0 * (x + K1 * x * square))
    return 0.5 * (1.0 + th) + (0.5 * K0) * x * (1.0 - th * th) * (1.0 + 3.0 * K1 * square)


def columns_of(x, pairs, width):
    return [x[:, width * k : width * (k + 1)] for k in range(pairs)]


def stem_kernel(pairs, cols, rows, x_ref, h_ref, head_ref, pre_ref, so_ref, f_ref, lw_ref, t_ref, w_ref, b_ref, lb_ref):
    step = pl.program_id(0)
    canvases = x_ref.shape[0]
    own_rows = canvases * rows
    total = (rows + 2 * HALO) * cols

    @pl.when(step == 0)
    def _():
        head = head_ref[...].astype(F32)
        w_ref[...] = jnp.zeros_like(w_ref)
        stem_w = head[LEAD : LEAD + PATCH].astype(BF)
        w_ref[:PATCH, :C] = stem_w
        w_ref[PATCH:, C:] = stem_w
        bias = head[LEAD + PATCH : LEAD + PATCH + 1]
        b_ref[...] = jnp.concatenate([bias, bias], axis=1)
        lw_ref[...] = head[LEAD + PATCH + 1 : TOWER_ROW - 1].astype(BF)
        lb_ref[...] = head[TOWER_ROW - 1 : TOWER_ROW]
        for c in range(canvases):
            for n in range(2):
                t_ref[c, n, 0:8, :] = jnp.zeros((8, LANE), F32)
                t_ref[c, n, 8 + total : 16 + total, :] = jnp.zeros((8, LANE), F32)

    x = x_ref[...].reshape(own_rows, x_ref.shape[2])
    own = columns_of(x, pairs, 2 * PATCH)
    rim = columns_of(h_ref[...], pairs, 2 * PATCH)
    pre = mm(jnp.concatenate(own + rim, axis=0), w_ref[...]) + b_ref[...]
    count = pairs * own_rows
    pre_ref[...] = pre[:count]
    out = gelu(pre).astype(BF)
    so_ref[...] = out[:count]
    for half in range(2):
        feat = mm(out[:, half * C : half * C + C], lw_ref[...]) + lb_ref[...]
        for k in range(pairs):
            j = step * 2 * pairs + 2 * k + half
            for c in range(canvases):
                at = k * own_rows + c * rows
                rim_at = count + k * 2 * HALO * canvases + c * 2 * HALO
                for n in range(2):
                    side = slice(n * LANE, n * LANE + LANE)
                    place = pl.ds(8 + HALO * cols + j, rows, stride=cols)
                    t_ref[c, n, place, :] = feat[at : at + rows, side]
                    place = pl.ds(8 + j, HALO, stride=cols)
                    t_ref[c, n, place, :] = feat[rim_at : rim_at + HALO, side]
                    place = pl.ds(8 + (HALO + rows) * cols + j, HALO, stride=cols)
                    t_ref[c, n, place, :] = feat[rim_at + HALO : rim_at + 2 * HALO, side]

    @pl.when(step == pl.num_programs(0) - 1)
    def _():
        piece = 4 * cols

        def move(i, carry):
            base = pl.multiple_of(i * piece, 16)
            for c in range(canvases):
                for n in range(2):
                    value = t_ref[c, n, pl.ds(base, piece + 16), :]
                    for k in range(3):
                        moved = value[7 + k : 7 + k + piece].astype(BF)
                        f_ref[c, k, pl.ds(base, piece), n * LANE : n * LANE + LANE] = moved
            return carry

        lax.fori_loop(0, total // piece, move, 0)


def stem_back_kernel(pairs, cols, rows, x_ref, fg_ref, so_ref, pre_ref, lw_ref, head_ref, sw_out, sb_out, lw_out, lb_out, h_ref):
    step = pl.program_id(0)
    canvases = x_ref.shape[0]

    @pl.when(step == 0)
    def _():
        sw_out[...] = jnp.zeros_like(sw_out)
        sb_out[...] = jnp.zeros_like(sb_out)
        lw_out[...] = jnp.zeros_like(lw_out)
        lb_out[...] = jnp.zeros_like(lb_out)

    x = x_ref[...].reshape(canvases * rows, x_ref.shape[2])
    own = jnp.concatenate(columns_of(x, pairs, 2 * PATCH), axis=0)
    low = []
    for half in range(2):
        parts = []
        for k in range(pairs):
            j = step * 2 * pairs + 2 * k + half
            for c in range(canvases):
                place = pl.ds(j, rows, stride=cols)
                parts.append(jnp.concatenate([fg_ref[c, n, place, :] for n in range(2)], axis=1))
        grad32 = jnp.concatenate(parts, axis=0)
        grad = grad32.astype(BF)
        cut = slice(half * C, half * C + C)
        lw_out[...] += mm(so_ref[:, cut], grad, TN)
        lb_out[...] += jnp.sum(grad32, axis=0, keepdims=True)
        back = mm(grad, lw_ref[...], NT) * gelu_slope(pre_ref[:, cut])
        back = back.astype(BF)
        sb_out[...] += jnp.sum(back.astype(F32), axis=0, keepdims=True)
        low.append(back)
    both = mm(own, jnp.concatenate(low, axis=1), TN)
    sw_out[...] += both[:PATCH, :C] + both[PATCH:, C:]

    @pl.when(step == pl.num_programs(0) - 1)
    def _():
        at = LEAD + PATCH
        h_ref[0:LEAD, :] = jnp.zeros((LEAD, C), F32)
        h_ref[LEAD:at, :] = sw_out[...]
        h_ref[at : at + 1, :] = sb_out[...]
        h_ref[at + 1 : TOWER_ROW - 1, :] = lw_out[...]
        h_ref[TOWER_ROW - 1 :, :] = lb_out[...]
        head_ref[...] = h_ref[...].astype(BF)


def aligned(value, multiple):
    return value if isinstance(value, int) else pl.multiple_of(value, multiple)


def many(mask, count):
    return jnp.concatenate([mask] * count, axis=1)


def weight_sums(canvas, cols, edge, own, grad, source, mx_ref, sum_ref):
    def go(x_ref):
        def triple(n, carry):
            at = pl.multiple_of(edge + cols * (n - 1), 16)
            for k in range(3):
                mask = mx_ref[n * 3 + k, edge : edge + own, :]
                x_ref[:, k * C : k * C + C] = source[k, pl.ds(at, own), :] * many(mask, 2)
            side = pl.ds(pl.multiple_of(n * 3 * C, C), 3 * C)
            sum_ref[:, side] = jnp.where(canvas > 0, sum_ref[:, side], 0.0) + mm(grad(), x_ref[...])
            return carry

        lax.fori_loop(0, 3, triple, 0)

    pl.run_scoped(go, pltpu.VMEM((own, 3 * C), BF))


def head_kernel(
    cols, rows, scal_ref, f_ref, mk_ref, lab_ref, btt_ref, e_ref, full_ref, tb_ref, head_ref, wb_ref,
    class_ref, tower_ref, dwb_ref, db_ref, fg_ref, sums_ref,
    mx_ref, pre_ref, bt_ref, lgt_ref, lgs_ref, g_ref, wt_ref, wct_ref, dwc_ref, dwt_ref, copy_sems,
):
    own = rows * cols
    edge = HALO * cols
    total = own + 2 * edge
    shift = [cols * di + dj for di, dj in TAPS]

    @pl.when(pl.program_id(0) == 0)
    def _():
        dwb_ref[...] = jnp.zeros_like(dwb_ref)
        db_ref[...] = jnp.zeros_like(db_ref)
        sums_ref[...] = jnp.zeros_like(sums_ref)
        def fetch(held_ref):
            copies = [pltpu.make_async_copy(head_ref, held_ref, copy_sems.at[2])]
            for n in range(2):
                rows_of = full_ref.at[TOWER_ROW + n * 9 * C : TOWER_ROW + (n + 1) * 9 * C, :]
                copies.append(pltpu.make_async_copy(rows_of, wt_ref.at[:, n * C : n * C + C], copy_sems.at[n]))
            for copy in copies:
                copy.start()
            copies[0].wait()

            def turn(t, carry):
                at = pl.multiple_of(t * C, C)
                wct_ref[:, pl.ds(at, C)] = held_ref[pl.ds(at, C), :].T
                return carry

            lax.fori_loop(0, 9, turn, 0)
            for copy in copies[1:]:
                copy.wait()

        pl.run_scoped(fetch, pltpu.VMEM((9 * C, WIDE), BF))

    def spread(i, carry):
        at = pl.multiple_of(i * 384, 128)
        wide = mm(mk_ref[0, :, pl.ds(at, 384)], e_ref[...], TN).astype(BF)
        for t in range(9):
            mx_ref[t, pl.ds(at, 384), :] = wide[:, t * LANE : (t + 1) * LANE]
        return carry

    lax.fori_loop(0, total // 384, spread, 0)

    def twice(mask):
        return jnp.concatenate([mask, mask], axis=1)

    def build(source, at, count, x_ref):
        for t, (di, dj) in enumerate(TAPS):
            value = source[dj + 1, pl.ds(pl.multiple_of(at + cols * di, 16), count), :]
            x_ref[:, t * C : (t + 1) * C] = value * twice(mx_ref[t, pl.ds(at, count), :])

    first_tower = cols
    tower_rows = total - 2 * cols
    first_logit = edge - 256
    logit_cells = own + 512
    first_g = edge - 128
    g_cells = own + 256

    def heads(ct32_ref, ct_ref):
        zero = jnp.zeros((cols + 8, C), F32)
        ct32_ref[0 : cols + 8, :] = zero
        ct32_ref[8 + total - cols : 16 + total, :] = zero
        zero = jnp.zeros((cols, C), BF)
        bt_ref[0:cols, :] = zero
        bt_ref[total - cols : total, :] = zero
        piece = tower_rows // 3

        def towers(x_ref):
            def tower(i, carry):
                row = pl.multiple_of(i * piece, 16)
                at = pl.multiple_of(first_tower + i * piece, 16)
                build(f_ref.at[0], at, piece, x_ref)
                pre = mm(x_ref[...], wt_ref[...]) + tb_ref[...]
                pre_ref[pl.ds(row, piece), :] = pre
                out = gelu(pre)
                ct32_ref[pl.ds(pl.multiple_of(8 + at, 8), piece), :] = out[:, :C]
                bt_ref[pl.ds(at, piece), :] = out[:, C:].astype(BF)
                return carry

            lax.fori_loop(0, 3, tower, 0)

        pl.run_scoped(towers, pltpu.VMEM((piece, 9 * C), BF))

        def move(i, carry):
            base = pl.multiple_of(i * edge, 16)
            value = ct32_ref[pl.ds(base, edge + 16), :]
            for k in range(3):
                ct_ref[k, pl.ds(base, edge), :] = value[7 + k : 7 + k + edge].astype(BF)
            return carry

        lax.fori_loop(0, total // edge, move, 0)
        def logits(xa_ref, la_ref):
            inv_ema = scal_ref[0]
            number = lax.broadcasted_iota(jnp.int32, (GROUP, 256), 0).astype(F32)
            lane = lax.broadcasted_iota(jnp.int32, (8, 256), 1)
            plan = column_plan()

            def ready(q, x_ref):
                build(ct_ref, pl.multiple_of(first_logit + q * 256, 128), 256, x_ref)

            def work(q, x_ref, l_ref):
                l_ref[...] = mm(wct_ref[...], x_ref[...], NT)

            def focal(q, l_ref):
                row = pl.multiple_of(q * 256, 128)
                at = pl.multiple_of(first_logit + row, 128)
                spot = lane + at
                mine = (spot >= edge) & (spot < edge + own)
                lines = [lab_ref[0, a : a + 1, pl.ds(at, 256)] for a in range(ANCH)]
                rest = [jnp.where(line > -1.5, 1.0 - ALPHA, 0.0) for line in lines]
                pulls = [line * inv_ema for line in rest]
                total_focal = jnp.zeros((8, 256), F32)
                for first in range(0, WIDE, GROUP):
                    value = l_ref[first : first + GROUP, :] + PRIOR
                    key = None
                    for begin, count, anchor, klass in plan:
                        if begin >= first + GROUP or begin + count <= first:
                            continue
                        if anchor < 0:
                            parts = [jnp.full((GROUP, 256), n, F32) for n in (-2.0, 0.0, 0.0)]
                        else:
                            parts = [lines[anchor] - float(klass - (begin - first)), rest[anchor], pulls[anchor]]
                            parts = [jnp.broadcast_to(part, (GROUP, 256)) for part in parts]
                        if key is None:
                            key, other, pull_other = parts
                        else:
                            later = number >= float(begin - first)
                            key = jnp.where(later, parts[0], key)
                            other = jnp.where(later, parts[1], other)
                            pull_other = jnp.where(later, parts[2], pull_other)
                    hit = key == number
                    side = jnp.where(hit, -value, value)
                    small = jnp.exp(-jnp.abs(side))
                    whole_one = 1.0 + small
                    ratio = pltpu.reciprocal(whole_one, approx=True)
                    ratio = ratio * (2.0 - whole_one * ratio)
                    part = small * ratio
                    up = side >= 0.0
                    prob = jnp.where(up, ratio, part)
                    miss = jnp.where(up, part, ratio)
                    tiny = small * (1.0 - 0.5 * small)
                    cross = jnp.maximum(side, 0.0) + jnp.where(small < 0.001, tiny, jnp.log(whole_one))
                    square = prob * prob
                    value = square * cross * jnp.where(hit, ALPHA, other)
                    pull = square * (2.0 * miss * cross + prob) * jnp.where(hit, -ALPHA * inv_ema, pull_other)
                    l_ref[first : first + GROUP, :] = pull
                    lgt_ref[first : first + GROUP, pl.ds(row, 256)] = pull.astype(BF)
                    total_focal += jnp.sum(value.reshape(GROUP // 8, 8, 256), axis=0)
                sums_ref[0:8, :] += jnp.where(mine, total_focal, 0.0)
                lgs_ref[pl.ds(row, 256), :] = l_ref[...].T.astype(BF)

            def logits_of(q, carry):
                ready(q, xa_ref)
                work(q, xa_ref, la_ref)
                focal(q, la_ref)
                return carry

            lax.fori_loop(0, logit_cells // 256, logits_of, 0)

        pl.run_scoped(logits, pltpu.VMEM((256, 9 * C), BF), pltpu.VMEM((WIDE, 256), F32))
        weight_sums(pl.program_id(0), cols, edge, own, lambda: lgt_ref[:, 256 : 256 + own], ct_ref, mx_ref, dwc_ref)

    pl.run_scoped(heads, pltpu.VMEM((total + 16, C), F32), pltpu.VMEM((3, total, C), BF))

    def box_forward(gg_ref, y_ref):
        inv_norm = scal_ref[1]

        def outer(i, carry):
            at = pl.multiple_of(i * 768, 128)
            y_ref[:, pl.ds(at, 768)] = mm(wb_ref[...], bt_ref[pl.ds(at, 768), :], NT)
            return carry

        lax.fori_loop(0, total // 768, outer, 0)
        lane = lax.broadcasted_iota(jnp.int32, (SLOT, total), 1)
        mine = (lane >= edge) & (lane < edge + own)

        def guess(m, carry):
            acc = jnp.zeros((SLOT, total), F32)
            for t in range(9):
                value = y_ref[pl.ds(pl.multiple_of(t * BOX_ROWS + m * SLOT, 8), SLOT), :]
                moved = pltpu.roll(value, (-shift[t]) % total, 1)
                acc += moved * mk_ref[0, t : t + 1, :].astype(F32)
            differ = acc - btt_ref[0, m]
            positive = lab_ref[0] >= 0.0
            size = jnp.abs(differ)
            loss = jnp.where(size < HUBER, 0.5 * differ * differ / HUBER, size - 0.5 * HUBER)
            loss = jnp.where(positive & mine, loss, 0.0)
            part = loss[:, 0:256]
            for k in range(1, total // 256):
                part += loss[:, k * 256 : (k + 1) * 256]
            sums_ref[8:16, :] += part[0:8] + part[8:16]
            pull = jnp.minimum(jnp.maximum(differ / HUBER, -1.0), 1.0) * inv_norm
            pull = jnp.where(positive, pull, 0.0)
            gg_ref[pl.ds(pl.multiple_of(m * SLOT, 8), SLOT), :] = pull
            return carry

        lax.fori_loop(0, 4, guess, 0)

    def box_back(gg_ref, xg_ref):
        for t in range(9):
            moved = pltpu.roll(gg_ref[...], shift[t] % total, 1)
            xg_ref[t * BOX_ROWS : (t + 1) * BOX_ROWS, :] = (moved * mk_ref[0, 8 - t : 9 - t, :].astype(F32)).astype(BF)
        dwb_ref[...] += mm(xg_ref[:, edge : edge + own], bt_ref[edge : edge + own, :])

        def into(q, carry):
            row = pl.multiple_of(q * 256, 128)
            grad = mm(xg_ref[:, pl.ds(pl.multiple_of(first_g + row, 128), 256)], wb_ref[...], TN)
            pre = pre_ref[pl.ds(pl.multiple_of(first_g - first_tower + row, 16), 256), C:]
            g_ref[pl.ds(row, 256), C:] = (grad * gelu_slope(pre)).astype(BF)
            return carry

        lax.fori_loop(0, g_cells // 256, into, 0)

    def boxes(gg_ref):
        pl.run_scoped(functools.partial(box_forward, gg_ref), pltpu.VMEM((9 * BOX_ROWS, total), F32))
        pl.run_scoped(functools.partial(box_back, gg_ref), pltpu.VMEM((9 * BOX_ROWS, total), BF))

    pl.run_scoped(boxes, pltpu.VMEM((BOX_ROWS, total), F32))

    def class_back(z_ref):
        z_ref[:, 0:8, :] = jnp.zeros((3, 8, C), F32)
        z_ref[:, 8 + g_cells : 16 + g_cells, :] = jnp.zeros((3, 8, C), F32)
        piece = g_cells // 4

        def multiply(i, carry):
            row = pl.multiple_of(i * piece, 16)
            for k in range(3):
                acc = jnp.zeros((piece, C), F32)
                for r in range(3):
                    t = r * 3 + k
                    source = row + first_g - cols * (r - 1)
                    mask = mx_ref[t, pl.ds(pl.multiple_of(source, 16), piece), :]
                    value = lgs_ref[pl.ds(pl.multiple_of(source - first_logit, 16), piece), :]
                    value = value * jnp.concatenate([mask] * (WIDE // LANE), axis=1)
                    acc += mm(value, wct_ref[:, t * C : t * C + C])
                z_ref[k, pl.ds(pl.multiple_of(8 + row, 8), piece), :] = acc
            return carry

        lax.fori_loop(0, 4, multiply, 0)

        def collect(q, carry):
            row = pl.multiple_of(q * 256, 128)
            grad = z_ref[1, pl.ds(pl.multiple_of(8 + row, 8), 256), :]
            grad += z_ref[0, pl.ds(row, 272), :][9:265] + z_ref[2, pl.ds(row, 272), :][7:263]
            pre = pre_ref[pl.ds(pl.multiple_of(first_g - first_tower + row, 16), 256), :C]
            g_ref[pl.ds(row, 256), :C] = (grad * gelu_slope(pre)).astype(BF)
            return carry

        lax.fori_loop(0, g_cells // 256, collect, 0)

    pl.run_scoped(class_back, pltpu.VMEM((3, g_cells + 16, C), F32))

    def tower_back(z_ref, gt_ref):
        def flip(q, carry):
            row = pl.multiple_of(q * 256, 128)
            part = g_ref[pl.ds(pl.multiple_of(edge - first_g + row, 16), 256), :].astype(F32)
            gt_ref[:, pl.ds(row, 256)] = part.T.astype(BF)
            db_ref[...] += jnp.sum(part, axis=0, keepdims=True)
            return carry

        lax.fori_loop(0, own // 256, flip, 0)
        weight_sums(pl.program_id(0), cols, edge, own, lambda: gt_ref[...], f_ref.at[0], mx_ref, dwt_ref)
        first_z = edge - 16
        piece = (own + 32) // 2

        def multiply(i, carry):
            row = pl.multiple_of(i * piece, 16)
            for k in range(3):
                acc = jnp.zeros((piece, C), F32)
                for r in range(3):
                    t = r * 3 + k
                    source = row + first_z - cols * (r - 1)
                    mask = mx_ref[t, pl.ds(pl.multiple_of(source, 16), piece), :]
                    value = g_ref[pl.ds(pl.multiple_of(source - first_g, 16), piece), :]
                    value = value * jnp.concatenate([mask] * (2 * C // LANE), axis=1)
                    acc += mm(value, wt_ref[t * C : t * C + C, :], NT)
                z_ref[k, pl.ds(row, piece), :] = acc
            return carry

        lax.fori_loop(0, 2, multiply, 0)

        def collect(q, carry):
            row = pl.multiple_of(q * 256, 128)
            base = pl.multiple_of(row + 8, 8)
            grad = z_ref[1, pl.ds(pl.multiple_of(16 + row, 8), 256), :]
            grad += z_ref[0, pl.ds(base, 272), :][9:265] + z_ref[2, pl.ds(base, 272), :][7:263]
            grad = grad.astype(BF).astype(F32)
            for n in range(2):
                fg_ref[0, n, pl.ds(row, 256), :] = grad[:, n * LANE : n * LANE + LANE]
            return carry

        lax.fori_loop(0, own // 256, collect, 0)

    pl.run_scoped(
        tower_back,
        pltpu.VMEM((3, own + 32, C), F32),
        pltpu.VMEM((2 * C, own), BF),
    )

    @pl.when(pl.program_id(0) == pl.num_programs(0) - 1)
    def _():
        def deliver(class_held, tower_held):
            def turn(t, carry):
                at = pl.multiple_of(t * C, C)
                tower_held[pl.ds(at, C), :] = dwt_ref[0:C, pl.ds(at, C)].astype(BF).T
                tower_held[pl.ds(pl.multiple_of(9 * C + at, C), C), :] = dwt_ref[C:, pl.ds(at, C)].astype(BF).T
                class_held[pl.ds(at, C), :] = dwc_ref[:, pl.ds(at, C)].astype(BF).T
                return carry

            lax.fori_loop(0, 9, turn, 0)
            copies = [
                pltpu.make_async_copy(class_held, class_ref, copy_sems.at[0]),
                pltpu.make_async_copy(tower_held, tower_ref, copy_sems.at[1]),
            ]
            for copy in copies:
                copy.start()
            for copy in copies:
                copy.wait()

        pl.run_scoped(deliver, pltpu.VMEM((9 * C, WIDE), BF), pltpu.VMEM((18 * C, C), BF))


def whole(shape):
    return pl.BlockSpec(shape, lambda *_: (0,) * len(shape))


def shape_of(shape, dtype=F32):
    return jax.ShapeDtypeStruct(shape, dtype)


VM = pl.BlockSpec(memory_space=pltpu.VMEM)
VMEM_LIMIT = 63 * 1024 * 1024


def stem_forward(patches, rim, head):
    canvases, rows, width = patches.shape
    cols = width // PATCH
    pairs = 8
    steps = cols // (2 * pairs)
    chunk = 2 * pairs * PATCH
    count = pairs * canvases * rows
    total = (rows + 2 * HALO) * cols
    return pl.pallas_call(
        functools.partial(stem_kernel, pairs, cols, rows),
        grid=(steps,),
        in_specs=[
            pl.BlockSpec((canvases, rows, chunk), lambda s: (0, 0, s)),
            pl.BlockSpec((2 * HALO * canvases, chunk), lambda s: (0, s)),
            whole(head.shape),
        ],
        out_specs=[
            pl.BlockSpec((count, 2 * C), lambda s: (s, 0)),
            pl.BlockSpec((count, 2 * C), lambda s: (s, 0)),
            whole((canvases, 3, total, C)),
            whole((C, C)),
        ],
        out_shape=[
            shape_of((steps * count, 2 * C)),
            shape_of((steps * count, 2 * C), BF),
            shape_of((canvases, 3, total, C), BF),
            shape_of((C, C), BF),
        ],
        scratch_shapes=[
            pltpu.VMEM((canvases, 2, total + 16, LANE), F32),
            pltpu.VMEM((2 * PATCH, 2 * C), BF),
            pltpu.VMEM((1, 2 * C), F32),
            pltpu.VMEM((1, C), F32),
        ],
        compiler_params=pltpu.CompilerParams(vmem_limit_bytes=VMEM_LIMIT),
        name="stem",
    )(patches, rim, head)


def stem_backward(patches, feature_grad, stem_out, stem_pre, lat_w):
    canvases, rows, width = patches.shape
    cols = width // PATCH
    pairs = 8
    steps = cols // (2 * pairs)
    chunk = 2 * pairs * PATCH
    count = pairs * canvases * rows
    return pl.pallas_call(
        functools.partial(stem_back_kernel, pairs, cols, rows),
        grid=(steps,),
        in_specs=[
            pl.BlockSpec((canvases, rows, chunk), lambda s: (0, 0, s)),
            whole((canvases, 2, rows * cols, LANE)),
            pl.BlockSpec((count, 2 * C), lambda s: (s, 0)),
            pl.BlockSpec((count, 2 * C), lambda s: (s, 0)),
            whole((C, C)),
        ],
        out_specs=whole((TOWER_ROW, C)),
        out_shape=shape_of((TOWER_ROW, C), BF),
        scratch_shapes=[
            pltpu.VMEM((PATCH, C), F32),
            pltpu.VMEM((1, C), F32),
            pltpu.VMEM((C, C), F32),
            pltpu.VMEM((1, C), F32),
            pltpu.VMEM((TOWER_ROW, C), F32),
        ],
        compiler_params=pltpu.CompilerParams(vmem_limit_bytes=VMEM_LIMIT),
        name="stem_back",
    )(patches, feature_grad, stem_out, stem_pre, lat_w)


BOX_CUTS = [(BOX_OUT * n // C, BOX_OUT * n % C) for n in range(64)]


def box_in_kernel(tail_ref, o_ref, t_ref, d_ref, u_ref):
    tail = tail_ref[...].astype(F32)
    count = tail.shape[0]
    lane = lax.broadcasted_iota(jnp.int32, (40, LANE), 1)
    for n in range(2):
        t_ref[n, 0:count, :] = tail[:, n * LANE : n * LANE + LANE]
        t_ref[n, count:, :] = jnp.zeros((t_ref.shape[1] - count, LANE), F32)
    lines = []
    for r in range(9):
        lines.append(jnp.concatenate([t_ref[n, pl.ds(2 + r, 40, stride=9), :] for n in range(2)], axis=1))
    for s, (r, at) in enumerate(BOX_CUTS):
        wide = jnp.concatenate([lines[r], lines[min(r + 1, 8)]], axis=1)
        d_ref[pl.ds(s, 40, stride=64), :] = jnp.where(lane < BOX_OUT, wide[:, at : at + LANE], 0.0)
    for t in range(9):
        turned = d_ref[t * C : t * C + C, :].T
        for n in range(2):
            u_ref[n] = turned[:, n * LANE : n * LANE + LANE]
        for m in range(4):
            here = t * BOX_ROWS + m * SLOT
            parts = [u_ref[n, pl.ds(m, SLOT, stride=4), :] for n in range(2)]
            o_ref[here : here + SLOT, :] = jnp.concatenate(parts, axis=1).astype(BF)


def box_out_kernel(w_ref, b_ref, o_ref, t_ref, d_ref, u_ref):
    u_ref[...] = jnp.zeros_like(u_ref)
    d_ref[9 * C :, :] = jnp.zeros((d_ref.shape[0] - 9 * C, LANE), F32)
    for t in range(9):
        for m in range(4):
            here = t * BOX_ROWS + m * SLOT
            for n in range(2):
                u_ref[n, pl.ds(m, SLOT, stride=4), :] = w_ref[here : here + SLOT, n * LANE : n * LANE + LANE]
        d_ref[t * C : t * C + C, :] = jnp.concatenate([u_ref[0], u_ref[1]], axis=1).T
    lines = [jnp.zeros((40, 2 * C), F32) for _ in range(9)]
    zero = jnp.zeros((40, 2 * C - LANE), F32)
    for s, (r, at) in enumerate(BOX_CUTS):
        wide = jnp.concatenate([d_ref[pl.ds(s, 40, stride=64), :], zero], axis=1)
        lines[r] = lines[r] + (pltpu.roll(wide, at, 1) if at else wide)
    t_ref[...] = jnp.zeros_like(t_ref)
    for r in range(9):
        line = lines[r][:, :C]
        if r:
            line = line + lines[r - 1][:, C:]
        for n in range(2):
            t_ref[n, pl.ds(2 + r, 40, stride=9), :] = line[:, n * LANE : n * LANE + LANE]
    for n in range(2):
        for k in range(2):
            at = k * C + n * LANE
            t_ref[n, k : k + 1, :] = b_ref[:, at : at + LANE]
    rows = o_ref.shape[0]
    o_ref[...] = jnp.concatenate([t_ref[0, 0:rows, :], t_ref[1, 0:rows, :]], axis=1).astype(BF)


def box_call(kernel, shape, kind, name, *args):
    return pl.pallas_call(
        kernel,
        in_specs=[VM] * len(args),
        out_specs=VM,
        out_shape=shape_of(shape, kind),
        scratch_shapes=[
            pltpu.VMEM((2, 368, LANE), F32),
            pltpu.VMEM((40 * 64, LANE), F32),
            pltpu.VMEM((2, LANE, LANE), F32),
        ],
        compiler_params=pltpu.CompilerParams(vmem_limit_bytes=VMEM_LIMIT),
        name=name,
    )(*args)


def heads_call(rows, cols, scal, feats, masks, labels, box_target, full, tb, head, wb):
    canvases = feats.shape[0]
    own = rows * cols
    total = own + 2 * HALO * cols
    spread = jnp.repeat(jnp.eye(SLOT, 9, dtype=BF), LANE, axis=1)

    def per(shape):
        return pl.BlockSpec((1,) + shape, lambda c: (c,) + (0,) * len(shape))

    return pl.pallas_call(
        functools.partial(head_kernel, cols, rows),
        grid=(canvases,),
        in_specs=[
            pl.BlockSpec(memory_space=pltpu.SMEM),
            pl.BlockSpec((1, 3, total, C), lambda c: (c, 0, 0, 0), pipeline_mode=pl.Buffered(1)),
            per((SLOT, total)),
            per((SLOT, total)),
            per((4, SLOT, total)),
            whole(spread.shape),
            pl.BlockSpec(memory_space=pl.ANY),
            whole(tb.shape),
            pl.BlockSpec(memory_space=pl.ANY),
            whole(wb.shape),
        ],
        out_specs=[
            pl.BlockSpec(memory_space=pl.ANY),
            pl.BlockSpec(memory_space=pl.ANY),
            whole((9 * BOX_ROWS, C)),
            whole((1, 2 * C)),
            per((2, own, LANE)),
            whole((16, 256)),
        ],
        out_shape=[
            shape_of((9 * C, WIDE), BF),
            shape_of((18 * C, C), BF),
            shape_of((9 * BOX_ROWS, C)),
            shape_of((1, 2 * C)),
            shape_of((canvases, 2, own, LANE)),
            shape_of((16, 256)),
        ],
        scratch_shapes=[
            pltpu.VMEM((9, total, LANE), BF),
            pltpu.VMEM((total - 2 * cols, 2 * C), F32),
            pltpu.VMEM((total, C), BF),
            pltpu.VMEM((WIDE, own + 512), BF),
            pltpu.VMEM((own + 512, WIDE), BF),
            pltpu.VMEM((own + 256, 2 * C), BF),
            pltpu.VMEM((9 * C, 2 * C), BF),
            pltpu.VMEM((WIDE, 9 * C), BF),
            pltpu.VMEM((WIDE, 9 * C), F32),
            pltpu.VMEM((2 * C, 9 * C), F32),
            pltpu.SemaphoreType.DMA((3,)),
        ],
        compiler_params=pltpu.CompilerParams(vmem_limit_bytes=VMEM_LIMIT),
        name="heads",
    )(scal, feats, masks, labels, box_target, spread, full, tb, head, wb)


def place():
    img = lax.axis_index("img")
    cls = lax.axis_index("cls")
    return img // 2, img % 2, cls // 2, cls % 2


def target(z, y, x, c):
    return (z * 2 + y, x * 2 + c)


def owner(z, y, x, c):
    return ((z * 2 + y) * 2 + x) * 2 + c


def enter(peers):
    barrier = pltpu.get_barrier_semaphore()
    for peer in peers:
        pl.semaphore_signal(barrier, inc=1, device_id=peer, device_id_type=MESH)
    pl.semaphore_wait(barrier, len(peers))


class Mail:
    def __init__(self, send_sems, recv_sems):
        self.send_sems, self.recv_sems, self.used, self.sent = send_sems, recv_sems, 0, []

    def push(self, source, landing, peer):
        copy = pltpu.make_async_remote_copy(
            src_ref=source,
            dst_ref=landing,
            send_sem=self.send_sems.at[self.used],
            recv_sem=self.recv_sems.at[self.used],
            device_id=peer,
            device_id_type=MESH,
        )
        self.used += 1
        copy.start()
        self.sent.append(copy)
        return copy

    def close(self):
        for copy in self.sent:
            copy.wait_send()


def window_row(index, shard):
    return pl.multiple_of((index * shard + LEAD * C) // (16 * C) * 16, 16)


def gather_kernel(shard, s_ref, k_ref, n_ref, full_ref, head_ref, count_ref, first_ref, last_ref, sh_ref, kx_ref, send_sems, recv_sems):
    z, y, x, c = place()
    block = k_ref.shape[0]
    win = s_ref.shape[0]
    others = [(k, j) for k in range(4) for j in range(2) if k or j]
    ring = [((z + k) % 4, (y + j) % 2) for k, j in others]
    enter([target(zz, yy, x, c) for zz, yy in ring] + [target(z, y, 1 - x, c), target(z, y, x, 1 - c)])
    mail = Mail(send_sems, recv_sems)
    me = owner(z, y, x, c)

    def rows(zz, yy):
        return pl.ds(pl.multiple_of((zz * 2 + yy) * block, 16), block)

    def lanes(cc):
        return pl.ds(pl.multiple_of(cc * HALF, LANE), HALF)

    got_kx = mail.push(k_ref, kx_ref, target(z, y, 1 - x, c))
    counts = [mail.push(n_ref, count_ref.at[z * 2 + y], target(zz, yy, x, c)) for zz, yy in ring]
    slot = sh_ref.at[me]
    got_z = [mail.push(s_ref, slot, target((z + k) % 4, y, x, c)) for k in range(1, 4)]
    got_y = [mail.push(s_ref, slot, target(z, 1 - y, x, c))]
    got_x = [mail.push(s_ref, slot, target(z, y, 1 - x, c))]
    got_c = [mail.push(s_ref, slot, target(z, y, x, 1 - c))]
    count_ref[z * 2 + y] = n_ref[...]
    sh_ref[me] = s_ref[...]

    got_kx.wait_recv()
    mine = head_ref.at[rows(z, y), lanes(c)]
    head_ref[rows(z, y), lanes(c)] = k_ref[...] + kx_ref[...]
    got_kz = [mail.push(mine, mine, target((z + k) % 4, y, x, c)) for k in range(1, 4)]
    got_ky = [mail.push(mine, mine, target(z, 1 - y, x, c))]
    got_kc = [mail.push(mine, mine, target(z, y, x, 1 - c))]

    for k in range(1, 4):
        got_z[k - 1].wait_recv()
        slot = sh_ref.at[owner((z + 4 - k) % 4, y, x, c)]
        got_y.append(mail.push(slot, slot, target(z, 1 - y, x, c)))
        got_x.append(mail.push(slot, slot, target(z, y, 1 - x, c)))
        got_c.append(mail.push(slot, slot, target(z, y, x, 1 - c)))
    for k in range(1, 4):
        got_kz[k - 1].wait_recv()
        part = head_ref.at[rows((z + 4 - k) % 4, y), lanes(c)]
        got_ky.append(mail.push(part, part, target(z, 1 - y, x, c)))
        got_kc.append(mail.push(part, part, target(z, y, x, 1 - c)))
    for k in range(4):
        got_y[k].wait_recv()
        slot = sh_ref.at[owner((z + 4 - k) % 4, 1 - y, x, c)]
        got_x.append(mail.push(slot, slot, target(z, y, 1 - x, c)))
        got_c.append(mail.push(slot, slot, target(z, y, x, 1 - c)))
    for k in range(4):
        got_ky[k].wait_recv()
        part = head_ref.at[rows((z + 4 - k) % 4, 1 - y), lanes(c)]
        got_kc.append(mail.push(part, part, target(z, y, x, 1 - c)))
    for k in range(8):
        got_x[k].wait_recv()
        slot = sh_ref.at[owner((z + 4 - k % 4) % 4, (y + k // 4) % 2, 1 - x, c)]
        got_c.append(mail.push(slot, slot, target(z, y, x, 1 - c)))
    for copy in got_c + got_kc + counts:
        copy.wait_recv()
    full_ref[...] = jnp.zeros_like(full_ref)

    def merge(d, carry):
        full_ref[pl.ds(window_row(d, shard), win), :] += sh_ref[d]
        return carry

    lax.fori_loop(0, 32, merge, 0)
    first_ref[...] = full_ref[0:TOWER_ROW, :]
    last_ref[...] = full_ref[TAIL_ROW:FULL_ROWS, :]
    mail.close()


def scatter_kernel(
    shard, head_ref, tower_ref, tail_ref, k_ref, n_ref, s_out, k_out, n_out,
    full_ref, sc_ref, sx_ref, sy_ref, sz_ref, kc_ref, ky_ref, kz_ref, kx_ref, mine_ref, peer_ref, far_ref, nz_ref, send_sems, recv_sems,
):
    z, y, x, c = place()
    block = kx_ref.shape[1]
    win = s_out.shape[0]
    enter([target((z + k) % 4, y, x, c) for k in range(1, 4)] + [target(z, 1 - y, x, c), target(z, y, 1 - x, c), target(z, y, x, 1 - c)])
    mail = Mail(send_sems, recv_sems)

    def rows(zz, yy):
        return pl.ds(pl.multiple_of((zz * 2 + yy) * block, 16), block)

    def lanes(cc):
        return pl.ds(pl.multiple_of(cc * HALF, LANE), HALF)

    def window(zz, yy, xx, cc):
        return pl.ds(window_row(owner(zz, yy, xx, cc), shard), win)

    mine_ref[0] = n_ref[...]
    sum_c = mail.push(mine_ref.at[0], peer_ref.at[0], target(z, y, x, 1 - c))
    spots = [(j, k) for j in (1, 0) for k in (1, 2, 3, 0)]
    got_kc = []
    for n, (j, k) in enumerate(spots):
        part = k_ref.at[rows((z + k) % 4, (y + j) % 2), lanes(1 - c)]
        got_kc.append(mail.push(part, kc_ref.at[n], target(z, y, x, 1 - c)))
    full_ref[0:TOWER_ROW, :] = head_ref[...]
    full_ref[TOWER_ROW:TAIL_ROW, :] = tower_ref[...]
    full_ref[TAIL_ROW:FULL_ROWS, :] = tail_ref[...]
    got_c = []
    for i in (1, 0):
        for n, (j, k) in enumerate(spots):
            part = full_ref.at[window((z + k) % 4, (y + j) % 2, (x + i) % 2, 1 - c), :]
            got_c.append(mail.push(part, sc_ref.at[(1 - i) * 8 + n], target(z, y, x, 1 - c)))

    sum_c.wait_recv()
    mine_ref[1] = mine_ref[0] + peer_ref[0]
    sum_x = mail.push(mine_ref.at[1], peer_ref.at[1], target(z, y, 1 - x, c))

    got_ky = []
    for n, (j, k) in enumerate(spots):
        got_kc[n].wait_recv()
        kc_ref[n] = kc_ref[n] + k_ref[rows((z + k) % 4, (y + j) % 2), lanes(c)]
        if j == 1:
            got_ky.append(mail.push(kc_ref.at[n], ky_ref.at[n], target(z, 1 - y, x, c)))
    got_x = []
    for n, (j, k) in enumerate(spots):
        got_c[n].wait_recv()
        sc_ref[n] = sc_ref[n] + full_ref[window((z + k) % 4, (y + j) % 2, 1 - x, c), :]
        got_x.append(mail.push(sc_ref.at[n], sx_ref.at[n], target(z, y, 1 - x, c)))

    sum_x.wait_recv()
    mine_ref[2] = mine_ref[1] + peer_ref[1]
    sum_y = mail.push(mine_ref.at[2], peer_ref.at[2], target(z, 1 - y, x, c))

    got_kz = []
    for n in range(4):
        got_ky[n].wait_recv()
        kc_ref[4 + n] = kc_ref[4 + n] + ky_ref[n]
        if n < 3:
            got_kz.append(mail.push(kc_ref.at[4 + n], kz_ref.at[n], target((z + n + 1) % 4, y, x, c)))
    got_y = []
    for n, (j, k) in enumerate(spots):
        got_c[8 + n].wait_recv()
        got_x[n].wait_recv()
        total = sc_ref[8 + n].astype(F32) + full_ref[window((z + k) % 4, (y + j) % 2, x, c), :].astype(F32)
        sc_ref[8 + n] = (total + sx_ref[n].astype(F32)).astype(BF)
        if j == 1:
            got_y.append(mail.push(sc_ref.at[8 + n], sy_ref.at[n], target(z, 1 - y, x, c)))

    sum_y.wait_recv()
    mine_ref[3] = mine_ref[2] + peer_ref[2]
    nz_ref[z] = mine_ref[3]
    sum_z = [mail.push(mine_ref.at[3], nz_ref.at[z], target((z + k) % 4, y, x, c)) for k in range(1, 4)]

    total = kc_ref[7].astype(F32)
    for n in range(3):
        got_kz[n].wait_recv()
        total += kz_ref[n].astype(F32)
    kx_ref[0] = total.astype(BF)
    got_kx = mail.push(kx_ref.at[0], kx_ref.at[1], target(z, y, 1 - x, c))
    got_z = []
    for n in range(4):
        got_y[n].wait_recv()
        sc_ref[12 + n] = sc_ref[12 + n] + sy_ref[n]
        if n < 3:
            got_z.append(mail.push(sc_ref.at[12 + n], sz_ref.at[n], target((z + n + 1) % 4, y, x, c)))
    total = sc_ref[15].astype(F32)
    for n in range(3):
        got_z[n].wait_recv()
        total += sz_ref[n].astype(F32)
    s_out[...] = total
    for copy in sum_z:
        copy.wait_recv()
    n_out[...] = (nz_ref[0] + nz_ref[1]) + (nz_ref[2] + nz_ref[3])
    got_kx.wait_recv()
    k_out[...] = kx_ref[0].astype(F32) + kx_ref[1].astype(F32)
    mail.close()


def fast_mesh(img_parts, cls_parts, class_rows):
    return img_parts == 8 and cls_parts == 4 and class_rows % 16 == 0


def flat_place(index, shard):
    return (index * shard + LEAD * C) % (16 * C)


def gather_all(shared_params, class_params, count):
    img, cls = lax.axis_index("img"), lax.axis_index("cls")
    img_parts, cls_parts = lax.axis_size("img"), lax.axis_size("cls")
    shard = shared_params.shape[0]
    block, part = class_params.shape
    if not fast_mesh(img_parts, cls_parts, block):
        flat = lax.all_gather(shared_params.astype(BF), ("img", "cls"), axis=0, tiled=True)
        full = jnp.pad(flat, (LEAD * C, FULL_ROWS * C - LEAD * C - flat.shape[0])).reshape(FULL_ROWS, C)
        head = lax.all_gather(class_params.astype(BF), ("img", "cls"), axis=0)
        head = head.reshape(img_parts, cls_parts, block, part).transpose(0, 2, 1, 3).reshape(-1, CLS_OUT)
        pieces = []
        for half in range(2):
            pieces += [head[:, 180 * half : 180 * half + 180], head[:, 360 + 180 * half : 540 + 180 * half]]
            pieces.append(jnp.zeros((head.shape[0], HALF - 360), BF))
        return full, full[:TOWER_ROW], full[TAIL_ROW:], jnp.concatenate(pieces, axis=1), lax.psum(count, "img")
    rows = -(-(shard + 16 * C) // (16 * C)) * 16
    window = lax.dynamic_update_slice(
        jnp.zeros((rows * C,), BF), shared_params.astype(BF), (flat_place(img * cls_parts + cls, shard),)
    ).reshape(rows, C)
    wide = jnp.pad(class_params.astype(BF), ((0, 0), (part, HALF - part)))
    wide = lax.dynamic_slice_in_dim(
        jnp.pad(wide, ((0, 0), (0, part))), jnp.where(cls // 2 == 0, part, 0), HALF, 1
    )
    number = jnp.broadcast_to(count, (8, LANE))
    full, head, counts, first, last = pl.pallas_call(
        functools.partial(gather_kernel, shard),
        in_specs=[VM, VM, VM],
        out_specs=[VM] * 5,
        out_shape=[
            shape_of((FULL_ROWS, C), BF),
            shape_of((img_parts * block, 2 * HALF), BF),
            shape_of((img_parts, 8, LANE)),
            shape_of((TOWER_ROW, C), BF),
            shape_of((FULL_ROWS - TAIL_ROW, C), BF),
        ],
        scratch_shapes=[
            pltpu.VMEM((img_parts * cls_parts, rows, C), BF),
            pltpu.VMEM((block, HALF), BF),
            pltpu.SemaphoreType.DMA((54,)),
            pltpu.SemaphoreType.DMA((54,)),
        ],
        compiler_params=pltpu.CompilerParams(collective_id=0, has_side_effects=True, vmem_limit_bytes=VMEM_LIMIT),
        name="gather",
    )(window, wide, number)
    return full, first, last, head, jnp.sum(counts[:, 0, 0])


def scatter_all(head, tower, tail, class_grad, sums, shard, block, part):
    img, cls = lax.axis_index("img"), lax.axis_index("cls")
    img_parts, cls_parts = lax.axis_size("img"), lax.axis_size("cls")
    if not fast_mesh(img_parts, cls_parts, block):
        flat = jnp.concatenate([head, tower, tail], axis=0).reshape(-1)
        flat = flat[LEAD * C : LEAD * C + shard * img_parts * cls_parts].astype(F32)
        shared = lax.psum_scatter(flat, ("img", "cls"), scatter_dimension=0, tiled=True)
        pieces = [class_grad[:, at : at + 180] for at in (0, HALF, 180, HALF + 180)]
        whole_grad = lax.psum_scatter(
            jnp.concatenate(pieces, axis=1).astype(F32), "img", scatter_dimension=0, tiled=True
        )
        return shared, lax.psum_scatter(whole_grad, "cls", scatter_dimension=1, tiled=True), lax.psum(sums, ("img", "cls"))
    rows = -(-(shard + 16 * C) // (16 * C)) * 16
    window, wide, sums = pl.pallas_call(
        functools.partial(scatter_kernel, shard),
        in_specs=[VM] * 5,
        out_specs=[VM] * 3,
        out_shape=[shape_of((rows, C)), shape_of((block, HALF)), shape_of(sums.shape)],
        scratch_shapes=[
            pltpu.VMEM((FULL_ROWS, C), BF),
            pltpu.VMEM((16, rows, C), BF),
            pltpu.VMEM((8, rows, C), BF),
            pltpu.VMEM((4, rows, C), BF),
            pltpu.VMEM((3, rows, C), BF),
            pltpu.VMEM((8, block, HALF), BF),
            pltpu.VMEM((4, block, HALF), BF),
            pltpu.VMEM((3, block, HALF), BF),
            pltpu.VMEM((2, block, HALF), BF),
            pltpu.VMEM((4,) + sums.shape, F32),
            pltpu.VMEM((3,) + sums.shape, F32),
            pltpu.VMEM((8, LANE), F32),
            pltpu.VMEM((4,) + sums.shape, F32),
            pltpu.SemaphoreType.DMA((53,)),
            pltpu.SemaphoreType.DMA((53,)),
        ],
        compiler_params=pltpu.CompilerParams(collective_id=1, has_side_effects=True, vmem_limit_bytes=VMEM_LIMIT),
        name="scatter",
    )(head, tower, tail, class_grad, sums)
    flat = lax.dynamic_slice_in_dim(window.reshape(-1), flat_place(img * cls_parts + cls, shard), shard)
    grad = lax.dynamic_slice_in_dim(wide, jnp.where(cls // 2 == 0, 0, part), part, 1)
    return flat, grad, sums


def column_plan():
    plan = []
    for half in range(2):
        for group in range(2):
            column, row, end = 360 * group + 180 * half, HALF * half + 180 * group, 360 * group + 180 * half + 180
            while column < end:
                count = min(end, (column // CLASSES + 1) * CLASSES) - column
                plan.append((row, count, column // CLASSES, column % CLASSES))
                column, row = column + count, row + count
        plan.append((HALF * half + 360, HALF - 360, -1, 0))
    return plan


def adamw_update(weight, first, second, grad):
    first_new = MOMENT_ONE * first + (1.0 - MOMENT_ONE) * grad
    second_new = MOMENT_TWO * second + (1.0 - MOMENT_TWO) * grad * grad
    first_hat = first_new / (1.0 - MOMENT_ONE**STEP)
    second_hat = second_new / (1.0 - MOMENT_TWO**STEP)
    weight_new = weight - RATE * (first_hat / (jnp.sqrt(second_hat) + EPSILON) + DECAY * weight)
    return (weight_new, first_new, second_new)


def valid_positives(boxes, match, full_rows, cols):
    place = jnp.arange(full_rows * cols, dtype=jnp.int32)
    row, col = place // cols, place % cols
    inside = jnp.zeros((boxes.shape[0], full_rows * cols), bool)
    for k in range(boxes.shape[1]):
        edge = boxes[:, k, :, None]
        inside |= (row >= edge[:, 0]) & (row < edge[:, 2]) & (col >= edge[:, 1]) & (col < edge[:, 3])
    return ((match >= 0) & inside[:, None]).astype(F32)


def cell_data(boxes, match, gt_labels, gt_deltas, first_row, rows, cols):
    full_rows = match.shape[2] // cols
    total = (rows + 2 * HALO) * cols
    place = jnp.arange(total, dtype=jnp.int32)[None]
    row = place // cols + (first_row - HALO)
    col = place % cols

    def crop(r, j):
        found = jnp.full((boxes.shape[0], total), -1, jnp.int32)
        for k in range(boxes.shape[1]):
            edge = boxes[:, k, :, None]
            inside = (r >= edge[:, 0]) & (r < edge[:, 2]) & (j >= edge[:, 1]) & (j < edge[:, 3])
            found = jnp.where(inside, k, found)
        return jnp.where((r >= 0) & (r < full_rows) & (j >= 0) & (j < cols), found, -1)

    centre = crop(row, col)
    valid = centre >= 0
    masks = jnp.stack([(crop(row + di, col + dj) == centre) & valid for di, dj in TAPS], axis=1)
    masks = jnp.pad(masks.astype(BF), ((0, 0), (0, SLOT - 9), (0, 0)))
    edge = HALO * cols
    near = jnp.pad(match, ((0, 0), (0, 0), (edge, edge)), constant_values=-2)
    near = lax.dynamic_slice_in_dim(near, first_row * cols, total, 2)
    near = jnp.where(valid[:, None], near, -2)
    near = jnp.pad(near, ((0, 0), (0, SLOT - 9), (0, 0)), constant_values=-2)
    labels = near
    targets = jnp.zeros((near.shape[0], 4) + near.shape[1:], F32)
    for g in range(gt_labels.shape[1]):
        labels = jnp.where(near == g, gt_labels[:, g, None, None], labels)
        targets = jnp.where((near == g)[:, None], gt_deltas[:, g, :, None, None], targets)
    return masks, labels.astype(F32), targets


def local(patches, boxes, match, gt_labels, gt_deltas, ema_old, shared_params, shared_m, shared_v, class_params, class_m, class_v):
    cls_rank = lax.axis_index("cls")
    cls_parts = lax.axis_size("cls")
    canvases, rows, width = patches.shape
    cols = width // PATCH
    masks, labels, targets = cell_data(boxes, match, gt_labels, gt_deltas, cls_rank * rows, rows, cols)
    full_rows = match.shape[2] // cols
    count = jnp.sum(valid_positives(boxes, match, full_rows, cols))
    full, first, last, head, positives = gather_all(shared_params, class_params, count)
    norm = jnp.maximum(positives, 1.0)
    ema_new = EMA_KEEP * ema_old + (1.0 - EMA_KEEP) * norm
    down = lax.ppermute(patches[:, rows - HALO :], "cls", [(i, i + 1) for i in range(cls_parts - 1)])
    up = lax.ppermute(patches[:, :HALO], "cls", [(i + 1, i) for i in range(cls_parts - 1)])
    rim = jnp.concatenate([down, up], axis=1).reshape(canvases * 2 * HALO, width)
    tb = last[0:2].reshape(1, 2 * C).astype(F32)
    wb = box_call(box_in_kernel, (9 * BOX_ROWS, C), BF, "box_in", last)
    stem_pre, stem_out, feats, lat_w = stem_forward(patches, rim, first)
    scal = jnp.stack([1.0 / ema_new, 1.0 / norm])
    class_grad, tower_grad, dwb, db, feature_grad, sums = heads_call(
        rows, cols, scal, feats, masks, labels, targets, full, tb, head, wb
    )
    first_grad = stem_backward(patches, feature_grad, stem_out, stem_pre, lat_w)
    last_grad = box_call(box_out_kernel, last.shape, BF, "box_out", dwb, db)
    shared_grad, class_grad, sums = scatter_all(
        first_grad, tower_grad, last_grad, class_grad, sums, shared_params.shape[0], *class_params.shape
    )
    loss = jnp.sum(sums[0:8]) / ema_new + jnp.sum(sums[8:16]) / norm
    return (
        loss,
        ema_new,
        *adamw_update(shared_params, shared_m, shared_v, shared_grad),
        *adamw_update(class_params, class_m, class_v, class_grad),
    )


def solution(mesh):
    spread = P(("img", "cls"))
    block = P("img", "cls")
    return jax.shard_map(
        local,
        mesh=mesh,
        in_specs=(
            P("img", "cls", None),
            P("img", None, None),
            P("img", None, None),
            P("img", None),
            P("img", None, None),
            P(),
            spread,
            spread,
            spread,
            block,
            block,
            block,
        ),
        out_specs=(P(), P(), spread, spread, spread, block, block, block),
        check_vma=False,
    )
```

```python
import functools

import jax
import jax.numpy as jnp
from jax import lax
from jax.experimental import pallas as pl
from jax.experimental.pallas import tpu as pltpu
from jax.sharding import PartitionSpec as P

C = 256
CLASSES = 80
ANCH = 9
PATCH = 192
BOX_OUT = 36
CLS_OUT = ANCH * CLASSES
STEP = 5
GT = 16
HALO = 4
SLOT = 16
BOX_ROWS = 4 * SLOT
LANE = 128
WIDE = 768
GROUP = 16

PRIOR = -4.59511985013459
ALPHA = 0.25
HUBER = 1.0 / 9.0
EMA_KEEP = 0.9
RATE = 0.01
MOMENT_ONE = 0.5
MOMENT_TWO = 0.5
DECAY = 0.05
EPSILON = 1e-08

LENGTHS = [PATCH * C, C, C * C, C, 18 * C * C, 2 * C, 9 * C * BOX_OUT]
TOWER_AT = sum(LENGTHS[:4]) // C
LEAD = -TOWER_AT % 16
TOWER_ROW = TOWER_AT + LEAD
TAIL_ROW = TOWER_ROW + 18 * C
FULL_ROWS = -(-(LEAD + sum(LENGTHS) // C) // 16) * 16
HALF = 384
MESH = pl.DeviceIdType.MESH

BF = jnp.bfloat16
F32 = jnp.float32
TAPS = [(di, dj) for di in (-1, 0, 1) for dj in (-1, 0, 1)]
NN = (((1,), (0,)), ((), ()))
NT = (((1,), (1,)), ((), ()))
TN = (((0,), (0,)), ((), ()))
K0 = 0.7978845608028654
K1 = 0.044715


def mm(a, b, dims=NN):
    return lax.dot_general(a, b, dims, preferred_element_type=F32)


def gelu(x):
    return 0.5 * x * (1.0 + jnp.tanh(K0 * (x + K1 * x * x * x)))


def gelu_slope(x):
    square = x * x
    th = jnp.tanh(K0 * (x + K1 * x * square))
    return 0.5 * (1.0 + th) + (0.5 * K0) * x * (1.0 - th * th) * (1.0 + 3.0 * K1 * square)


def columns_of(x, pairs, width):
    return [x[:, width * k : width * (k + 1)] for k in range(pairs)]


def stem_kernel(pairs, cols, rows, x_ref, h_ref, head_ref, pre_ref, so_ref, f_ref, lw_ref, t_ref, w_ref, b_ref, lb_ref):
    step = pl.program_id(0)
    canvases = x_ref.shape[0]
    own_rows = canvases * rows
    total = (rows + 2 * HALO) * cols

    @pl.when(step == 0)
    def _():
        head = head_ref[...].astype(F32)
        w_ref[...] = jnp.zeros_like(w_ref)
        stem_w = head[LEAD : LEAD + PATCH].astype(BF)
        w_ref[:PATCH, :C] = stem_w
        w_ref[PATCH:, C:] = stem_w
        bias = head[LEAD + PATCH : LEAD + PATCH + 1]
        b_ref[...] = jnp.concatenate([bias, bias], axis=1)
        lw_ref[...] = head[LEAD + PATCH + 1 : TOWER_ROW - 1].astype(BF)
        lb_ref[...] = head[TOWER_ROW - 1 : TOWER_ROW]
        for c in range(canvases):
            for n in range(2):
                t_ref[c, n, 0:8, :] = jnp.zeros((8, LANE), F32)
                t_ref[c, n, 8 + total : 16 + total, :] = jnp.zeros((8, LANE), F32)

    x = x_ref[...].reshape(own_rows, x_ref.shape[2])
    own = columns_of(x, pairs, 2 * PATCH)
    half = pl.num_programs(0) // 2
    lanes = pl.ds(pl.multiple_of(step % half * x.shape[1], LANE), x.shape[1])
    many_rows = h_ref.shape[1] // 2
    near = [h_ref[n, :, lanes].astype(F32) for n in range(2)]
    near = [jnp.where(step < half, one[:many_rows], one[many_rows:]) for one in near]
    rim = columns_of(jnp.concatenate(near, axis=0).astype(BF), pairs, 2 * PATCH)
    pre = mm(jnp.concatenate(own + rim, axis=0), w_ref[...]) + b_ref[...]
    count = pairs * own_rows
    pre_ref[...] = pre[:count]
    out = gelu(pre).astype(BF)
    so_ref[...] = out[:count]
    for half in range(2):
        feat = mm(out[:, half * C : half * C + C], lw_ref[...]) + lb_ref[...]
        for k in range(pairs):
            j = step * 2 * pairs + 2 * k + half
            for c in range(canvases):
                at = k * own_rows + c * rows
                up_at = count + k * 2 * HALO * canvases + c * HALO
                down_at = up_at + HALO * canvases
                for n in range(2):
                    side = slice(n * LANE, n * LANE + LANE)
                    place = pl.ds(8 + HALO * cols + j, rows, stride=cols)
                    t_ref[c, n, place, :] = feat[at : at + rows, side]
                    place = pl.ds(8 + j, HALO, stride=cols)
                    t_ref[c, n, place, :] = feat[up_at : up_at + HALO, side]
                    place = pl.ds(8 + (HALO + rows) * cols + j, HALO, stride=cols)
                    t_ref[c, n, place, :] = feat[down_at : down_at + HALO, side]

    @pl.when(step == pl.num_programs(0) - 1)
    def _():
        piece = 4 * cols

        def move(i, carry):
            base = pl.multiple_of(i * piece, 16)
            for c in range(canvases):
                for n in range(2):
                    value = t_ref[c, n, pl.ds(base, piece + 16), :]
                    for k in range(3):
                        moved = value[7 + k : 7 + k + piece].astype(BF)
                        f_ref[c, k, pl.ds(base, piece), n * LANE : n * LANE + LANE] = moved
            return carry

        lax.fori_loop(0, total // piece, move, 0)


def stem_back_kernel(pairs, cols, rows, x_ref, fg_ref, so_ref, pre_ref, lw_ref, head_ref, sw_out, sb_out, lw_out, lb_out, h_ref):
    step = pl.program_id(0)
    canvases = x_ref.shape[0]

    @pl.when(step == 0)
    def _():
        sw_out[...] = jnp.zeros_like(sw_out)
        sb_out[...] = jnp.zeros_like(sb_out)
        lw_out[...] = jnp.zeros_like(lw_out)
        lb_out[...] = jnp.zeros_like(lb_out)

    x = x_ref[...].reshape(canvases * rows, x_ref.shape[2])
    own = jnp.concatenate(columns_of(x, pairs, 2 * PATCH), axis=0)
    low = []
    for half in range(2):
        parts = []
        for k in range(pairs):
            j = step * 2 * pairs + 2 * k + half
            for c in range(canvases):
                place = pl.ds(j, rows, stride=cols)
                parts.append(jnp.concatenate([fg_ref[c, n, place, :] for n in range(2)], axis=1))
        grad32 = jnp.concatenate(parts, axis=0)
        grad = grad32.astype(BF)
        cut = slice(half * C, half * C + C)
        lw_out[...] += mm(so_ref[:, cut], grad, TN)
        lb_out[...] += jnp.sum(grad32, axis=0, keepdims=True)
        back = mm(grad, lw_ref[...], NT) * gelu_slope(pre_ref[:, cut])
        back = back.astype(BF)
        sb_out[...] += jnp.sum(back.astype(F32), axis=0, keepdims=True)
        low.append(back)
    both = mm(own, jnp.concatenate(low, axis=1), TN)
    sw_out[...] += both[:PATCH, :C] + both[PATCH:, C:]

    @pl.when(step == pl.num_programs(0) - 1)
    def _():
        at = LEAD + PATCH
        h_ref[0:LEAD, :] = jnp.zeros((LEAD, C), F32)
        h_ref[LEAD:at, :] = sw_out[...]
        h_ref[at : at + 1, :] = sb_out[...]
        h_ref[at + 1 : TOWER_ROW - 1, :] = lw_out[...]
        h_ref[TOWER_ROW - 1 :, :] = lb_out[...]
        head_ref[...] = h_ref[...].astype(BF)


def aligned(value, multiple):
    return value if isinstance(value, int) else pl.multiple_of(value, multiple)


def many(mask, count):
    return jnp.concatenate([mask] * count, axis=1)


def weight_sums(canvas, cols, edge, own, grad, source, mx_ref, sum_ref):
    def go(x_ref):
        def triple(n, carry):
            at = pl.multiple_of(edge + cols * (n - 1), 16)
            for k in range(3):
                mask = mx_ref[n * 3 + k, edge : edge + own, :]
                x_ref[:, k * C : k * C + C] = source[k, pl.ds(at, own), :] * many(mask, 2)
            side = pl.ds(pl.multiple_of(n * 3 * C, C), 3 * C)
            sum_ref[:, side] = jnp.where(canvas > 0, sum_ref[:, side], 0.0) + mm(grad(), x_ref[...])
            return carry

        lax.fori_loop(0, 3, triple, 0)

    pl.run_scoped(go, pltpu.VMEM((own, 3 * C), BF))


def head_kernel(
    cols, rows, scal_ref, f_ref, mk_ref, lab_ref, btt_ref, e_ref, full_ref, tb_ref, head_ref, wb_ref,
    class_ref, tower_ref, dwb_ref, db_ref, fg_ref, sums_ref,
    mx_ref, pre_ref, bt_ref, lgt_ref, lgs_ref, g_ref, wt_ref, wct_ref, dwc_ref, dwt_ref, copy_sems,
):
    own = rows * cols
    edge = HALO * cols
    total = own + 2 * edge
    shift = [cols * di + dj for di, dj in TAPS]

    @pl.when(pl.program_id(0) == 0)
    def _():
        dwb_ref[...] = jnp.zeros_like(dwb_ref)
        db_ref[...] = jnp.zeros_like(db_ref)
        sums_ref[...] = jnp.zeros_like(sums_ref)
        def fetch(held_ref):
            copies = [pltpu.make_async_copy(head_ref, held_ref, copy_sems.at[2])]
            for n in range(2):
                rows_of = full_ref.at[TOWER_ROW + n * 9 * C : TOWER_ROW + (n + 1) * 9 * C, :]
                copies.append(pltpu.make_async_copy(rows_of, wt_ref.at[:, n * C : n * C + C], copy_sems.at[n]))
            for copy in copies:
                copy.start()
            copies[0].wait()

            def turn(t, carry):
                at = pl.multiple_of(t * C, C)
                wct_ref[:, pl.ds(at, C)] = held_ref[pl.ds(at, C), :].T
                return carry

            lax.fori_loop(0, 9, turn, 0)
            for copy in copies[1:]:
                copy.wait()

        pl.run_scoped(fetch, pltpu.VMEM((9 * C, WIDE), BF))

    def spread(i, carry):
        at = pl.multiple_of(i * 384, 128)
        wide = mm(mk_ref[0, :, pl.ds(at, 384)], e_ref[...], TN).astype(BF)
        for t in range(9):
            mx_ref[t, pl.ds(at, 384), :] = wide[:, t * LANE : (t + 1) * LANE]
        return carry

    lax.fori_loop(0, total // 384, spread, 0)

    def twice(mask):
        return jnp.concatenate([mask, mask], axis=1)

    def build(source, at, count, x_ref):
        for t, (di, dj) in enumerate(TAPS):
            value = source[dj + 1, pl.ds(pl.multiple_of(at + cols * di, 16), count), :]
            x_ref[:, t * C : (t + 1) * C] = value * twice(mx_ref[t, pl.ds(at, count), :])

    first_tower = cols
    tower_rows = total - 2 * cols
    first_logit = edge - 256
    logit_cells = own + 512
    first_g = edge - 128
    g_cells = own + 256

    def heads(ct32_ref, ct_ref):
        zero = jnp.zeros((cols + 8, C), F32)
        ct32_ref[0 : cols + 8, :] = zero
        ct32_ref[8 + total - cols : 16 + total, :] = zero
        zero = jnp.zeros((cols, C), BF)
        bt_ref[0:cols, :] = zero
        bt_ref[total - cols : total, :] = zero
        piece = tower_rows // 3

        def towers(x_ref):
            def tower(i, carry):
                row = pl.multiple_of(i * piece, 16)
                at = pl.multiple_of(first_tower + i * piece, 16)
                build(f_ref.at[0], at, piece, x_ref)
                pre = mm(x_ref[...], wt_ref[...]) + tb_ref[...]
                pre_ref[pl.ds(row, piece), :] = pre
                out = gelu(pre)
                ct32_ref[pl.ds(pl.multiple_of(8 + at, 8), piece), :] = out[:, :C]
                bt_ref[pl.ds(at, piece), :] = out[:, C:].astype(BF)
                return carry

            lax.fori_loop(0, 3, tower, 0)

        pl.run_scoped(towers, pltpu.VMEM((piece, 9 * C), BF))

        def move(i, carry):
            base = pl.multiple_of(i * edge, 16)
            value = ct32_ref[pl.ds(base, edge + 16), :]
            for k in range(3):
                ct_ref[k, pl.ds(base, edge), :] = value[7 + k : 7 + k + edge].astype(BF)
            return carry

        lax.fori_loop(0, total // edge, move, 0)
        def logits(xa_ref, la_ref):
            inv_ema = scal_ref[0]
            number = lax.broadcasted_iota(jnp.int32, (GROUP, 256), 0).astype(F32)
            lane = lax.broadcasted_iota(jnp.int32, (8, 256), 1)
            plan = column_plan()

            def ready(q, x_ref):
                build(ct_ref, pl.multiple_of(first_logit + q * 256, 128), 256, x_ref)

            def work(q, x_ref, l_ref):
                l_ref[...] = mm(wct_ref[...], x_ref[...], NT)

            def focal(q, l_ref):
                row = pl.multiple_of(q * 256, 128)
                at = pl.multiple_of(first_logit + row, 128)
                spot = lane + at
                mine = (spot >= edge) & (spot < edge + own)
                lines = [lab_ref[0, a : a + 1, pl.ds(at, 256)] for a in range(ANCH)]
                rest = [jnp.where(line > -1.5, 1.0 - ALPHA, 0.0) for line in lines]
                pulls = [line * inv_ema for line in rest]
                total_focal = jnp.zeros((8, 256), F32)
                for first in range(0, WIDE, GROUP):
                    value = l_ref[first : first + GROUP, :] + PRIOR
                    key = None
                    for begin, count, anchor, klass in plan:
                        if begin >= first + GROUP or begin + count <= first:
                            continue
                        if anchor < 0:
                            parts = [jnp.full((GROUP, 256), n, F32) for n in (-2.0, 0.0, 0.0)]
                        else:
                            parts = [lines[anchor] - float(klass - (begin - first)), rest[anchor], pulls[anchor]]
                            parts = [jnp.broadcast_to(part, (GROUP, 256)) for part in parts]
                        if key is None:
                            key, other, pull_other = parts
                        else:
                            later = number >= float(begin - first)
                            key = jnp.where(later, parts[0], key)
                            other = jnp.where(later, parts[1], other)
                            pull_other = jnp.where(later, parts[2], pull_other)
                    hit = key == number
                    side = jnp.where(hit, -value, value)
                    small = jnp.exp(-jnp.abs(side))
                    whole_one = 1.0 + small
                    ratio = pltpu.reciprocal(whole_one, approx=True)
                    ratio = ratio * (2.0 - whole_one * ratio)
                    part = small * ratio
                    up = side >= 0.0
                    prob = jnp.where(up, ratio, part)
                    miss = jnp.where(up, part, ratio)
                    tiny = small * (1.0 - 0.5 * small)
                    cross = jnp.maximum(side, 0.0) + jnp.where(small < 0.001, tiny, jnp.log(whole_one))
                    square = prob * prob
                    value = square * cross * jnp.where(hit, ALPHA, other)
                    pull = square * (2.0 * miss * cross + prob) * jnp.where(hit, -ALPHA * inv_ema, pull_other)
                    l_ref[first : first + GROUP, :] = pull
                    lgt_ref[first : first + GROUP, pl.ds(row, 256)] = pull.astype(BF)
                    total_focal += jnp.sum(value.reshape(GROUP // 8, 8, 256), axis=0)
                sums_ref[0:8, :] += jnp.where(mine, total_focal, 0.0)
                lgs_ref[pl.ds(row, 256), :] = l_ref[...].T.astype(BF)

            def logits_of(q, carry):
                ready(q, xa_ref)
                work(q, xa_ref, la_ref)
                focal(q, la_ref)
                return carry

            lax.fori_loop(0, logit_cells // 256, logits_of, 0)

        pl.run_scoped(logits, pltpu.VMEM((256, 9 * C), BF), pltpu.VMEM((WIDE, 256), F32))
        weight_sums(pl.program_id(0), cols, edge, own, lambda: lgt_ref[:, 256 : 256 + own], ct_ref, mx_ref, dwc_ref)

    pl.run_scoped(heads, pltpu.VMEM((total + 16, C), F32), pltpu.VMEM((3, total, C), BF))

    def box_forward(gg_ref, y_ref):
        inv_norm = scal_ref[1]

        def outer(i, carry):
            at = pl.multiple_of(i * 768, 128)
            y_ref[:, pl.ds(at, 768)] = mm(wb_ref[...], bt_ref[pl.ds(at, 768), :], NT)
            return carry

        lax.fori_loop(0, total // 768, outer, 0)
        lane = lax.broadcasted_iota(jnp.int32, (SLOT, total), 1)
        mine = (lane >= edge) & (lane < edge + own)

        def guess(m, carry):
            acc = jnp.zeros((SLOT, total), F32)
            for t in range(9):
                value = y_ref[pl.ds(pl.multiple_of(t * BOX_ROWS + m * SLOT, 8), SLOT), :]
                moved = pltpu.roll(value, (-shift[t]) % total, 1)
                acc += moved * mk_ref[0, t : t + 1, :].astype(F32)
            differ = acc - btt_ref[0, m]
            positive = lab_ref[0] >= 0.0
            size = jnp.abs(differ)
            loss = jnp.where(size < HUBER, 0.5 * differ * differ / HUBER, size - 0.5 * HUBER)
            loss = jnp.where(positive & mine, loss, 0.0)
            part = loss[:, 0:256]
            for k in range(1, total // 256):
                part += loss[:, k * 256 : (k + 1) * 256]
            sums_ref[8:16, :] += part[0:8] + part[8:16]
            pull = jnp.minimum(jnp.maximum(differ / HUBER, -1.0), 1.0) * inv_norm
            pull = jnp.where(positive, pull, 0.0)
            gg_ref[pl.ds(pl.multiple_of(m * SLOT, 8), SLOT), :] = pull
            return carry

        lax.fori_loop(0, 4, guess, 0)

    def box_back(gg_ref, xg_ref):
        for t in range(9):
            moved = pltpu.roll(gg_ref[...], shift[t] % total, 1)
            xg_ref[t * BOX_ROWS : (t + 1) * BOX_ROWS, :] = (moved * mk_ref[0, 8 - t : 9 - t, :].astype(F32)).astype(BF)
        dwb_ref[...] += mm(xg_ref[:, edge : edge + own], bt_ref[edge : edge + own, :])

        def into(q, carry):
            row = pl.multiple_of(q * 256, 128)
            grad = mm(xg_ref[:, pl.ds(pl.multiple_of(first_g + row, 128), 256)], wb_ref[...], TN)
            pre = pre_ref[pl.ds(pl.multiple_of(first_g - first_tower + row, 16), 256), C:]
            g_ref[pl.ds(row, 256), C:] = (grad * gelu_slope(pre)).astype(BF)
            return carry

        lax.fori_loop(0, g_cells // 256, into, 0)

    def boxes(gg_ref):
        pl.run_scoped(functools.partial(box_forward, gg_ref), pltpu.VMEM((9 * BOX_ROWS, total), F32))
        pl.run_scoped(functools.partial(box_back, gg_ref), pltpu.VMEM((9 * BOX_ROWS, total), BF))

    pl.run_scoped(boxes, pltpu.VMEM((BOX_ROWS, total), F32))

    def class_back(z_ref):
        z_ref[:, 0:8, :] = jnp.zeros((3, 8, C), F32)
        z_ref[:, 8 + g_cells : 16 + g_cells, :] = jnp.zeros((3, 8, C), F32)
        piece = g_cells // 4

        def multiply(i, carry):
            row = pl.multiple_of(i * piece, 16)
            for k in range(3):
                acc = jnp.zeros((piece, C), F32)
                for r in range(3):
                    t = r * 3 + k
                    source = row + first_g - cols * (r - 1)
                    mask = mx_ref[t, pl.ds(pl.multiple_of(source, 16), piece), :]
                    value = lgs_ref[pl.ds(pl.multiple_of(source - first_logit, 16), piece), :]
                    value = value * jnp.concatenate([mask] * (WIDE // LANE), axis=1)
                    acc += mm(value, wct_ref[:, t * C : t * C + C])
                z_ref[k, pl.ds(pl.multiple_of(8 + row, 8), piece), :] = acc
            return carry

        lax.fori_loop(0, 4, multiply, 0)

        def collect(q, carry):
            row = pl.multiple_of(q * 256, 128)
            grad = z_ref[1, pl.ds(pl.multiple_of(8 + row, 8), 256), :]
            grad += z_ref[0, pl.ds(row, 272), :][9:265] + z_ref[2, pl.ds(row, 272), :][7:263]
            pre = pre_ref[pl.ds(pl.multiple_of(first_g - first_tower + row, 16), 256), :C]
            g_ref[pl.ds(row, 256), :C] = (grad * gelu_slope(pre)).astype(BF)
            return carry

        lax.fori_loop(0, g_cells // 256, collect, 0)

    pl.run_scoped(class_back, pltpu.VMEM((3, g_cells + 16, C), F32))

    def tower_back(z_ref, gt_ref):
        def flip(q, carry):
            row = pl.multiple_of(q * 256, 128)
            part = g_ref[pl.ds(pl.multiple_of(edge - first_g + row, 16), 256), :].astype(F32)
            gt_ref[:, pl.ds(row, 256)] = part.T.astype(BF)
            db_ref[...] += jnp.sum(part, axis=0, keepdims=True)
            return carry

        lax.fori_loop(0, own // 256, flip, 0)
        weight_sums(pl.program_id(0), cols, edge, own, lambda: gt_ref[...], f_ref.at[0], mx_ref, dwt_ref)
        first_z = edge - 16
        piece = (own + 32) // 2

        def multiply(i, carry):
            row = pl.multiple_of(i * piece, 16)
            for k in range(3):
                acc = jnp.zeros((piece, C), F32)
                for r in range(3):
                    t = r * 3 + k
                    source = row + first_z - cols * (r - 1)
                    mask = mx_ref[t, pl.ds(pl.multiple_of(source, 16), piece), :]
                    value = g_ref[pl.ds(pl.multiple_of(source - first_g, 16), piece), :]
                    value = value * jnp.concatenate([mask] * (2 * C // LANE), axis=1)
                    acc += mm(value, wt_ref[t * C : t * C + C, :], NT)
                z_ref[k, pl.ds(row, piece), :] = acc
            return carry

        lax.fori_loop(0, 2, multiply, 0)

        def collect(q, carry):
            row = pl.multiple_of(q * 256, 128)
            base = pl.multiple_of(row + 8, 8)
            grad = z_ref[1, pl.ds(pl.multiple_of(16 + row, 8), 256), :]
            grad += z_ref[0, pl.ds(base, 272), :][9:265] + z_ref[2, pl.ds(base, 272), :][7:263]
            grad = grad.astype(BF).astype(F32)
            for n in range(2):
                fg_ref[0, n, pl.ds(row, 256), :] = grad[:, n * LANE : n * LANE + LANE]
            return carry

        lax.fori_loop(0, own // 256, collect, 0)

    pl.run_scoped(
        tower_back,
        pltpu.VMEM((3, own + 32, C), F32),
        pltpu.VMEM((2 * C, own), BF),
    )

    @pl.when(pl.program_id(0) == pl.num_programs(0) - 1)
    def _():
        def deliver(class_held, tower_held):
            def turn(t, carry):
                at = pl.multiple_of(t * C, C)
                tower_held[pl.ds(at, C), :] = dwt_ref[0:C, pl.ds(at, C)].astype(BF).T
                tower_held[pl.ds(pl.multiple_of(9 * C + at, C), C), :] = dwt_ref[C:, pl.ds(at, C)].astype(BF).T
                class_held[pl.ds(at, C), :] = dwc_ref[:, pl.ds(at, C)].astype(BF).T
                return carry

            lax.fori_loop(0, 9, turn, 0)
            copies = [
                pltpu.make_async_copy(class_held, class_ref, copy_sems.at[0]),
                pltpu.make_async_copy(tower_held, tower_ref, copy_sems.at[1]),
            ]
            for copy in copies:
                copy.start()
            for copy in copies:
                copy.wait()

        pl.run_scoped(deliver, pltpu.VMEM((9 * C, WIDE), BF), pltpu.VMEM((18 * C, C), BF))


def whole(shape):
    return pl.BlockSpec(shape, lambda *_: (0,) * len(shape))


def shape_of(shape, dtype=F32):
    return jax.ShapeDtypeStruct(shape, dtype)


VM = pl.BlockSpec(memory_space=pltpu.VMEM)
VMEM_LIMIT = 63 * 1024 * 1024


def stem_forward(patches, rim, head):
    canvases, rows, width = patches.shape
    cols = width // PATCH
    pairs = 8
    steps = cols // (2 * pairs)
    chunk = 2 * pairs * PATCH
    count = pairs * canvases * rows
    total = (rows + 2 * HALO) * cols
    return pl.pallas_call(
        functools.partial(stem_kernel, pairs, cols, rows),
        grid=(steps,),
        in_specs=[
            pl.BlockSpec((canvases, rows, chunk), lambda s: (0, 0, s)),
            whole(rim.shape),
            whole(head.shape),
        ],
        out_specs=[
            pl.BlockSpec((count, 2 * C), lambda s: (s, 0)),
            pl.BlockSpec((count, 2 * C), lambda s: (s, 0)),
            whole((canvases, 3, total, C)),
            whole((C, C)),
        ],
        out_shape=[
            shape_of((steps * count, 2 * C)),
            shape_of((steps * count, 2 * C), BF),
            shape_of((canvases, 3, total, C), BF),
            shape_of((C, C), BF),
        ],
        scratch_shapes=[
            pltpu.VMEM((canvases, 2, total + 16, LANE), F32),
            pltpu.VMEM((2 * PATCH, 2 * C), BF),
            pltpu.VMEM((1, 2 * C), F32),
            pltpu.VMEM((1, C), F32),
        ],
        compiler_params=pltpu.CompilerParams(vmem_limit_bytes=VMEM_LIMIT),
        name="stem",
    )(patches, rim, head)


def stem_backward(patches, feature_grad, stem_out, stem_pre, lat_w):
    canvases, rows, width = patches.shape
    cols = width // PATCH
    pairs = 8
    steps = cols // (2 * pairs)
    chunk = 2 * pairs * PATCH
    count = pairs * canvases * rows
    return pl.pallas_call(
        functools.partial(stem_back_kernel, pairs, cols, rows),
        grid=(steps,),
        in_specs=[
            pl.BlockSpec((canvases, rows, chunk), lambda s: (0, 0, s)),
            whole((canvases, 2, rows * cols, LANE)),
            pl.BlockSpec((count, 2 * C), lambda s: (s, 0)),
            pl.BlockSpec((count, 2 * C), lambda s: (s, 0)),
            whole((C, C)),
        ],
        out_specs=whole((TOWER_ROW, C)),
        out_shape=shape_of((TOWER_ROW, C), BF),
        scratch_shapes=[
            pltpu.VMEM((PATCH, C), F32),
            pltpu.VMEM((1, C), F32),
            pltpu.VMEM((C, C), F32),
            pltpu.VMEM((1, C), F32),
            pltpu.VMEM((TOWER_ROW, C), F32),
        ],
        compiler_params=pltpu.CompilerParams(vmem_limit_bytes=VMEM_LIMIT),
        name="stem_back",
    )(patches, feature_grad, stem_out, stem_pre, lat_w)


BOX_CUTS = [(BOX_OUT * n // C, BOX_OUT * n % C) for n in range(64)]


def box_in_kernel(tail_ref, o_ref, t_ref, d_ref, u_ref):
    tail = tail_ref[...].astype(F32)
    count = tail.shape[0]
    lane = lax.broadcasted_iota(jnp.int32, (40, LANE), 1)
    for n in range(2):
        t_ref[n, 0:count, :] = tail[:, n * LANE : n * LANE + LANE]
        t_ref[n, count:, :] = jnp.zeros((t_ref.shape[1] - count, LANE), F32)
    lines = []
    for r in range(9):
        lines.append(jnp.concatenate([t_ref[n, pl.ds(2 + r, 40, stride=9), :] for n in range(2)], axis=1))
    for s, (r, at) in enumerate(BOX_CUTS):
        wide = jnp.concatenate([lines[r], lines[min(r + 1, 8)]], axis=1)
        d_ref[pl.ds(s, 40, stride=64), :] = jnp.where(lane < BOX_OUT, wide[:, at : at + LANE], 0.0)
    for t in range(9):
        turned = d_ref[t * C : t * C + C, :].T
        for n in range(2):
            u_ref[n] = turned[:, n * LANE : n * LANE + LANE]
        for m in range(4):
            here = t * BOX_ROWS + m * SLOT
            parts = [u_ref[n, pl.ds(m, SLOT, stride=4), :] for n in range(2)]
            o_ref[here : here + SLOT, :] = jnp.concatenate(parts, axis=1).astype(BF)


def box_out_kernel(w_ref, b_ref, o_ref, t_ref, d_ref, u_ref):
    u_ref[...] = jnp.zeros_like(u_ref)
    d_ref[9 * C :, :] = jnp.zeros((d_ref.shape[0] - 9 * C, LANE), F32)
    for t in range(9):
        for m in range(4):
            here = t * BOX_ROWS + m * SLOT
            for n in range(2):
                u_ref[n, pl.ds(m, SLOT, stride=4), :] = w_ref[here : here + SLOT, n * LANE : n * LANE + LANE]
        d_ref[t * C : t * C + C, :] = jnp.concatenate([u_ref[0], u_ref[1]], axis=1).T
    lines = [jnp.zeros((40, 2 * C), F32) for _ in range(9)]
    zero = jnp.zeros((40, 2 * C - LANE), F32)
    for s, (r, at) in enumerate(BOX_CUTS):
        wide = jnp.concatenate([d_ref[pl.ds(s, 40, stride=64), :], zero], axis=1)
        lines[r] = lines[r] + (pltpu.roll(wide, at, 1) if at else wide)
    t_ref[...] = jnp.zeros_like(t_ref)
    for r in range(9):
        line = lines[r][:, :C]
        if r:
            line = line + lines[r - 1][:, C:]
        for n in range(2):
            t_ref[n, pl.ds(2 + r, 40, stride=9), :] = line[:, n * LANE : n * LANE + LANE]
    for n in range(2):
        for k in range(2):
            at = k * C + n * LANE
            t_ref[n, k : k + 1, :] = b_ref[:, at : at + LANE]
    rows = o_ref.shape[0]
    o_ref[...] = jnp.concatenate([t_ref[0, 0:rows, :], t_ref[1, 0:rows, :]], axis=1).astype(BF)


def box_call(kernel, shape, kind, name, *args):
    return pl.pallas_call(
        kernel,
        in_specs=[VM] * len(args),
        out_specs=VM,
        out_shape=shape_of(shape, kind),
        scratch_shapes=[
            pltpu.VMEM((2, 368, LANE), F32),
            pltpu.VMEM((40 * 64, LANE), F32),
            pltpu.VMEM((2, LANE, LANE), F32),
        ],
        compiler_params=pltpu.CompilerParams(vmem_limit_bytes=VMEM_LIMIT),
        name=name,
    )(*args)


def heads_call(rows, cols, scal, feats, masks, labels, box_target, full, tb, head, wb):
    canvases = feats.shape[0]
    own = rows * cols
    total = own + 2 * HALO * cols
    spread = jnp.repeat(jnp.eye(SLOT, 9, dtype=BF), LANE, axis=1)

    def per(shape):
        return pl.BlockSpec((1,) + shape, lambda c: (c,) + (0,) * len(shape))

    return pl.pallas_call(
        functools.partial(head_kernel, cols, rows),
        grid=(canvases,),
        in_specs=[
            pl.BlockSpec(memory_space=pltpu.SMEM),
            pl.BlockSpec((1, 3, total, C), lambda c: (c, 0, 0, 0), pipeline_mode=pl.Buffered(1)),
            per((SLOT, total)),
            per((SLOT, total)),
            per((4, SLOT, total)),
            whole(spread.shape),
            pl.BlockSpec(memory_space=pl.ANY),
            whole(tb.shape),
            pl.BlockSpec(memory_space=pl.ANY),
            whole(wb.shape),
        ],
        out_specs=[
            pl.BlockSpec(memory_space=pl.ANY),
            pl.BlockSpec(memory_space=pl.ANY),
            whole((9 * BOX_ROWS, C)),
            whole((1, 2 * C)),
            per((2, own, LANE)),
            whole((16, 256)),
        ],
        out_shape=[
            shape_of((9 * C, WIDE), BF),
            shape_of((18 * C, C), BF),
            shape_of((9 * BOX_ROWS, C)),
            shape_of((1, 2 * C)),
            shape_of((canvases, 2, own, LANE)),
            shape_of((16, 256)),
        ],
        scratch_shapes=[
            pltpu.VMEM((9, total, LANE), BF),
            pltpu.VMEM((total - 2 * cols, 2 * C), F32),
            pltpu.VMEM((total, C), BF),
            pltpu.VMEM((WIDE, own + 512), BF),
            pltpu.VMEM((own + 512, WIDE), BF),
            pltpu.VMEM((own + 256, 2 * C), BF),
            pltpu.VMEM((9 * C, 2 * C), BF),
            pltpu.VMEM((WIDE, 9 * C), BF),
            pltpu.VMEM((WIDE, 9 * C), F32),
            pltpu.VMEM((2 * C, 9 * C), F32),
            pltpu.SemaphoreType.DMA((3,)),
        ],
        compiler_params=pltpu.CompilerParams(vmem_limit_bytes=VMEM_LIMIT),
        name="heads",
    )(scal, feats, masks, labels, box_target, spread, full, tb, head, wb)


def place():
    img = lax.axis_index("img")
    cls = lax.axis_index("cls")
    return img // 2, img % 2, cls // 2, cls % 2


def target(z, y, x, c):
    return (z * 2 + y, x * 2 + c)


def owner(z, y, x, c):
    return ((z * 2 + y) * 2 + x) * 2 + c


def enter(peers):
    barrier = pltpu.get_barrier_semaphore()
    for peer in peers:
        pl.semaphore_signal(barrier, inc=1, device_id=peer, device_id_type=MESH)
    pl.semaphore_wait(barrier, len(peers))


class Mail:
    def __init__(self, send_sems, recv_sems):
        self.send_sems, self.recv_sems, self.used, self.sent = send_sems, recv_sems, 0, []

    def push(self, source, landing, peer):
        copy = pltpu.make_async_remote_copy(
            src_ref=source,
            dst_ref=landing,
            send_sem=self.send_sems.at[self.used],
            recv_sem=self.recv_sems.at[self.used],
            device_id=peer,
            device_id_type=MESH,
        )
        self.used += 1
        copy.start()
        self.sent.append(copy)
        return copy

    def close(self):
        for copy in self.sent:
            copy.wait_send()


def window_row(index, shard):
    return pl.multiple_of((index * shard + LEAD * C) // (16 * C) * 16, 16)


def gather_kernel(shard, s_ref, k_ref, n_ref, r_ref, full_ref, head_ref, count_ref, first_ref, last_ref, rim_ref, sh_ref, kx_ref, send_sems, recv_sems):
    z, y, x, c = place()
    block = k_ref.shape[0]
    win = s_ref.shape[0]
    others = [(k, j) for k in range(4) for j in range(2) if k or j]
    ring = [((z + k) % 4, (y + j) % 2) for k, j in others]
    line = [(z * 2 + y, (x * 2 + c + step) % 4) for step in (1, 3)]
    enter([target(zz, yy, x, c) for zz, yy in ring] + [target(z, y, 1 - x, c), target(z, y, x, 1 - c)] + line)
    mail = Mail(send_sems, recv_sems)
    me = owner(z, y, x, c)

    def rows(zz, yy):
        return pl.ds(pl.multiple_of((zz * 2 + yy) * block, 16), block)

    def lanes(cc):
        return pl.ds(pl.multiple_of(cc * HALF, LANE), HALF)

    got_kx = mail.push(k_ref, kx_ref, target(z, y, 1 - x, c))
    counts = [mail.push(n_ref, count_ref.at[z * 2 + y], target(zz, yy, x, c)) for zz, yy in ring]
    slot = sh_ref.at[me]
    got_z = [mail.push(s_ref, slot, target((z + k) % 4, y, x, c)) for k in range(1, 4)]
    got_y = [mail.push(s_ref, slot, target(z, 1 - y, x, c))]
    got_x = [mail.push(s_ref, slot, target(z, y, 1 - x, c))]
    got_c = [mail.push(s_ref, slot, target(z, y, x, 1 - c))]
    rims = [mail.push(r_ref.at[n], rim_ref.at[n], line[n]) for n in range(2)]
    count_ref[z * 2 + y] = n_ref[...]
    sh_ref[me] = s_ref[...]

    got_kx.wait_recv()
    mine = head_ref.at[rows(z, y), lanes(c)]
    head_ref[rows(z, y), lanes(c)] = k_ref[...] + kx_ref[...]
    got_kz = [mail.push(mine, mine, target((z + k) % 4, y, x, c)) for k in range(1, 4)]
    got_ky = [mail.push(mine, mine, target(z, 1 - y, x, c))]
    got_kc = [mail.push(mine, mine, target(z, y, x, 1 - c))]

    for k in range(1, 4):
        got_z[k - 1].wait_recv()
        slot = sh_ref.at[owner((z + 4 - k) % 4, y, x, c)]
        got_y.append(mail.push(slot, slot, target(z, 1 - y, x, c)))
        got_x.append(mail.push(slot, slot, target(z, y, 1 - x, c)))
        got_c.append(mail.push(slot, slot, target(z, y, x, 1 - c)))
    for k in range(1, 4):
        got_kz[k - 1].wait_recv()
        part = head_ref.at[rows((z + 4 - k) % 4, y), lanes(c)]
        got_ky.append(mail.push(part, part, target(z, 1 - y, x, c)))
        got_kc.append(mail.push(part, part, target(z, y, x, 1 - c)))
    for k in range(4):
        got_y[k].wait_recv()
        slot = sh_ref.at[owner((z + 4 - k) % 4, 1 - y, x, c)]
        got_x.append(mail.push(slot, slot, target(z, y, 1 - x, c)))
        got_c.append(mail.push(slot, slot, target(z, y, x, 1 - c)))
    for k in range(4):
        got_ky[k].wait_recv()
        part = head_ref.at[rows((z + 4 - k) % 4, 1 - y), lanes(c)]
        got_kc.append(mail.push(part, part, target(z, y, x, 1 - c)))
    for k in range(8):
        got_x[k].wait_recv()
        slot = sh_ref.at[owner((z + 4 - k % 4) % 4, (y + k // 4) % 2, 1 - x, c)]
        got_c.append(mail.push(slot, slot, target(z, y, x, 1 - c)))
    for copy in got_c + got_kc + counts + rims:
        copy.wait_recv()
    full_ref[...] = jnp.zeros_like(full_ref)

    def merge(d, carry):
        full_ref[pl.ds(window_row(d, shard), win), :] += sh_ref[d]
        return carry

    lax.fori_loop(0, 32, merge, 0)
    first_ref[...] = full_ref[0:TOWER_ROW, :]
    last_ref[...] = full_ref[TAIL_ROW:FULL_ROWS, :]
    mail.close()


def scatter_kernel(
    shard, head_ref, tower_ref, tail_ref, k_ref, n_ref, s_out, k_out, n_out,
    full_ref, sc_ref, sx_ref, sy_ref, sz_ref, kc_ref, ky_ref, kz_ref, kx_ref, mine_ref, peer_ref, far_ref, nz_ref, send_sems, recv_sems,
):
    z, y, x, c = place()
    block = kx_ref.shape[1]
    win = s_out.shape[0]
    enter([target((z + k) % 4, y, x, c) for k in range(1, 4)] + [target(z, 1 - y, x, c), target(z, y, 1 - x, c), target(z, y, x, 1 - c)])
    mail = Mail(send_sems, recv_sems)

    def rows(zz, yy):
        return pl.ds(pl.multiple_of((zz * 2 + yy) * block, 16), block)

    def lanes(cc):
        return pl.ds(pl.multiple_of(cc * HALF, LANE), HALF)

    def window(zz, yy, xx, cc):
        return pl.ds(window_row(owner(zz, yy, xx, cc), shard), win)

    mine_ref[0] = n_ref[...]
    sum_c = mail.push(mine_ref.at[0], peer_ref.at[0], target(z, y, x, 1 - c))
    spots = [(j, k) for j in (1, 0) for k in (1, 2, 3, 0)]
    got_kc = []
    for n, (j, k) in enumerate(spots):
        part = k_ref.at[rows((z + k) % 4, (y + j) % 2), lanes(1 - c)]
        got_kc.append(mail.push(part, kc_ref.at[n], target(z, y, x, 1 - c)))
    full_ref[0:TOWER_ROW, :] = head_ref[...]
    full_ref[TOWER_ROW:TAIL_ROW, :] = tower_ref[...]
    full_ref[TAIL_ROW:FULL_ROWS, :] = tail_ref[...]
    got_c = []
    for i in (1, 0):
        for n, (j, k) in enumerate(spots):
            part = full_ref.at[window((z + k) % 4, (y + j) % 2, (x + i) % 2, 1 - c), :]
            got_c.append(mail.push(part, sc_ref.at[(1 - i) * 8 + n], target(z, y, x, 1 - c)))

    sum_c.wait_recv()
    mine_ref[1] = mine_ref[0] + peer_ref[0]
    sum_x = mail.push(mine_ref.at[1], peer_ref.at[1], target(z, y, 1 - x, c))

    got_ky = []
    for n, (j, k) in enumerate(spots):
        got_kc[n].wait_recv()
        kc_ref[n] = kc_ref[n] + k_ref[rows((z + k) % 4, (y + j) % 2), lanes(c)]
        if j == 1:
            got_ky.append(mail.push(kc_ref.at[n], ky_ref.at[n], target(z, 1 - y, x, c)))
    got_x = []
    for n, (j, k) in enumerate(spots):
        got_c[n].wait_recv()
        sc_ref[n] = sc_ref[n] + full_ref[window((z + k) % 4, (y + j) % 2, 1 - x, c), :]
        got_x.append(mail.push(sc_ref.at[n], sx_ref.at[n], target(z, y, 1 - x, c)))

    sum_x.wait_recv()
    mine_ref[2] = mine_ref[1] + peer_ref[1]
    sum_y = mail.push(mine_ref.at[2], peer_ref.at[2], target(z, 1 - y, x, c))

    got_kz = []
    for n in range(4):
        got_ky[n].wait_recv()
        kc_ref[4 + n] = kc_ref[4 + n] + ky_ref[n]
        if n < 3:
            got_kz.append(mail.push(kc_ref.at[4 + n], kz_ref.at[n], target((z + n + 1) % 4, y, x, c)))
    got_y = []
    for n, (j, k) in enumerate(spots):
        got_c[8 + n].wait_recv()
        got_x[n].wait_recv()
        total = sc_ref[8 + n].astype(F32) + full_ref[window((z + k) % 4, (y + j) % 2, x, c), :].astype(F32)
        sc_ref[8 + n] = (total + sx_ref[n].astype(F32)).astype(BF)
        if j == 1:
            got_y.append(mail.push(sc_ref.at[8 + n], sy_ref.at[n], target(z, 1 - y, x, c)))

    sum_y.wait_recv()
    mine_ref[3] = mine_ref[2] + peer_ref[2]
    nz_ref[z] = mine_ref[3]
    sum_z = [mail.push(mine_ref.at[3], nz_ref.at[z], target((z + k) % 4, y, x, c)) for k in range(1, 4)]

    total = kc_ref[7].astype(F32)
    for n in range(3):
        got_kz[n].wait_recv()
        total += kz_ref[n].astype(F32)
    kx_ref[0] = total.astype(BF)
    got_kx = mail.push(kx_ref.at[0], kx_ref.at[1], target(z, y, 1 - x, c))
    got_z = []
    for n in range(4):
        got_y[n].wait_recv()
        sc_ref[12 + n] = sc_ref[12 + n] + sy_ref[n]
        if n < 3:
            got_z.append(mail.push(sc_ref.at[12 + n], sz_ref.at[n], target((z + n + 1) % 4, y, x, c)))
    total = sc_ref[15].astype(F32)
    for n in range(3):
        got_z[n].wait_recv()
        total += sz_ref[n].astype(F32)
    s_out[...] = total
    for copy in sum_z:
        copy.wait_recv()
    n_out[...] = (nz_ref[0] + nz_ref[1]) + (nz_ref[2] + nz_ref[3])
    got_kx.wait_recv()
    k_out[...] = kx_ref[0].astype(F32) + kx_ref[1].astype(F32)
    mail.close()


def fast_mesh(img_parts, cls_parts, class_rows):
    return img_parts == 8 and cls_parts == 4 and class_rows % 16 == 0


def flat_place(index, shard):
    return (index * shard + LEAD * C) % (16 * C)


def gather_all(shared_params, class_params, count, edges):
    img, cls = lax.axis_index("img"), lax.axis_index("cls")
    img_parts, cls_parts = lax.axis_size("img"), lax.axis_size("cls")
    shard = shared_params.shape[0]
    block, part = class_params.shape
    if not fast_mesh(img_parts, cls_parts, block):
        flat = lax.all_gather(shared_params.astype(BF), ("img", "cls"), axis=0, tiled=True)
        full = jnp.pad(flat, (LEAD * C, FULL_ROWS * C - LEAD * C - flat.shape[0])).reshape(FULL_ROWS, C)
        head = lax.all_gather(class_params.astype(BF), ("img", "cls"), axis=0)
        head = head.reshape(img_parts, cls_parts, block, part).transpose(0, 2, 1, 3).reshape(-1, CLS_OUT)
        pieces = []
        for half in range(2):
            pieces += [head[:, 180 * half : 180 * half + 180], head[:, 360 + 180 * half : 540 + 180 * half]]
            pieces.append(jnp.zeros((head.shape[0], HALF - 360), BF))
        ways = [[(i, (i + step) % cls_parts) for i in range(cls_parts)] for step in (1, cls_parts - 1)]
        rim = jnp.stack([lax.ppermute(edges[n], "cls", ways[n]) for n in range(2)])
        return full, full[:TOWER_ROW], full[TAIL_ROW:], jnp.concatenate(pieces, axis=1), lax.psum(count, "img"), rim
    rows = -(-(shard + 16 * C) // (16 * C)) * 16
    window = lax.dynamic_update_slice(
        jnp.zeros((rows * C,), BF), shared_params.astype(BF), (flat_place(img * cls_parts + cls, shard),)
    ).reshape(rows, C)
    wide = jnp.pad(class_params.astype(BF), ((0, 0), (part, HALF - part)))
    wide = lax.dynamic_slice_in_dim(
        jnp.pad(wide, ((0, 0), (0, part))), jnp.where(cls // 2 == 0, part, 0), HALF, 1
    )
    number = jnp.broadcast_to(count, (8, LANE))
    full, head, counts, first, last, rim = pl.pallas_call(
        functools.partial(gather_kernel, shard),
        in_specs=[VM] * 4,
        out_specs=[VM] * 6,
        out_shape=[
            shape_of((FULL_ROWS, C), BF),
            shape_of((img_parts * block, 2 * HALF), BF),
            shape_of((img_parts, 8, LANE)),
            shape_of((TOWER_ROW, C), BF),
            shape_of((FULL_ROWS - TAIL_ROW, C), BF),
            shape_of(edges.shape, BF),
        ],
        scratch_shapes=[
            pltpu.VMEM((img_parts * cls_parts, rows, C), BF),
            pltpu.VMEM((block, HALF), BF),
            pltpu.SemaphoreType.DMA((56,)),
            pltpu.SemaphoreType.DMA((56,)),
        ],
        compiler_params=pltpu.CompilerParams(collective_id=0, has_side_effects=True, vmem_limit_bytes=VMEM_LIMIT),
        name="gather",
    )(window, wide, number, edges)
    return full, first, last, head, jnp.sum(counts[:, 0, 0]), rim


def scatter_all(head, tower, tail, class_grad, sums, shard, block, part):
    img, cls = lax.axis_index("img"), lax.axis_index("cls")
    img_parts, cls_parts = lax.axis_size("img"), lax.axis_size("cls")
    if not fast_mesh(img_parts, cls_parts, block):
        flat = jnp.concatenate([head, tower, tail], axis=0).reshape(-1)
        flat = flat[LEAD * C : LEAD * C + shard * img_parts * cls_parts].astype(F32)
        shared = lax.psum_scatter(flat, ("img", "cls"), scatter_dimension=0, tiled=True)
        pieces = [class_grad[:, at : at + 180] for at in (0, HALF, 180, HALF + 180)]
        whole_grad = lax.psum_scatter(
            jnp.concatenate(pieces, axis=1).astype(F32), "img", scatter_dimension=0, tiled=True
        )
        return shared, lax.psum_scatter(whole_grad, "cls", scatter_dimension=1, tiled=True), lax.psum(sums, ("img", "cls"))
    rows = -(-(shard + 16 * C) // (16 * C)) * 16
    window, wide, sums = pl.pallas_call(
        functools.partial(scatter_kernel, shard),
        in_specs=[VM] * 5,
        out_specs=[VM] * 3,
        out_shape=[shape_of((rows, C)), shape_of((block, HALF)), shape_of(sums.shape)],
        scratch_shapes=[
            pltpu.VMEM((FULL_ROWS, C), BF),
            pltpu.VMEM((16, rows, C), BF),
            pltpu.VMEM((8, rows, C), BF),
            pltpu.VMEM((4, rows, C), BF),
            pltpu.VMEM((3, rows, C), BF),
            pltpu.VMEM((8, block, HALF), BF),
            pltpu.VMEM((4, block, HALF), BF),
            pltpu.VMEM((3, block, HALF), BF),
            pltpu.VMEM((2, block, HALF), BF),
            pltpu.VMEM((4,) + sums.shape, F32),
            pltpu.VMEM((3,) + sums.shape, F32),
            pltpu.VMEM((8, LANE), F32),
            pltpu.VMEM((4,) + sums.shape, F32),
            pltpu.SemaphoreType.DMA((53,)),
            pltpu.SemaphoreType.DMA((53,)),
        ],
        compiler_params=pltpu.CompilerParams(collective_id=1, has_side_effects=True, vmem_limit_bytes=VMEM_LIMIT),
        name="scatter",
    )(head, tower, tail, class_grad, sums)
    flat = lax.dynamic_slice_in_dim(window.reshape(-1), flat_place(img * cls_parts + cls, shard), shard)
    grad = lax.dynamic_slice_in_dim(wide, jnp.where(cls // 2 == 0, 0, part), part, 1)
    return flat, grad, sums


def column_plan():
    plan = []
    for half in range(2):
        for group in range(2):
            column, row, end = 360 * group + 180 * half, HALF * half + 180 * group, 360 * group + 180 * half + 180
            while column < end:
                count = min(end, (column // CLASSES + 1) * CLASSES) - column
                plan.append((row, count, column // CLASSES, column % CLASSES))
                column, row = column + count, row + count
        plan.append((HALF * half + 360, HALF - 360, -1, 0))
    return plan


def adamw_update(weight, first, second, grad):
    first_new = MOMENT_ONE * first + (1.0 - MOMENT_ONE) * grad
    second_new = MOMENT_TWO * second + (1.0 - MOMENT_TWO) * grad * grad
    first_hat = first_new / (1.0 - MOMENT_ONE**STEP)
    second_hat = second_new / (1.0 - MOMENT_TWO**STEP)
    weight_new = weight - RATE * (first_hat / (jnp.sqrt(second_hat) + EPSILON) + DECAY * weight)
    return (weight_new, first_new, second_new)


def valid_positives(boxes, match, full_rows, cols):
    place = jnp.arange(full_rows * cols, dtype=jnp.int32)
    row, col = place // cols, place % cols
    inside = jnp.zeros((boxes.shape[0], full_rows * cols), bool)
    for k in range(boxes.shape[1]):
        edge = boxes[:, k, :, None]
        inside |= (row >= edge[:, 0]) & (row < edge[:, 2]) & (col >= edge[:, 1]) & (col < edge[:, 3])
    return ((match >= 0) & inside[:, None]).astype(F32)


def cell_data(boxes, match, gt_labels, gt_deltas, first_row, rows, cols):
    full_rows = match.shape[2] // cols
    total = (rows + 2 * HALO) * cols
    place = jnp.arange(total, dtype=jnp.int32)[None]
    row = place // cols + (first_row - HALO)
    col = place % cols

    def crop(r, j):
        found = jnp.full((boxes.shape[0], total), -1, jnp.int32)
        for k in range(boxes.shape[1]):
            edge = boxes[:, k, :, None]
            inside = (r >= edge[:, 0]) & (r < edge[:, 2]) & (j >= edge[:, 1]) & (j < edge[:, 3])
            found = jnp.where(inside, k, found)
        return jnp.where((r >= 0) & (r < full_rows) & (j >= 0) & (j < cols), found, -1)

    centre = crop(row, col)
    valid = centre >= 0
    masks = jnp.stack([(crop(row + di, col + dj) == centre) & valid for di, dj in TAPS], axis=1)
    masks = jnp.pad(masks.astype(BF), ((0, 0), (0, SLOT - 9), (0, 0)))
    edge = HALO * cols
    near = jnp.pad(match, ((0, 0), (0, 0), (edge, edge)), constant_values=-2)
    near = lax.dynamic_slice_in_dim(near, first_row * cols, total, 2)
    near = jnp.where(valid[:, None], near, -2)
    near = jnp.pad(near, ((0, 0), (0, SLOT - 9), (0, 0)), constant_values=-2)
    labels = near
    targets = jnp.zeros((near.shape[0], 4) + near.shape[1:], F32)
    for g in range(gt_labels.shape[1]):
        labels = jnp.where(near == g, gt_labels[:, g, None, None], labels)
        targets = jnp.where((near == g)[:, None], gt_deltas[:, g, :, None, None], targets)
    return masks, labels.astype(F32), targets


def local(patches, boxes, match, gt_labels, gt_deltas, ema_old, shared_params, shared_m, shared_v, class_params, class_m, class_v):
    cls_rank = lax.axis_index("cls")
    canvases, rows, width = patches.shape
    cols = width // PATCH
    masks, labels, targets = cell_data(boxes, match, gt_labels, gt_deltas, cls_rank * rows, rows, cols)
    full_rows = match.shape[2] // cols
    count = jnp.sum(valid_positives(boxes, match, full_rows, cols))
    edges = jnp.stack([patches[:, rows - HALO :], patches[:, :HALO]]).reshape(2, canvases * HALO, width)
    edges = jnp.concatenate([edges[..., : width // 2], edges[..., width // 2 :]], axis=1)
    full, first, last, head, positives, rim = gather_all(shared_params, class_params, count, edges)
    norm = jnp.maximum(positives, 1.0)
    ema_new = EMA_KEEP * ema_old + (1.0 - EMA_KEEP) * norm
    tb = last[0:2].reshape(1, 2 * C).astype(F32)
    wb = box_call(box_in_kernel, (9 * BOX_ROWS, C), BF, "box_in", last)
    stem_pre, stem_out, feats, lat_w = stem_forward(patches, rim, first)
    scal = jnp.stack([1.0 / ema_new, 1.0 / norm])
    class_grad, tower_grad, dwb, db, feature_grad, sums = heads_call(
        rows, cols, scal, feats, masks, labels, targets, full, tb, head, wb
    )
    first_grad = stem_backward(patches, feature_grad, stem_out, stem_pre, lat_w)
    last_grad = box_call(box_out_kernel, last.shape, BF, "box_out", dwb, db)
    shared_grad, class_grad, sums = scatter_all(
        first_grad, tower_grad, last_grad, class_grad, sums, shared_params.shape[0], *class_params.shape
    )
    loss = jnp.sum(sums[0:8]) / ema_new + jnp.sum(sums[8:16]) / norm
    return (
        loss,
        ema_new,
        *adamw_update(shared_params, shared_m, shared_v, shared_grad),
        *adamw_update(class_params, class_m, class_v, class_grad),
    )


def solution(mesh):
    spread = P(("img", "cls"))
    block = P("img", "cls")
    return jax.shard_map(
        local,
        mesh=mesh,
        in_specs=(
            P("img", "cls", None),
            P("img", None, None),
            P("img", None, None),
            P("img", None),
            P("img", None, None),
            P(),
            spread,
            spread,
            spread,
            block,
            block,
            block,
        ),
        out_specs=(P(), P(), spread, spread, spread, block, block, block),
        check_vma=False,
    )
```

```python
import functools

import jax
import jax.numpy as jnp
from jax import lax
from jax.experimental import pallas as pl
from jax.experimental.pallas import tpu as pltpu
from jax.sharding import PartitionSpec as P

C = 256
CLASSES = 80
ANCH = 9
PATCH = 192
BOX_OUT = 36
CLS_OUT = ANCH * CLASSES
STEP = 5
GT = 16
HALO = 4
SLOT = 16
BOX_ROWS = 4 * SLOT
LANE = 128
WIDE = 768
GROUP = 16

PRIOR = -4.59511985013459
ALPHA = 0.25
HUBER = 1.0 / 9.0
EMA_KEEP = 0.9
RATE = 0.01
MOMENT_ONE = 0.5
MOMENT_TWO = 0.5
DECAY = 0.05
EPSILON = 1e-08

LENGTHS = [PATCH * C, C, C * C, C, 18 * C * C, 2 * C, 9 * C * BOX_OUT]
TOWER_AT = sum(LENGTHS[:4]) // C
LEAD = -TOWER_AT % 16
TOWER_ROW = TOWER_AT + LEAD
TAIL_ROW = TOWER_ROW + 18 * C
FULL_ROWS = -(-(LEAD + sum(LENGTHS) // C) // 16) * 16
HALF = 384
MESH = pl.DeviceIdType.MESH

BF = jnp.bfloat16
F32 = jnp.float32
TAPS = [(di, dj) for di in (-1, 0, 1) for dj in (-1, 0, 1)]
NN = (((1,), (0,)), ((), ()))
NT = (((1,), (1,)), ((), ()))
TN = (((0,), (0,)), ((), ()))
K0 = 0.7978845608028654
K1 = 0.044715


def mm(a, b, dims=NN):
    return lax.dot_general(a, b, dims, preferred_element_type=F32)


def gelu(x):
    return 0.5 * x * (1.0 + jnp.tanh(K0 * (x + K1 * x * x * x)))


def gelu_slope(x):
    square = x * x
    th = jnp.tanh(K0 * (x + K1 * x * square))
    return 0.5 * (1.0 + th) + (0.5 * K0) * x * (1.0 - th * th) * (1.0 + 3.0 * K1 * square)


def columns_of(x, pairs, width):
    return [x[:, width * k : width * (k + 1)] for k in range(pairs)]


def stem_kernel(pairs, cols, rows, x_ref, h_ref, head_ref, pre_ref, so_ref, f_ref, lw_ref, t_ref, w_ref, b_ref, lb_ref):
    step = pl.program_id(0)
    canvases = x_ref.shape[0]
    own_rows = canvases * rows
    total = (rows + 2 * HALO) * cols

    @pl.when(step == 0)
    def _():
        head = head_ref[...].astype(F32)
        w_ref[...] = jnp.zeros_like(w_ref)
        stem_w = head[LEAD : LEAD + PATCH].astype(BF)
        w_ref[:PATCH, :C] = stem_w
        w_ref[PATCH:, C:] = stem_w
        bias = head[LEAD + PATCH : LEAD + PATCH + 1]
        b_ref[...] = jnp.concatenate([bias, bias], axis=1)
        lw_ref[...] = head[LEAD + PATCH + 1 : TOWER_ROW - 1].astype(BF)
        lb_ref[...] = head[TOWER_ROW - 1 : TOWER_ROW]
        for c in range(canvases):
            for n in range(2):
                t_ref[c, n, 0:8, :] = jnp.zeros((8, LANE), F32)
                t_ref[c, n, 8 + total : 16 + total, :] = jnp.zeros((8, LANE), F32)

    x = x_ref[...].reshape(own_rows, x_ref.shape[2])
    own = columns_of(x, pairs, 2 * PATCH)
    half = pl.num_programs(0) // 2
    lanes = pl.ds(pl.multiple_of(step % half * x.shape[1], LANE), x.shape[1])
    many_rows = h_ref.shape[1] // 2
    near = [h_ref[n, :, lanes].astype(F32) for n in range(2)]
    near = [jnp.where(step < half, one[:many_rows], one[many_rows:]) for one in near]
    rim = columns_of(jnp.concatenate(near, axis=0).astype(BF), pairs, 2 * PATCH)
    pre = mm(jnp.concatenate(own + rim, axis=0), w_ref[...]) + b_ref[...]
    count = pairs * own_rows
    pre_ref[...] = pre[:count]
    out = gelu(pre).astype(BF)
    so_ref[...] = out[:count]
    for half in range(2):
        feat = mm(out[:, half * C : half * C + C], lw_ref[...]) + lb_ref[...]
        for k in range(pairs):
            j = step * 2 * pairs + 2 * k + half
            for c in range(canvases):
                at = k * own_rows + c * rows
                up_at = count + k * 2 * HALO * canvases + c * HALO
                down_at = up_at + HALO * canvases
                for n in range(2):
                    side = slice(n * LANE, n * LANE + LANE)
                    place = pl.ds(8 + HALO * cols + j, rows, stride=cols)
                    t_ref[c, n, place, :] = feat[at : at + rows, side]
                    place = pl.ds(8 + j, HALO, stride=cols)
                    t_ref[c, n, place, :] = feat[up_at : up_at + HALO, side]
                    place = pl.ds(8 + (HALO + rows) * cols + j, HALO, stride=cols)
                    t_ref[c, n, place, :] = feat[down_at : down_at + HALO, side]

    @pl.when(step == pl.num_programs(0) - 1)
    def _():
        piece = 4 * cols

        def move(i, carry):
            base = pl.multiple_of(i * piece, 16)
            for c in range(canvases):
                for n in range(2):
                    value = t_ref[c, n, pl.ds(base, piece + 16), :]
                    for k in range(3):
                        moved = value[7 + k : 7 + k + piece].astype(BF)
                        f_ref[c, k, pl.ds(base, piece), n * LANE : n * LANE + LANE] = moved
            return carry

        lax.fori_loop(0, total // piece, move, 0)


def stem_back_kernel(pairs, cols, rows, x_ref, fg_ref, so_ref, pre_ref, lw_ref, head_ref, sw_out, sb_out, lw_out, lb_out, h_ref):
    step = pl.program_id(0)
    canvases = x_ref.shape[0]

    @pl.when(step == 0)
    def _():
        sw_out[...] = jnp.zeros_like(sw_out)
        sb_out[...] = jnp.zeros_like(sb_out)
        lw_out[...] = jnp.zeros_like(lw_out)
        lb_out[...] = jnp.zeros_like(lb_out)

    x = x_ref[...].reshape(canvases * rows, x_ref.shape[2])
    own = jnp.concatenate(columns_of(x, pairs, 2 * PATCH), axis=0)
    low = []
    for half in range(2):
        parts = []
        for k in range(pairs):
            j = step * 2 * pairs + 2 * k + half
            for c in range(canvases):
                place = pl.ds(j, rows, stride=cols)
                parts.append(jnp.concatenate([fg_ref[c, n, place, :] for n in range(2)], axis=1))
        grad32 = jnp.concatenate(parts, axis=0)
        grad = grad32.astype(BF)
        cut = slice(half * C, half * C + C)
        lw_out[...] += mm(so_ref[:, cut], grad, TN)
        lb_out[...] += jnp.sum(grad32, axis=0, keepdims=True)
        back = mm(grad, lw_ref[...], NT) * gelu_slope(pre_ref[:, cut])
        back = back.astype(BF)
        sb_out[...] += jnp.sum(back.astype(F32), axis=0, keepdims=True)
        low.append(back)
    both = mm(own, jnp.concatenate(low, axis=1), TN)
    sw_out[...] += both[:PATCH, :C] + both[PATCH:, C:]

    @pl.when(step == pl.num_programs(0) - 1)
    def _():
        at = LEAD + PATCH
        h_ref[0:LEAD, :] = jnp.zeros((LEAD, C), F32)
        h_ref[LEAD:at, :] = sw_out[...]
        h_ref[at : at + 1, :] = sb_out[...]
        h_ref[at + 1 : TOWER_ROW - 1, :] = lw_out[...]
        h_ref[TOWER_ROW - 1 :, :] = lb_out[...]
        head_ref[...] = h_ref[...].astype(BF)


def aligned(value, multiple):
    return value if isinstance(value, int) else pl.multiple_of(value, multiple)


def many(mask, count):
    return jnp.concatenate([mask] * count, axis=1)


def weight_sums(canvas, cols, edge, own, grad, source, mx_ref, sum_ref):
    def go(x_ref):
        def triple(n, carry):
            at = pl.multiple_of(edge + cols * (n - 1), 16)
            for k in range(3):
                mask = mx_ref[n * 3 + k, edge : edge + own, :]
                x_ref[:, k * C : k * C + C] = source[k, pl.ds(at, own), :] * many(mask, 2)
            side = pl.ds(pl.multiple_of(n * 3 * C, C), 3 * C)
            sum_ref[:, side] = jnp.where(canvas > 0, sum_ref[:, side], 0.0) + mm(grad(), x_ref[...])
            return carry

        lax.fori_loop(0, 3, triple, 0)

    pl.run_scoped(go, pltpu.VMEM((own, 3 * C), BF))


def head_kernel(
    cols, rows, scal_ref, f_ref, mk_ref, lab_ref, btt_ref, e_ref, full_ref, tb_ref, head_ref, wb_ref,
    class_ref, tower_ref, dwb_ref, db_ref, fg_ref, sums_ref,
    mx_ref, pre_ref, bt_ref, lgt_ref, lgs_ref, g_ref, wt_ref, wct_ref, dwc_ref, dwt_ref, copy_sems,
):
    own = rows * cols
    edge = HALO * cols
    total = own + 2 * edge
    shift = [cols * di + dj for di, dj in TAPS]

    @pl.when(pl.program_id(0) == 0)
    def _():
        dwb_ref[...] = jnp.zeros_like(dwb_ref)
        db_ref[...] = jnp.zeros_like(db_ref)
        sums_ref[...] = jnp.zeros_like(sums_ref)
        def fetch(held_ref):
            copies = [pltpu.make_async_copy(head_ref, held_ref, copy_sems.at[2])]
            for n in range(2):
                rows_of = full_ref.at[TOWER_ROW + n * 9 * C : TOWER_ROW + (n + 1) * 9 * C, :]
                copies.append(pltpu.make_async_copy(rows_of, wt_ref.at[:, n * C : n * C + C], copy_sems.at[n]))
            for copy in copies:
                copy.start()
            copies[0].wait()

            def turn(t, carry):
                at = pl.multiple_of(t * C, C)
                wct_ref[:, pl.ds(at, C)] = held_ref[pl.ds(at, C), :].T
                return carry

            lax.fori_loop(0, 9, turn, 0)
            for copy in copies[1:]:
                copy.wait()

        pl.run_scoped(fetch, pltpu.VMEM((9 * C, WIDE), BF))

    def spread(i, carry):
        at = pl.multiple_of(i * 384, 128)
        wide = mm(mk_ref[0, :, pl.ds(at, 384)], e_ref[...], TN).astype(BF)
        for t in range(9):
            mx_ref[t, pl.ds(at, 384), :] = wide[:, t * LANE : (t + 1) * LANE]
        return carry

    lax.fori_loop(0, total // 384, spread, 0)

    def twice(mask):
        return jnp.concatenate([mask, mask], axis=1)

    def build(source, at, count, x_ref):
        for t, (di, dj) in enumerate(TAPS):
            value = source[dj + 1, pl.ds(pl.multiple_of(at + cols * di, 16), count), :]
            x_ref[:, t * C : (t + 1) * C] = value * twice(mx_ref[t, pl.ds(at, count), :])

    first_tower = cols
    tower_rows = total - 2 * cols
    first_logit = edge - 256
    logit_cells = own + 512
    first_g = edge - 128
    g_cells = own + 256

    def heads(ct32_ref, ct_ref):
        zero = jnp.zeros((cols + 8, C), F32)
        ct32_ref[0 : cols + 8, :] = zero
        ct32_ref[8 + total - cols : 16 + total, :] = zero
        zero = jnp.zeros((cols, C), BF)
        bt_ref[0:cols, :] = zero
        bt_ref[total - cols : total, :] = zero
        piece = tower_rows // 3

        def towers(x_ref):
            def tower(i, carry):
                row = pl.multiple_of(i * piece, 16)
                at = pl.multiple_of(first_tower + i * piece, 16)
                build(f_ref.at[0], at, piece, x_ref)
                pre = mm(x_ref[...], wt_ref[...]) + tb_ref[...]
                pre_ref[pl.ds(row, piece), :] = pre
                out = gelu(pre)
                ct32_ref[pl.ds(pl.multiple_of(8 + at, 8), piece), :] = out[:, :C]
                bt_ref[pl.ds(at, piece), :] = out[:, C:].astype(BF)
                return carry

            lax.fori_loop(0, 3, tower, 0)

        pl.run_scoped(towers, pltpu.VMEM((piece, 9 * C), BF))

        def move(i, carry):
            base = pl.multiple_of(i * edge, 16)
            value = ct32_ref[pl.ds(base, edge + 16), :]
            for k in range(3):
                ct_ref[k, pl.ds(base, edge), :] = value[7 + k : 7 + k + edge].astype(BF)
            return carry

        lax.fori_loop(0, total // edge, move, 0)
        def logits(xa_ref, la_ref):
            inv_ema = scal_ref[0]
            number = lax.broadcasted_iota(jnp.int32, (GROUP, 256), 0).astype(F32)
            lane = lax.broadcasted_iota(jnp.int32, (8, 256), 1)
            plan = column_plan()

            def ready(q, x_ref):
                build(ct_ref, pl.multiple_of(first_logit + q * 256, 128), 256, x_ref)

            def work(q, x_ref, l_ref):
                l_ref[...] = mm(wct_ref[...], x_ref[...], NT)

            def focal(q, l_ref):
                row = pl.multiple_of(q * 256, 128)
                at = pl.multiple_of(first_logit + row, 128)
                spot = lane + at
                mine = (spot >= edge) & (spot < edge + own)
                lines = [lab_ref[0, a : a + 1, pl.ds(at, 256)] for a in range(ANCH)]
                rest = [jnp.where(line > -1.5, 1.0 - ALPHA, 0.0) for line in lines]
                pulls = [line * inv_ema for line in rest]
                total_focal = jnp.zeros((8, 256), F32)
                for first in range(0, WIDE, GROUP):
                    value = l_ref[first : first + GROUP, :] + PRIOR
                    key = None
                    for begin, count, anchor, klass in plan:
                        if begin >= first + GROUP or begin + count <= first:
                            continue
                        if anchor < 0:
                            parts = [jnp.full((GROUP, 256), n, F32) for n in (-2.0, 0.0, 0.0)]
                        else:
                            parts = [lines[anchor] - float(klass - (begin - first)), rest[anchor], pulls[anchor]]
                            parts = [jnp.broadcast_to(part, (GROUP, 256)) for part in parts]
                        if key is None:
                            key, other, pull_other = parts
                        else:
                            later = number >= float(begin - first)
                            key = jnp.where(later, parts[0], key)
                            other = jnp.where(later, parts[1], other)
                            pull_other = jnp.where(later, parts[2], pull_other)
                    hit = key == number
                    side = jnp.where(hit, -value, value)
                    small = jnp.exp(-jnp.abs(side))
                    whole_one = 1.0 + small
                    ratio = pltpu.reciprocal(whole_one, approx=True)
                    ratio = ratio * (2.0 - whole_one * ratio)
                    part = small * ratio
                    up = side >= 0.0
                    prob = jnp.where(up, ratio, part)
                    miss = jnp.where(up, part, ratio)
                    tiny = small * (1.0 - 0.5 * small)
                    cross = jnp.maximum(side, 0.0) + jnp.where(small < 0.001, tiny, jnp.log(whole_one))
                    square = prob * prob
                    value = square * cross * jnp.where(hit, ALPHA, other)
                    pull = square * (2.0 * miss * cross + prob) * jnp.where(hit, -ALPHA * inv_ema, pull_other)
                    l_ref[first : first + GROUP, :] = pull
                    lgt_ref[first : first + GROUP, pl.ds(row, 256)] = pull.astype(BF)
                    total_focal += jnp.sum(value.reshape(GROUP // 8, 8, 256), axis=0)
                sums_ref[0:8, :] += jnp.where(mine, total_focal, 0.0)
                lgs_ref[pl.ds(row, 256), :] = l_ref[...].T.astype(BF)

            def logits_of(q, carry):
                ready(q, xa_ref)
                work(q, xa_ref, la_ref)
                focal(q, la_ref)
                return carry

            lax.fori_loop(0, logit_cells // 256, logits_of, 0)

        pl.run_scoped(logits, pltpu.VMEM((256, 9 * C), BF), pltpu.VMEM((WIDE, 256), F32))
        weight_sums(pl.program_id(0), cols, edge, own, lambda: lgt_ref[:, 256 : 256 + own], ct_ref, mx_ref, dwc_ref)

    pl.run_scoped(heads, pltpu.VMEM((total + 16, C), F32), pltpu.VMEM((3, total, C), BF))

    def box_forward(gg_ref, y_ref):
        inv_norm = scal_ref[1]

        def outer(i, carry):
            at = pl.multiple_of(i * 768, 128)
            y_ref[:, pl.ds(at, 768)] = mm(wb_ref[...], bt_ref[pl.ds(at, 768), :], NT)
            return carry

        lax.fori_loop(0, total // 768, outer, 0)
        lane = lax.broadcasted_iota(jnp.int32, (SLOT, total), 1)
        mine = (lane >= edge) & (lane < edge + own)

        def guess(m, carry):
            acc = jnp.zeros((SLOT, total), F32)
            for t in range(9):
                value = y_ref[pl.ds(pl.multiple_of(t * BOX_ROWS + m * SLOT, 8), SLOT), :]
                moved = pltpu.roll(value, (-shift[t]) % total, 1)
                acc += moved * mk_ref[0, t : t + 1, :].astype(F32)
            differ = acc - btt_ref[0, m]
            positive = lab_ref[0] >= 0.0
            size = jnp.abs(differ)
            loss = jnp.where(size < HUBER, 0.5 * differ * differ / HUBER, size - 0.5 * HUBER)
            loss = jnp.where(positive & mine, loss, 0.0)
            part = loss[:, 0:256]
            for k in range(1, total // 256):
                part += loss[:, k * 256 : (k + 1) * 256]
            sums_ref[8:16, :] += part[0:8] + part[8:16]
            pull = jnp.minimum(jnp.maximum(differ / HUBER, -1.0), 1.0) * inv_norm
            pull = jnp.where(positive, pull, 0.0)
            gg_ref[pl.ds(pl.multiple_of(m * SLOT, 8), SLOT), :] = pull
            return carry

        lax.fori_loop(0, 4, guess, 0)

    def box_back(gg_ref, xg_ref):
        for t in range(9):
            moved = pltpu.roll(gg_ref[...], shift[t] % total, 1)
            xg_ref[t * BOX_ROWS : (t + 1) * BOX_ROWS, :] = (moved * mk_ref[0, 8 - t : 9 - t, :].astype(F32)).astype(BF)
        dwb_ref[...] += mm(xg_ref[:, edge : edge + own], bt_ref[edge : edge + own, :])

        def into(q, carry):
            row = pl.multiple_of(q * 256, 128)
            grad = mm(xg_ref[:, pl.ds(pl.multiple_of(first_g + row, 128), 256)], wb_ref[...], TN)
            pre = pre_ref[pl.ds(pl.multiple_of(first_g - first_tower + row, 16), 256), C:]
            g_ref[pl.ds(row, 256), C:] = (grad * gelu_slope(pre)).astype(BF)
            return carry

        lax.fori_loop(0, g_cells // 256, into, 0)

    def boxes(gg_ref):
        pl.run_scoped(functools.partial(box_forward, gg_ref), pltpu.VMEM((9 * BOX_ROWS, total), F32))
        pl.run_scoped(functools.partial(box_back, gg_ref), pltpu.VMEM((9 * BOX_ROWS, total), BF))

    pl.run_scoped(boxes, pltpu.VMEM((BOX_ROWS, total), F32))

    def class_back(z_ref):
        z_ref[:, 0:8, :] = jnp.zeros((3, 8, C), F32)
        z_ref[:, 8 + g_cells : 16 + g_cells, :] = jnp.zeros((3, 8, C), F32)
        piece = g_cells // 4

        def multiply(i, carry):
            row = pl.multiple_of(i * piece, 16)
            for k in range(3):
                acc = jnp.zeros((piece, C), F32)
                for r in range(3):
                    t = r * 3 + k
                    source = row + first_g - cols * (r - 1)
                    mask = mx_ref[t, pl.ds(pl.multiple_of(source, 16), piece), :]
                    value = lgs_ref[pl.ds(pl.multiple_of(source - first_logit, 16), piece), :]
                    value = value * jnp.concatenate([mask] * (WIDE // LANE), axis=1)
                    acc += mm(value, wct_ref[:, t * C : t * C + C])
                z_ref[k, pl.ds(pl.multiple_of(8 + row, 8), piece), :] = acc
            return carry

        lax.fori_loop(0, 4, multiply, 0)

        def collect(q, carry):
            row = pl.multiple_of(q * 256, 128)
            grad = z_ref[1, pl.ds(pl.multiple_of(8 + row, 8), 256), :]
            grad += z_ref[0, pl.ds(row, 272), :][9:265] + z_ref[2, pl.ds(row, 272), :][7:263]
            pre = pre_ref[pl.ds(pl.multiple_of(first_g - first_tower + row, 16), 256), :C]
            g_ref[pl.ds(row, 256), :C] = (grad * gelu_slope(pre)).astype(BF)
            return carry

        lax.fori_loop(0, g_cells // 256, collect, 0)

    pl.run_scoped(class_back, pltpu.VMEM((3, g_cells + 16, C), F32))

    def tower_back(z_ref, gt_ref):
        def flip(q, carry):
            row = pl.multiple_of(q * 256, 128)
            part = g_ref[pl.ds(pl.multiple_of(edge - first_g + row, 16), 256), :].astype(F32)
            gt_ref[:, pl.ds(row, 256)] = part.T.astype(BF)
            db_ref[...] += jnp.sum(part, axis=0, keepdims=True)
            return carry

        lax.fori_loop(0, own // 256, flip, 0)
        weight_sums(pl.program_id(0), cols, edge, own, lambda: gt_ref[...], f_ref.at[0], mx_ref, dwt_ref)
        first_z = edge - 16
        piece = (own + 32) // 2

        def multiply(i, carry):
            row = pl.multiple_of(i * piece, 16)
            for k in range(3):
                acc = jnp.zeros((piece, C), F32)
                for r in range(3):
                    t = r * 3 + k
                    source = row + first_z - cols * (r - 1)
                    mask = mx_ref[t, pl.ds(pl.multiple_of(source, 16), piece), :]
                    value = g_ref[pl.ds(pl.multiple_of(source - first_g, 16), piece), :]
                    value = value * jnp.concatenate([mask] * (2 * C // LANE), axis=1)
                    acc += mm(value, wt_ref[t * C : t * C + C, :], NT)
                z_ref[k, pl.ds(row, piece), :] = acc
            return carry

        lax.fori_loop(0, 2, multiply, 0)

        def collect(q, carry):
            row = pl.multiple_of(q * 256, 128)
            base = pl.multiple_of(row + 8, 8)
            grad = z_ref[1, pl.ds(pl.multiple_of(16 + row, 8), 256), :]
            grad += z_ref[0, pl.ds(base, 272), :][9:265] + z_ref[2, pl.ds(base, 272), :][7:263]
            grad = grad.astype(BF).astype(F32)
            for n in range(2):
                fg_ref[0, n, pl.ds(row, 256), :] = grad[:, n * LANE : n * LANE + LANE]
            return carry

        lax.fori_loop(0, own // 256, collect, 0)

    pl.run_scoped(
        tower_back,
        pltpu.VMEM((3, own + 32, C), F32),
        pltpu.VMEM((2 * C, own), BF),
    )

    @pl.when(pl.program_id(0) == pl.num_programs(0) - 1)
    def _():
        def deliver(class_held, tower_held):
            def turn(t, carry):
                at = pl.multiple_of(t * C, C)
                tower_held[pl.ds(at, C), :] = dwt_ref[0:C, pl.ds(at, C)].astype(BF).T
                tower_held[pl.ds(pl.multiple_of(9 * C + at, C), C), :] = dwt_ref[C:, pl.ds(at, C)].astype(BF).T
                class_held[pl.ds(at, C), :] = dwc_ref[:, pl.ds(at, C)].astype(BF).T
                return carry

            lax.fori_loop(0, 9, turn, 0)
            copies = [
                pltpu.make_async_copy(class_held, class_ref, copy_sems.at[0]),
                pltpu.make_async_copy(tower_held, tower_ref, copy_sems.at[1]),
            ]
            for copy in copies:
                copy.start()
            for copy in copies:
                copy.wait()

        pl.run_scoped(deliver, pltpu.VMEM((9 * C, WIDE), BF), pltpu.VMEM((18 * C, C), BF))


def whole(shape):
    return pl.BlockSpec(shape, lambda *_: (0,) * len(shape))


def shape_of(shape, dtype=F32):
    return jax.ShapeDtypeStruct(shape, dtype)


VM = pl.BlockSpec(memory_space=pltpu.VMEM)
VMEM_LIMIT = 63 * 1024 * 1024


def stem_forward(patches, rim, head):
    canvases, rows, width = patches.shape
    cols = width // PATCH
    pairs = 8
    steps = cols // (2 * pairs)
    chunk = 2 * pairs * PATCH
    count = pairs * canvases * rows
    total = (rows + 2 * HALO) * cols
    return pl.pallas_call(
        functools.partial(stem_kernel, pairs, cols, rows),
        grid=(steps,),
        in_specs=[
            pl.BlockSpec((canvases, rows, chunk), lambda s: (0, 0, s)),
            whole(rim.shape),
            whole(head.shape),
        ],
        out_specs=[
            pl.BlockSpec((count, 2 * C), lambda s: (s, 0)),
            pl.BlockSpec((count, 2 * C), lambda s: (s, 0)),
            whole((canvases, 3, total, C)),
            whole((C, C)),
        ],
        out_shape=[
            shape_of((steps * count, 2 * C)),
            shape_of((steps * count, 2 * C), BF),
            shape_of((canvases, 3, total, C), BF),
            shape_of((C, C), BF),
        ],
        scratch_shapes=[
            pltpu.VMEM((canvases, 2, total + 16, LANE), F32),
            pltpu.VMEM((2 * PATCH, 2 * C), BF),
            pltpu.VMEM((1, 2 * C), F32),
            pltpu.VMEM((1, C), F32),
        ],
        compiler_params=pltpu.CompilerParams(vmem_limit_bytes=VMEM_LIMIT),
        name="stem",
    )(patches, rim, head)


def stem_backward(patches, feature_grad, stem_out, stem_pre, lat_w):
    canvases, rows, width = patches.shape
    cols = width // PATCH
    pairs = 8
    steps = cols // (2 * pairs)
    chunk = 2 * pairs * PATCH
    count = pairs * canvases * rows
    return pl.pallas_call(
        functools.partial(stem_back_kernel, pairs, cols, rows),
        grid=(steps,),
        in_specs=[
            pl.BlockSpec((canvases, rows, chunk), lambda s: (0, 0, s)),
            whole((canvases, 2, rows * cols, LANE)),
            pl.BlockSpec((count, 2 * C), lambda s: (s, 0)),
            pl.BlockSpec((count, 2 * C), lambda s: (s, 0)),
            whole((C, C)),
        ],
        out_specs=whole((TOWER_ROW, C)),
        out_shape=shape_of((TOWER_ROW, C), BF),
        scratch_shapes=[
            pltpu.VMEM((PATCH, C), F32),
            pltpu.VMEM((1, C), F32),
            pltpu.VMEM((C, C), F32),
            pltpu.VMEM((1, C), F32),
            pltpu.VMEM((TOWER_ROW, C), F32),
        ],
        compiler_params=pltpu.CompilerParams(vmem_limit_bytes=VMEM_LIMIT),
        name="stem_back",
    )(patches, feature_grad, stem_out, stem_pre, lat_w)


BOX_CUTS = [(BOX_OUT * n // C, BOX_OUT * n % C) for n in range(64)]


def box_in_kernel(tail_ref, o_ref, t_ref, d_ref, u_ref):
    tail = tail_ref[...].astype(F32)
    count = tail.shape[0]
    lane = lax.broadcasted_iota(jnp.int32, (40, LANE), 1)
    for n in range(2):
        t_ref[n, 0:count, :] = tail[:, n * LANE : n * LANE + LANE]
        t_ref[n, count:, :] = jnp.zeros((t_ref.shape[1] - count, LANE), F32)
    lines = []
    for r in range(9):
        lines.append(jnp.concatenate([t_ref[n, pl.ds(2 + r, 40, stride=9), :] for n in range(2)], axis=1))
    for s, (r, at) in enumerate(BOX_CUTS):
        wide = jnp.concatenate([lines[r], lines[min(r + 1, 8)]], axis=1)
        d_ref[pl.ds(s, 40, stride=64), :] = jnp.where(lane < BOX_OUT, wide[:, at : at + LANE], 0.0)
    for t in range(9):
        turned = d_ref[t * C : t * C + C, :].T
        for n in range(2):
            u_ref[n] = turned[:, n * LANE : n * LANE + LANE]
        for m in range(4):
            here = t * BOX_ROWS + m * SLOT
            parts = [u_ref[n, pl.ds(m, SLOT, stride=4), :] for n in range(2)]
            o_ref[here : here + SLOT, :] = jnp.concatenate(parts, axis=1).astype(BF)


def box_out_kernel(w_ref, b_ref, o_ref, t_ref, d_ref, u_ref):
    u_ref[...] = jnp.zeros_like(u_ref)
    d_ref[9 * C :, :] = jnp.zeros((d_ref.shape[0] - 9 * C, LANE), F32)
    for t in range(9):
        for m in range(4):
            here = t * BOX_ROWS + m * SLOT
            for n in range(2):
                u_ref[n, pl.ds(m, SLOT, stride=4), :] = w_ref[here : here + SLOT, n * LANE : n * LANE + LANE]
        d_ref[t * C : t * C + C, :] = jnp.concatenate([u_ref[0], u_ref[1]], axis=1).T
    lines = [jnp.zeros((40, 2 * C), F32) for _ in range(9)]
    zero = jnp.zeros((40, 2 * C - LANE), F32)
    for s, (r, at) in enumerate(BOX_CUTS):
        wide = jnp.concatenate([d_ref[pl.ds(s, 40, stride=64), :], zero], axis=1)
        lines[r] = lines[r] + (pltpu.roll(wide, at, 1) if at else wide)
    t_ref[...] = jnp.zeros_like(t_ref)
    for r in range(9):
        line = lines[r][:, :C]
        if r:
            line = line + lines[r - 1][:, C:]
        for n in range(2):
            t_ref[n, pl.ds(2 + r, 40, stride=9), :] = line[:, n * LANE : n * LANE + LANE]
    for n in range(2):
        for k in range(2):
            at = k * C + n * LANE
            t_ref[n, k : k + 1, :] = b_ref[:, at : at + LANE]
    rows = o_ref.shape[0]
    o_ref[...] = jnp.concatenate([t_ref[0, 0:rows, :], t_ref[1, 0:rows, :]], axis=1).astype(BF)


def box_call(kernel, shape, kind, name, *args):
    return pl.pallas_call(
        kernel,
        in_specs=[VM] * len(args),
        out_specs=VM,
        out_shape=shape_of(shape, kind),
        scratch_shapes=[
            pltpu.VMEM((2, 368, LANE), F32),
            pltpu.VMEM((40 * 64, LANE), F32),
            pltpu.VMEM((2, LANE, LANE), F32),
        ],
        compiler_params=pltpu.CompilerParams(vmem_limit_bytes=VMEM_LIMIT),
        name=name,
    )(*args)


def heads_call(rows, cols, scal, feats, masks, labels, box_target, full, tb, head, wb):
    canvases = feats.shape[0]
    own = rows * cols
    total = own + 2 * HALO * cols
    spread = jnp.repeat(jnp.eye(SLOT, 9, dtype=BF), LANE, axis=1)

    def per(shape):
        return pl.BlockSpec((1,) + shape, lambda c: (c,) + (0,) * len(shape))

    return pl.pallas_call(
        functools.partial(head_kernel, cols, rows),
        grid=(canvases,),
        in_specs=[
            pl.BlockSpec(memory_space=pltpu.SMEM),
            per((3, total, C)),
            per((SLOT, total)),
            per((SLOT, total)),
            per((4, SLOT, total)),
            whole(spread.shape),
            pl.BlockSpec(memory_space=pl.ANY),
            whole(tb.shape),
            pl.BlockSpec(memory_space=pl.ANY),
            whole(wb.shape),
        ],
        out_specs=[
            pl.BlockSpec(memory_space=pl.ANY),
            pl.BlockSpec(memory_space=pl.ANY),
            whole((9 * BOX_ROWS, C)),
            whole((1, 2 * C)),
            per((2, own, LANE)),
            whole((16, 256)),
        ],
        out_shape=[
            shape_of((9 * C, WIDE), BF),
            shape_of((18 * C, C), BF),
            shape_of((9 * BOX_ROWS, C)),
            shape_of((1, 2 * C)),
            shape_of((canvases, 2, own, LANE)),
            shape_of((16, 256)),
        ],
        scratch_shapes=[
            pltpu.VMEM((9, total, LANE), BF),
            pltpu.VMEM((total - 2 * cols, 2 * C), F32),
            pltpu.VMEM((total, C), BF),
            pltpu.VMEM((WIDE, own + 512), BF),
            pltpu.VMEM((own + 512, WIDE), BF),
            pltpu.VMEM((own + 256, 2 * C), BF),
            pltpu.VMEM((9 * C, 2 * C), BF),
            pltpu.VMEM((WIDE, 9 * C), BF),
            pltpu.VMEM((WIDE, 9 * C), F32),
            pltpu.VMEM((2 * C, 9 * C), F32),
            pltpu.SemaphoreType.DMA((3,)),
        ],
        compiler_params=pltpu.CompilerParams(vmem_limit_bytes=VMEM_LIMIT),
        name="heads",
    )(scal, feats, masks, labels, box_target, spread, full, tb, head, wb)


def place():
    img = lax.axis_index("img")
    cls = lax.axis_index("cls")
    return img // 2, img % 2, cls // 2, cls % 2


def target(z, y, x, c):
    return (z * 2 + y, x * 2 + c)


def owner(z, y, x, c):
    return ((z * 2 + y) * 2 + x) * 2 + c


def enter(peers):
    barrier = pltpu.get_barrier_semaphore()
    for peer in peers:
        pl.semaphore_signal(barrier, inc=1, device_id=peer, device_id_type=MESH)
    pl.semaphore_wait(barrier, len(peers))


class Mail:
    def __init__(self, send_sems, recv_sems):
        self.send_sems, self.recv_sems, self.used, self.sent = send_sems, recv_sems, 0, []

    def push(self, source, landing, peer):
        copy = pltpu.make_async_remote_copy(
            src_ref=source,
            dst_ref=landing,
            send_sem=self.send_sems.at[self.used],
            recv_sem=self.recv_sems.at[self.used],
            device_id=peer,
            device_id_type=MESH,
        )
        self.used += 1
        copy.start()
        self.sent.append(copy)
        return copy

    def close(self):
        for copy in self.sent:
            copy.wait_send()


def window_row(index, shard):
    return pl.multiple_of((index * shard + LEAD * C) // (16 * C) * 16, 16)


def gather_kernel(shard, s_ref, k_ref, n_ref, r_ref, full_ref, head_ref, all_ref, first_ref, last_ref, rim_ref, count_ref, sh_ref, kx_ref, send_sems, recv_sems):
    z, y, x, c = place()
    block = k_ref.shape[0]
    win = s_ref.shape[0]
    others = [(k, j) for k in range(4) for j in range(2) if k or j]
    ring = [((z + k) % 4, (y + j) % 2) for k, j in others]
    line = [(z * 2 + y, (x * 2 + c + step) % 4) for step in (1, 3)]
    enter([target(zz, yy, x, c) for zz, yy in ring] + [target(z, y, 1 - x, c), target(z, y, x, 1 - c)] + line)
    mail = Mail(send_sems, recv_sems)
    me = owner(z, y, x, c)

    def rows(zz, yy):
        return pl.ds(pl.multiple_of((zz * 2 + yy) * block, 16), block)

    def lanes(cc):
        return pl.ds(pl.multiple_of(cc * HALF, LANE), HALF)

    got_kx = mail.push(k_ref, kx_ref, target(z, y, 1 - x, c))
    counts = [mail.push(n_ref, count_ref.at[z * 2 + y], target(zz, yy, x, c)) for zz, yy in ring]
    slot = sh_ref.at[me]
    got_z = [mail.push(s_ref, slot, target((z + k) % 4, y, x, c)) for k in range(1, 4)]
    got_y = [mail.push(s_ref, slot, target(z, 1 - y, x, c))]
    got_x = [mail.push(s_ref, slot, target(z, y, 1 - x, c))]
    got_c = [mail.push(s_ref, slot, target(z, y, x, 1 - c))]
    rims = [mail.push(r_ref.at[n], rim_ref.at[n], line[n]) for n in range(2)]
    count_ref[z * 2 + y] = n_ref[...]
    sh_ref[me] = s_ref[...]

    got_kx.wait_recv()
    mine = head_ref.at[rows(z, y), lanes(c)]
    head_ref[rows(z, y), lanes(c)] = k_ref[...] + kx_ref[...]
    got_kz = [mail.push(mine, mine, target((z + k) % 4, y, x, c)) for k in range(1, 4)]
    got_ky = [mail.push(mine, mine, target(z, 1 - y, x, c))]
    got_kc = [mail.push(mine, mine, target(z, y, x, 1 - c))]

    for k in range(1, 4):
        got_z[k - 1].wait_recv()
        slot = sh_ref.at[owner((z + 4 - k) % 4, y, x, c)]
        got_y.append(mail.push(slot, slot, target(z, 1 - y, x, c)))
        got_x.append(mail.push(slot, slot, target(z, y, 1 - x, c)))
        got_c.append(mail.push(slot, slot, target(z, y, x, 1 - c)))
    for k in range(1, 4):
        got_kz[k - 1].wait_recv()
        part = head_ref.at[rows((z + 4 - k) % 4, y), lanes(c)]
        got_ky.append(mail.push(part, part, target(z, 1 - y, x, c)))
        got_kc.append(mail.push(part, part, target(z, y, x, 1 - c)))
    for k in range(4):
        got_y[k].wait_recv()
        slot = sh_ref.at[owner((z + 4 - k) % 4, 1 - y, x, c)]
        got_x.append(mail.push(slot, slot, target(z, y, 1 - x, c)))
        got_c.append(mail.push(slot, slot, target(z, y, x, 1 - c)))
    for k in range(4):
        got_ky[k].wait_recv()
        part = head_ref.at[rows((z + 4 - k) % 4, 1 - y), lanes(c)]
        got_kc.append(mail.push(part, part, target(z, y, x, 1 - c)))
    for k in range(8):
        got_x[k].wait_recv()
        slot = sh_ref.at[owner((z + 4 - k % 4) % 4, (y + k // 4) % 2, 1 - x, c)]
        got_c.append(mail.push(slot, slot, target(z, y, x, 1 - c)))
    for copy in got_c + got_kc + counts + rims:
        copy.wait_recv()
    all_ref[...] = jnp.sum(count_ref[...], axis=0)
    full_ref[...] = jnp.zeros_like(full_ref)

    def merge(d, carry):
        full_ref[pl.ds(window_row(d, shard), win), :] += sh_ref[d]
        return carry

    lax.fori_loop(0, 32, merge, 0)
    first_ref[...] = full_ref[0:TOWER_ROW, :]
    last_ref[...] = full_ref[TAIL_ROW:FULL_ROWS, :]
    mail.close()


def scatter_kernel(
    shard, head_ref, tower_ref, tail_ref, k_ref, n_ref, s_out, k_out, n_out,
    full_ref, sc_ref, sx_ref, sy_ref, sz_ref, kc_ref, ky_ref, kz_ref, kx_ref, mine_ref, peer_ref, far_ref, nz_ref, send_sems, recv_sems,
):
    z, y, x, c = place()
    block = kx_ref.shape[1]
    win = s_out.shape[0]
    enter([target((z + k) % 4, y, x, c) for k in range(1, 4)] + [target(z, 1 - y, x, c), target(z, y, 1 - x, c), target(z, y, x, 1 - c)])
    mail = Mail(send_sems, recv_sems)

    def rows(zz, yy):
        return pl.ds(pl.multiple_of((zz * 2 + yy) * block, 16), block)

    def lanes(cc):
        return pl.ds(pl.multiple_of(cc * HALF, LANE), HALF)

    def window(zz, yy, xx, cc):
        return pl.ds(window_row(owner(zz, yy, xx, cc), shard), win)

    mine_ref[0] = n_ref[...]
    sum_c = mail.push(mine_ref.at[0], peer_ref.at[0], target(z, y, x, 1 - c))
    spots = [(j, k) for j in (1, 0) for k in (1, 2, 3, 0)]
    got_kc = []
    for n, (j, k) in enumerate(spots):
        part = k_ref.at[rows((z + k) % 4, (y + j) % 2), lanes(1 - c)]
        got_kc.append(mail.push(part, kc_ref.at[n], target(z, y, x, 1 - c)))
    full_ref[0:TOWER_ROW, :] = head_ref[...]
    full_ref[TOWER_ROW:TAIL_ROW, :] = tower_ref[...]
    full_ref[TAIL_ROW:FULL_ROWS, :] = tail_ref[...]
    got_c = []
    for i in (1, 0):
        for n, (j, k) in enumerate(spots):
            part = full_ref.at[window((z + k) % 4, (y + j) % 2, (x + i) % 2, 1 - c), :]
            got_c.append(mail.push(part, sc_ref.at[(1 - i) * 8 + n], target(z, y, x, 1 - c)))

    sum_c.wait_recv()
    mine_ref[1] = mine_ref[0] + peer_ref[0]
    sum_x = mail.push(mine_ref.at[1], peer_ref.at[1], target(z, y, 1 - x, c))

    got_ky = []
    for n, (j, k) in enumerate(spots):
        got_kc[n].wait_recv()
        kc_ref[n] = kc_ref[n] + k_ref[rows((z + k) % 4, (y + j) % 2), lanes(c)]
        if j == 1:
            got_ky.append(mail.push(kc_ref.at[n], ky_ref.at[n], target(z, 1 - y, x, c)))
    got_x = []
    for n, (j, k) in enumerate(spots):
        got_c[n].wait_recv()
        sc_ref[n] = sc_ref[n] + full_ref[window((z + k) % 4, (y + j) % 2, 1 - x, c), :]
        got_x.append(mail.push(sc_ref.at[n], sx_ref.at[n], target(z, y, 1 - x, c)))

    sum_x.wait_recv()
    mine_ref[2] = mine_ref[1] + peer_ref[1]
    sum_y = mail.push(mine_ref.at[2], peer_ref.at[2], target(z, 1 - y, x, c))

    got_kz = []
    for n in range(4):
        got_ky[n].wait_recv()
        kc_ref[4 + n] = kc_ref[4 + n] + ky_ref[n]
        if n < 3:
            got_kz.append(mail.push(kc_ref.at[4 + n], kz_ref.at[n], target((z + n + 1) % 4, y, x, c)))
    got_y = []
    for n, (j, k) in enumerate(spots):
        got_c[8 + n].wait_recv()
        got_x[n].wait_recv()
        total = sc_ref[8 + n].astype(F32) + full_ref[window((z + k) % 4, (y + j) % 2, x, c), :].astype(F32)
        sc_ref[8 + n] = (total + sx_ref[n].astype(F32)).astype(BF)
        if j == 1:
            got_y.append(mail.push(sc_ref.at[8 + n], sy_ref.at[n], target(z, 1 - y, x, c)))

    sum_y.wait_recv()
    mine_ref[3] = mine_ref[2] + peer_ref[2]
    nz_ref[z] = mine_ref[3]
    sum_z = [mail.push(mine_ref.at[3], nz_ref.at[z], target((z + k) % 4, y, x, c)) for k in range(1, 4)]

    total = kc_ref[7].astype(F32)
    for n in range(3):
        got_kz[n].wait_recv()
        total += kz_ref[n].astype(F32)
    kx_ref[0] = total.astype(BF)
    got_kx = mail.push(kx_ref.at[0], kx_ref.at[1], target(z, y, 1 - x, c))
    got_z = []
    for n in range(4):
        got_y[n].wait_recv()
        sc_ref[12 + n] = sc_ref[12 + n] + sy_ref[n]
        if n < 3:
            got_z.append(mail.push(sc_ref.at[12 + n], sz_ref.at[n], target((z + n + 1) % 4, y, x, c)))
    total = sc_ref[15].astype(F32)
    for n in range(3):
        got_z[n].wait_recv()
        total += sz_ref[n].astype(F32)
    s_out[...] = total
    for copy in sum_z:
        copy.wait_recv()
    n_out[...] = (nz_ref[0] + nz_ref[1]) + (nz_ref[2] + nz_ref[3])
    got_kx.wait_recv()
    k_out[...] = kx_ref[0].astype(F32) + kx_ref[1].astype(F32)
    mail.close()


def fast_mesh(img_parts, cls_parts, class_rows):
    return img_parts == 8 and cls_parts == 4 and class_rows % 16 == 0


def flat_place(index, shard):
    return (index * shard + LEAD * C) % (16 * C)


def gather_all(shared_params, class_params, count, edges):
    img, cls = lax.axis_index("img"), lax.axis_index("cls")
    img_parts, cls_parts = lax.axis_size("img"), lax.axis_size("cls")
    shard = shared_params.shape[0]
    block, part = class_params.shape
    if not fast_mesh(img_parts, cls_parts, block):
        flat = lax.all_gather(shared_params.astype(BF), ("img", "cls"), axis=0, tiled=True)
        full = jnp.pad(flat, (LEAD * C, FULL_ROWS * C - LEAD * C - flat.shape[0])).reshape(FULL_ROWS, C)
        head = lax.all_gather(class_params.astype(BF), ("img", "cls"), axis=0)
        head = head.reshape(img_parts, cls_parts, block, part).transpose(0, 2, 1, 3).reshape(-1, CLS_OUT)
        pieces = []
        for half in range(2):
            pieces += [head[:, 180 * half : 180 * half + 180], head[:, 360 + 180 * half : 540 + 180 * half]]
            pieces.append(jnp.zeros((head.shape[0], HALF - 360), BF))
        ways = [[(i, (i + step) % cls_parts) for i in range(cls_parts)] for step in (1, cls_parts - 1)]
        rim = jnp.stack([lax.ppermute(edges[n], "cls", ways[n]) for n in range(2)])
        return full, full[:TOWER_ROW], full[TAIL_ROW:], jnp.concatenate(pieces, axis=1), lax.psum(count, "img"), rim
    rows = -(-(shard + 16 * C) // (16 * C)) * 16
    window = lax.dynamic_update_slice(
        jnp.zeros((rows * C,), BF), shared_params.astype(BF), (flat_place(img * cls_parts + cls, shard),)
    ).reshape(rows, C)
    wide = jnp.pad(class_params.astype(BF), ((0, 0), (part, HALF - part)))
    wide = lax.dynamic_slice_in_dim(
        jnp.pad(wide, ((0, 0), (0, part))), jnp.where(cls // 2 == 0, part, 0), HALF, 1
    )
    number = jnp.broadcast_to(count, (8, LANE))
    full, head, counts, first, last, rim = pl.pallas_call(
        functools.partial(gather_kernel, shard),
        in_specs=[VM] * 4,
        out_specs=[VM] * 6,
        out_shape=[
            shape_of((FULL_ROWS, C), BF),
            shape_of((img_parts * block, 2 * HALF), BF),
            shape_of((8, LANE)),
            shape_of((TOWER_ROW, C), BF),
            shape_of((FULL_ROWS - TAIL_ROW, C), BF),
            shape_of(edges.shape, BF),
        ],
        scratch_shapes=[
            pltpu.VMEM((img_parts, 8, LANE), F32),
            pltpu.VMEM((img_parts * cls_parts, rows, C), BF),
            pltpu.VMEM((block, HALF), BF),
            pltpu.SemaphoreType.DMA((56,)),
            pltpu.SemaphoreType.DMA((56,)),
        ],
        compiler_params=pltpu.CompilerParams(collective_id=0, has_side_effects=True, vmem_limit_bytes=VMEM_LIMIT),
        name="gather",
    )(window, wide, number, edges)
    return full, first, last, head, counts[0, 0], rim


def scatter_all(head, tower, tail, class_grad, sums, shard, block, part):
    img, cls = lax.axis_index("img"), lax.axis_index("cls")
    img_parts, cls_parts = lax.axis_size("img"), lax.axis_size("cls")
    if not fast_mesh(img_parts, cls_parts, block):
        flat = jnp.concatenate([head, tower, tail], axis=0).reshape(-1)
        flat = flat[LEAD * C : LEAD * C + shard * img_parts * cls_parts].astype(F32)
        shared = lax.psum_scatter(flat, ("img", "cls"), scatter_dimension=0, tiled=True)
        pieces = [class_grad[:, at : at + 180] for at in (0, HALF, 180, HALF + 180)]
        whole_grad = lax.psum_scatter(
            jnp.concatenate(pieces, axis=1).astype(F32), "img", scatter_dimension=0, tiled=True
        )
        return shared, lax.psum_scatter(whole_grad, "cls", scatter_dimension=1, tiled=True), lax.psum(sums, ("img", "cls"))
    rows = -(-(shard + 16 * C) // (16 * C)) * 16
    window, wide, sums = pl.pallas_call(
        functools.partial(scatter_kernel, shard),
        in_specs=[VM] * 5,
        out_specs=[VM] * 3,
        out_shape=[shape_of((rows, C)), shape_of((block, HALF)), shape_of(sums.shape)],
        scratch_shapes=[
            pltpu.VMEM((FULL_ROWS, C), BF),
            pltpu.VMEM((16, rows, C), BF),
            pltpu.VMEM((8, rows, C), BF),
            pltpu.VMEM((4, rows, C), BF),
            pltpu.VMEM((3, rows, C), BF),
            pltpu.VMEM((8, block, HALF), BF),
            pltpu.VMEM((4, block, HALF), BF),
            pltpu.VMEM((3, block, HALF), BF),
            pltpu.VMEM((2, block, HALF), BF),
            pltpu.VMEM((4,) + sums.shape, F32),
            pltpu.VMEM((3,) + sums.shape, F32),
            pltpu.VMEM((8, LANE), F32),
            pltpu.VMEM((4,) + sums.shape, F32),
            pltpu.SemaphoreType.DMA((53,)),
            pltpu.SemaphoreType.DMA((53,)),
        ],
        compiler_params=pltpu.CompilerParams(collective_id=1, has_side_effects=True, vmem_limit_bytes=VMEM_LIMIT),
        name="scatter",
    )(head, tower, tail, class_grad, sums)
    flat = lax.dynamic_slice_in_dim(window.reshape(-1), flat_place(img * cls_parts + cls, shard), shard)
    grad = lax.dynamic_slice_in_dim(wide, jnp.where(cls // 2 == 0, 0, part), part, 1)
    grad = lax.optimization_barrier(grad.T).T
    return flat, grad, sums


def column_plan():
    plan = []
    for half in range(2):
        for group in range(2):
            column, row, end = 360 * group + 180 * half, HALF * half + 180 * group, 360 * group + 180 * half + 180
            while column < end:
                count = min(end, (column // CLASSES + 1) * CLASSES) - column
                plan.append((row, count, column // CLASSES, column % CLASSES))
                column, row = column + count, row + count
        plan.append((HALF * half + 360, HALF - 360, -1, 0))
    return plan


def adamw_update(weight, first, second, grad):
    first_new = MOMENT_ONE * first + (1.0 - MOMENT_ONE) * grad
    second_new = MOMENT_TWO * second + (1.0 - MOMENT_TWO) * grad * grad
    first_hat = first_new / (1.0 - MOMENT_ONE**STEP)
    second_hat = second_new / (1.0 - MOMENT_TWO**STEP)
    weight_new = weight - RATE * (first_hat / (jnp.sqrt(second_hat) + EPSILON) + DECAY * weight)
    return (weight_new, first_new, second_new)


def valid_positives(boxes, match, full_rows, cols):
    place = jnp.arange(full_rows * cols, dtype=jnp.int32)
    row, col = place // cols, place % cols
    inside = jnp.zeros((boxes.shape[0], full_rows * cols), bool)
    for k in range(boxes.shape[1]):
        edge = boxes[:, k, :, None]
        inside |= (row >= edge[:, 0]) & (row < edge[:, 2]) & (col >= edge[:, 1]) & (col < edge[:, 3])
    return ((match >= 0) & inside[:, None]).astype(F32)


def cell_data(boxes, match, gt_labels, gt_deltas, first_row, rows, cols):
    full_rows = match.shape[2] // cols
    total = (rows + 2 * HALO) * cols
    place = jnp.arange(total, dtype=jnp.int32)[None]
    row = place // cols + (first_row - HALO)
    col = place % cols

    def crop(r, j):
        found = jnp.full((boxes.shape[0], total), -1, jnp.int32)
        for k in range(boxes.shape[1]):
            edge = boxes[:, k, :, None]
            inside = (r >= edge[:, 0]) & (r < edge[:, 2]) & (j >= edge[:, 1]) & (j < edge[:, 3])
            found = jnp.where(inside, k, found)
        return jnp.where((r >= 0) & (r < full_rows) & (j >= 0) & (j < cols), found, -1)

    centre = crop(row, col)
    valid = centre >= 0
    masks = jnp.stack([(crop(row + di, col + dj) == centre) & valid for di, dj in TAPS], axis=1)
    masks = jnp.pad(masks.astype(BF), ((0, 0), (0, SLOT - 9), (0, 0)))
    edge = HALO * cols
    near = jnp.pad(match, ((0, 0), (0, 0), (edge, edge)), constant_values=-2)
    near = lax.dynamic_slice_in_dim(near, first_row * cols, total, 2)
    near = jnp.where(valid[:, None], near, -2)
    near = jnp.pad(near, ((0, 0), (0, SLOT - 9), (0, 0)), constant_values=-2)
    labels = near
    targets = jnp.zeros((near.shape[0], 4) + near.shape[1:], F32)
    for g in range(gt_labels.shape[1]):
        labels = jnp.where(near == g, gt_labels[:, g, None, None], labels)
        targets = jnp.where((near == g)[:, None], gt_deltas[:, g, :, None, None], targets)
    return masks, labels.astype(F32), targets


def local(patches, boxes, match, gt_labels, gt_deltas, ema_old, shared_params, shared_m, shared_v, class_params, class_m, class_v):
    cls_rank = lax.axis_index("cls")
    canvases, rows, width = patches.shape
    cols = width // PATCH
    masks, labels, targets = cell_data(boxes, match, gt_labels, gt_deltas, cls_rank * rows, rows, cols)
    full_rows = match.shape[2] // cols
    count = jnp.sum(valid_positives(boxes, match, full_rows, cols))
    edges = jnp.stack([patches[:, rows - HALO :], patches[:, :HALO]]).reshape(2, canvases * HALO, width)
    edges = jnp.concatenate([edges[..., : width // 2], edges[..., width // 2 :]], axis=1)
    full, first, last, head, positives, rim = gather_all(shared_params, class_params, count, edges)
    norm = jnp.maximum(positives, 1.0)
    ema_new = EMA_KEEP * ema_old + (1.0 - EMA_KEEP) * norm
    tb = last[0:2].reshape(1, 2 * C).astype(F32)
    wb = box_call(box_in_kernel, (9 * BOX_ROWS, C), BF, "box_in", last)
    stem_pre, stem_out, feats, lat_w = stem_forward(patches, rim, first)
    scal = jnp.stack([1.0 / ema_new, 1.0 / norm])
    class_grad, tower_grad, dwb, db, feature_grad, sums = heads_call(
        rows, cols, scal, feats, masks, labels, targets, full, tb, head, wb
    )
    first_grad = stem_backward(patches, feature_grad, stem_out, stem_pre, lat_w)
    last_grad = box_call(box_out_kernel, last.shape, BF, "box_out", dwb, db)
    shared_grad, class_grad, sums = scatter_all(
        first_grad, tower_grad, last_grad, class_grad, sums, shared_params.shape[0], *class_params.shape
    )
    loss = jnp.sum(sums[0:8]) / ema_new + jnp.sum(sums[8:16]) / norm
    return (
        loss,
        ema_new,
        *adamw_update(shared_params, shared_m, shared_v, shared_grad),
        *adamw_update(class_params, class_m, class_v, class_grad),
    )


def solution(mesh):
    spread = P(("img", "cls"))
    block = P("img", "cls")
    return jax.shard_map(
        local,
        mesh=mesh,
        in_specs=(
            P("img", "cls", None),
            P("img", None, None),
            P("img", None, None),
            P("img", None),
            P("img", None, None),
            P(),
            spread,
            spread,
            spread,
            block,
            block,
            block,
        ),
        out_specs=(P(), P(), spread, spread, spread, block, block, block),
        check_vma=False,
    )
```

```python
import functools

import jax
import jax.numpy as jnp
from jax import lax
from jax.experimental import pallas as pl
from jax.experimental.pallas import tpu as pltpu
from jax.sharding import PartitionSpec as P

C = 256
CLASSES = 80
ANCH = 9
PATCH = 192
BOX_OUT = 36
CLS_OUT = ANCH * CLASSES
STEP = 5
GT = 16
HALO = 4
SLOT = 16
BOX_ROWS = 4 * SLOT
LANE = 128
WIDE = 768
GROUP = 16

PRIOR = -4.59511985013459
ALPHA = 0.25
HUBER = 1.0 / 9.0
EMA_KEEP = 0.9
RATE = 0.01
MOMENT_ONE = 0.5
MOMENT_TWO = 0.5
DECAY = 0.05
EPSILON = 1e-08

LENGTHS = [PATCH * C, C, C * C, C, 18 * C * C, 2 * C, 9 * C * BOX_OUT]
TOWER_AT = sum(LENGTHS[:4]) // C
LEAD = -TOWER_AT % 16
TOWER_ROW = TOWER_AT + LEAD
TAIL_ROW = TOWER_ROW + 18 * C
FULL_ROWS = -(-(LEAD + sum(LENGTHS) // C) // 16) * 16
HALF = 384
MESH = pl.DeviceIdType.MESH

BF = jnp.bfloat16
F32 = jnp.float32
TAPS = [(di, dj) for di in (-1, 0, 1) for dj in (-1, 0, 1)]
NN = (((1,), (0,)), ((), ()))
NT = (((1,), (1,)), ((), ()))
TN = (((0,), (0,)), ((), ()))
K0 = 0.7978845608028654
K1 = 0.044715


def mm(a, b, dims=NN):
    return lax.dot_general(a, b, dims, preferred_element_type=F32)


def gelu(x):
    return 0.5 * x * (1.0 + jnp.tanh(K0 * (x + K1 * x * x * x)))


def gelu_slope(x):
    square = x * x
    th = jnp.tanh(K0 * (x + K1 * x * square))
    return 0.5 * (1.0 + th) + (0.5 * K0) * x * (1.0 - th * th) * (1.0 + 3.0 * K1 * square)


def columns_of(x, pairs, width):
    return [x[:, width * k : width * (k + 1)] for k in range(pairs)]


def stem_kernel(pairs, cols, rows, x_ref, h_ref, head_ref, pre_ref, so_ref, f_ref, lw_ref, t_ref, w_ref, b_ref, lb_ref):
    step = pl.program_id(0)
    canvases = x_ref.shape[0]
    own_rows = canvases * rows
    total = (rows + 2 * HALO) * cols

    @pl.when(step == 0)
    def _():
        head = head_ref[...].astype(F32)
        w_ref[...] = jnp.zeros_like(w_ref)
        stem_w = head[LEAD : LEAD + PATCH].astype(BF)
        w_ref[:PATCH, :C] = stem_w
        w_ref[PATCH:, C:] = stem_w
        bias = head[LEAD + PATCH : LEAD + PATCH + 1]
        b_ref[...] = jnp.concatenate([bias, bias], axis=1)
        lw_ref[...] = head[LEAD + PATCH + 1 : TOWER_ROW - 1].astype(BF)
        lb_ref[...] = head[TOWER_ROW - 1 : TOWER_ROW]
        for c in range(canvases):
            for n in range(2):
                t_ref[c, n, 0:8, :] = jnp.zeros((8, LANE), F32)
                t_ref[c, n, 8 + total : 16 + total, :] = jnp.zeros((8, LANE), F32)

    x = x_ref[...].reshape(own_rows, x_ref.shape[2])
    own = columns_of(x, pairs, 2 * PATCH)
    half = pl.num_programs(0) // 2
    lanes = pl.ds(pl.multiple_of(step % half * x.shape[1], LANE), x.shape[1])
    many_rows = h_ref.shape[1] // 2
    near = [h_ref[n, :, lanes].astype(F32) for n in range(2)]
    near = [jnp.where(step < half, one[:many_rows], one[many_rows:]) for one in near]
    rim = columns_of(jnp.concatenate(near, axis=0).astype(BF), pairs, 2 * PATCH)
    pre = mm(jnp.concatenate(own + rim, axis=0), w_ref[...]) + b_ref[...]
    count = pairs * own_rows
    pre_ref[...] = pre[:count]
    out = gelu(pre).astype(BF)
    so_ref[...] = out[:count]
    for half in range(2):
        feat = mm(out[:, half * C : half * C + C], lw_ref[...]) + lb_ref[...]
        for k in range(pairs):
            j = step * 2 * pairs + 2 * k + half
            for c in range(canvases):
                at = k * own_rows + c * rows
                up_at = count + k * 2 * HALO * canvases + c * HALO
                down_at = up_at + HALO * canvases
                for n in range(2):
                    side = slice(n * LANE, n * LANE + LANE)
                    place = pl.ds(8 + HALO * cols + j, rows, stride=cols)
                    t_ref[c, n, place, :] = feat[at : at + rows, side]
                    place = pl.ds(8 + j, HALO, stride=cols)
                    t_ref[c, n, place, :] = feat[up_at : up_at + HALO, side]
                    place = pl.ds(8 + (HALO + rows) * cols + j, HALO, stride=cols)
                    t_ref[c, n, place, :] = feat[down_at : down_at + HALO, side]

    @pl.when(step == pl.num_programs(0) - 1)
    def _():
        piece = 4 * cols

        def move(i, carry):
            base = pl.multiple_of(i * piece, 16)
            for c in range(canvases):
                for n in range(2):
                    value = t_ref[c, n, pl.ds(base, piece + 16), :]
                    for k in range(3):
                        moved = value[7 + k : 7 + k + piece].astype(BF)
                        f_ref[c, k, pl.ds(base, piece), n * LANE : n * LANE + LANE] = moved
            return carry

        lax.fori_loop(0, total // piece, move, 0)


def stem_back_kernel(pairs, cols, rows, x_ref, fg_ref, so_ref, pre_ref, lw_ref, head_ref, sw_out, sb_out, lw_out, lb_out, h_ref):
    step = pl.program_id(0)
    canvases = x_ref.shape[0]

    @pl.when(step == 0)
    def _():
        sw_out[...] = jnp.zeros_like(sw_out)
        sb_out[...] = jnp.zeros_like(sb_out)
        lw_out[...] = jnp.zeros_like(lw_out)
        lb_out[...] = jnp.zeros_like(lb_out)

    x = x_ref[...].reshape(canvases * rows, x_ref.shape[2])
    own = jnp.concatenate(columns_of(x, pairs, 2 * PATCH), axis=0)
    low = []
    for half in range(2):
        parts = []
        for k in range(pairs):
            j = step * 2 * pairs + 2 * k + half
            for c in range(canvases):
                place = pl.ds(j, rows, stride=cols)
                parts.append(jnp.concatenate([fg_ref[c, n, place, :] for n in range(2)], axis=1))
        grad32 = jnp.concatenate(parts, axis=0)
        grad = grad32.astype(BF)
        cut = slice(half * C, half * C + C)
        lw_out[...] += mm(so_ref[:, cut], grad, TN)
        lb_out[...] += jnp.sum(grad32, axis=0, keepdims=True)
        back = mm(grad, lw_ref[...], NT) * gelu_slope(pre_ref[:, cut])
        back = back.astype(BF)
        sb_out[...] += jnp.sum(back.astype(F32), axis=0, keepdims=True)
        low.append(back)
    both = mm(own, jnp.concatenate(low, axis=1), TN)
    sw_out[...] += both[:PATCH, :C] + both[PATCH:, C:]

    @pl.when(step == pl.num_programs(0) - 1)
    def _():
        at = LEAD + PATCH
        h_ref[0:LEAD, :] = jnp.zeros((LEAD, C), F32)
        h_ref[LEAD:at, :] = sw_out[...]
        h_ref[at : at + 1, :] = sb_out[...]
        h_ref[at + 1 : TOWER_ROW - 1, :] = lw_out[...]
        h_ref[TOWER_ROW - 1 :, :] = lb_out[...]
        head_ref[...] = h_ref[...].astype(BF)


def aligned(value, multiple):
    return value if isinstance(value, int) else pl.multiple_of(value, multiple)


def many(mask, count):
    return jnp.concatenate([mask] * count, axis=1)


def weight_sums(canvas, cols, edge, own, grad, source, mx_ref, sum_ref):
    def go(x_ref):
        def triple(n, carry):
            at = pl.multiple_of(edge + cols * (n - 1), 16)
            for k in range(3):
                mask = mx_ref[n * 3 + k, edge : edge + own, :]
                x_ref[:, k * C : k * C + C] = source[k, pl.ds(at, own), :] * many(mask, 2)
            side = pl.ds(pl.multiple_of(n * 3 * C, C), 3 * C)
            sum_ref[:, side] = jnp.where(canvas > 0, sum_ref[:, side], 0.0) + mm(grad(), x_ref[...])
            return carry

        lax.fori_loop(0, 3, triple, 0)

    pl.run_scoped(go, pltpu.VMEM((own, 3 * C), BF))


def head_kernel(
    cols, rows, scal_ref, f_ref, mk_ref, lab_ref, btt_ref, e_ref, full_ref, tb_ref, head_ref, wb_ref,
    class_ref, tower_ref, dwb_ref, db_ref, fg_ref, sums_ref,
    mx_ref, pre_ref, bt_ref, lgt_ref, lgs_ref, g_ref, wt_ref, wct_ref, dwc_ref, dwt_ref, copy_sems,
):
    own = rows * cols
    edge = HALO * cols
    total = own + 2 * edge
    shift = [cols * di + dj for di, dj in TAPS]

    @pl.when(pl.program_id(0) == 0)
    def _():
        dwb_ref[...] = jnp.zeros_like(dwb_ref)
        db_ref[...] = jnp.zeros_like(db_ref)
        sums_ref[...] = jnp.zeros_like(sums_ref)
        def fetch(held_ref):
            copies = [pltpu.make_async_copy(head_ref, held_ref, copy_sems.at[2])]
            for n in range(2):
                rows_of = full_ref.at[TOWER_ROW + n * 9 * C : TOWER_ROW + (n + 1) * 9 * C, :]
                copies.append(pltpu.make_async_copy(rows_of, wt_ref.at[:, n * C : n * C + C], copy_sems.at[n]))
            for copy in copies:
                copy.start()
            copies[0].wait()

            def turn(t, carry):
                at = pl.multiple_of(t * C, C)
                wct_ref[:, pl.ds(at, C)] = held_ref[pl.ds(at, C), :].T
                return carry

            lax.fori_loop(0, 9, turn, 0)
            for copy in copies[1:]:
                copy.wait()

        pl.run_scoped(fetch, pltpu.VMEM((9 * C, WIDE), BF))

    def spread(i, carry):
        at = pl.multiple_of(i * 384, 128)
        wide = mm(mk_ref[0, :, pl.ds(at, 384)], e_ref[...], TN).astype(BF)
        for t in range(9):
            mx_ref[t, pl.ds(at, 384), :] = wide[:, t * LANE : (t + 1) * LANE]
        return carry

    lax.fori_loop(0, total // 384, spread, 0)

    def twice(mask):
        return jnp.concatenate([mask, mask], axis=1)

    def build(source, at, count, x_ref):
        for t, (di, dj) in enumerate(TAPS):
            value = source[dj + 1, pl.ds(pl.multiple_of(at + cols * di, 16), count), :]
            x_ref[:, t * C : (t + 1) * C] = value * twice(mx_ref[t, pl.ds(at, count), :])

    first_tower = cols
    tower_rows = total - 2 * cols
    first_logit = edge - 256
    logit_cells = own + 512
    first_g = edge - 128
    g_cells = own + 256

    def heads(ct32_ref, ct_ref):
        zero = jnp.zeros((cols + 8, C), F32)
        ct32_ref[0 : cols + 8, :] = zero
        ct32_ref[8 + total - cols : 16 + total, :] = zero
        zero = jnp.zeros((cols, C), BF)
        bt_ref[0:cols, :] = zero
        bt_ref[total - cols : total, :] = zero
        piece = tower_rows // 2

        def towers(x_ref):
            def tower(i, carry):
                row = pl.multiple_of(i * piece, 16)
                at = pl.multiple_of(first_tower + i * piece, 16)
                build(f_ref.at[0], at, piece, x_ref)
                pre = mm(x_ref[...], wt_ref[...]) + tb_ref[...]
                pre_ref[pl.ds(row, piece), :] = pre
                out = gelu(pre)
                ct32_ref[pl.ds(pl.multiple_of(8 + at, 8), piece), :] = out[:, :C]
                bt_ref[pl.ds(at, piece), :] = out[:, C:].astype(BF)
                return carry

            lax.fori_loop(0, 2, tower, 0)

        pl.run_scoped(towers, pltpu.VMEM((piece, 9 * C), BF))

        def move(i, carry):
            base = pl.multiple_of(i * edge, 16)
            value = ct32_ref[pl.ds(base, edge + 16), :]
            for k in range(3):
                ct_ref[k, pl.ds(base, edge), :] = value[7 + k : 7 + k + edge].astype(BF)
            return carry

        lax.fori_loop(0, total // edge, move, 0)
        def logits(xa_ref, la_ref):
            inv_ema = scal_ref[0]
            number = lax.broadcasted_iota(jnp.int32, (GROUP, 256), 0).astype(F32)
            lane = lax.broadcasted_iota(jnp.int32, (8, 256), 1)
            plan = column_plan()

            def ready(q, x_ref):
                build(ct_ref, pl.multiple_of(first_logit + q * 256, 128), 256, x_ref)

            def work(q, x_ref, l_ref):
                l_ref[...] = mm(wct_ref[...], x_ref[...], NT)

            def focal(q, l_ref):
                row = pl.multiple_of(q * 256, 128)
                at = pl.multiple_of(first_logit + row, 128)
                spot = lane + at
                mine = (spot >= edge) & (spot < edge + own)
                lines = [lab_ref[0, a : a + 1, pl.ds(at, 256)] for a in range(ANCH)]
                rest = [jnp.where(line > -1.5, 1.0 - ALPHA, 0.0) for line in lines]
                pulls = [line * inv_ema for line in rest]
                total_focal = jnp.zeros((8, 256), F32)
                for first in range(0, WIDE, GROUP):
                    value = l_ref[first : first + GROUP, :] + PRIOR
                    key = None
                    for begin, count, anchor, klass in plan:
                        if begin >= first + GROUP or begin + count <= first:
                            continue
                        if anchor < 0:
                            parts = [jnp.full((GROUP, 256), n, F32) for n in (-2.0, 0.0, 0.0)]
                        else:
                            parts = [lines[anchor] - float(klass - (begin - first)), rest[anchor], pulls[anchor]]
                            parts = [jnp.broadcast_to(part, (GROUP, 256)) for part in parts]
                        if key is None:
                            key, other, pull_other = parts
                        else:
                            later = number >= float(begin - first)
                            key = jnp.where(later, parts[0], key)
                            other = jnp.where(later, parts[1], other)
                            pull_other = jnp.where(later, parts[2], pull_other)
                    hit = key == number
                    side = jnp.where(hit, -value, value)
                    small = jnp.exp(-jnp.abs(side))
                    whole_one = 1.0 + small
                    ratio = pltpu.reciprocal(whole_one, approx=True)
                    ratio = ratio * (2.0 - whole_one * ratio)
                    part = small * ratio
                    up = side >= 0.0
                    prob = jnp.where(up, ratio, part)
                    miss = jnp.where(up, part, ratio)
                    tiny = small * (1.0 - 0.5 * small)
                    cross = jnp.maximum(side, 0.0) + jnp.where(small < 0.001, tiny, jnp.log(whole_one))
                    square = prob * prob
                    value = square * cross * jnp.where(hit, ALPHA, other)
                    pull = square * (2.0 * miss * cross + prob) * jnp.where(hit, -ALPHA * inv_ema, pull_other)
                    l_ref[first : first + GROUP, :] = pull
                    lgt_ref[first : first + GROUP, pl.ds(row, 256)] = pull.astype(BF)
                    total_focal += jnp.sum(value.reshape(GROUP // 8, 8, 256), axis=0)
                sums_ref[0:8, :] += jnp.where(mine, total_focal, 0.0)
                lgs_ref[pl.ds(row, 256), :] = l_ref[...].T.astype(BF)

            def logits_of(q, carry):
                ready(q, xa_ref)
                work(q, xa_ref, la_ref)
                focal(q, la_ref)
                return carry

            lax.fori_loop(0, logit_cells // 256, logits_of, 0)

        pl.run_scoped(logits, pltpu.VMEM((256, 9 * C), BF), pltpu.VMEM((WIDE, 256), F32))
        weight_sums(pl.program_id(0), cols, edge, own, lambda: lgt_ref[:, 256 : 256 + own], ct_ref, mx_ref, dwc_ref)

    pl.run_scoped(heads, pltpu.VMEM((total + 16, C), F32), pltpu.VMEM((3, total, C), BF))

    def box_forward(gg_ref, y_ref):
        inv_norm = scal_ref[1]

        def outer(i, carry):
            at = pl.multiple_of(i * 768, 128)
            y_ref[:, pl.ds(at, 768)] = mm(wb_ref[...], bt_ref[pl.ds(at, 768), :], NT)
            return carry

        lax.fori_loop(0, total // 768, outer, 0)
        lane = lax.broadcasted_iota(jnp.int32, (SLOT, total), 1)
        mine = (lane >= edge) & (lane < edge + own)

        def guess(m, carry):
            acc = jnp.zeros((SLOT, total), F32)
            for t in range(9):
                value = y_ref[pl.ds(pl.multiple_of(t * BOX_ROWS + m * SLOT, 8), SLOT), :]
                moved = pltpu.roll(value, (-shift[t]) % total, 1)
                acc += moved * mk_ref[0, t : t + 1, :].astype(F32)
            differ = acc - btt_ref[0, m]
            positive = lab_ref[0] >= 0.0
            size = jnp.abs(differ)
            loss = jnp.where(size < HUBER, 0.5 * differ * differ / HUBER, size - 0.5 * HUBER)
            loss = jnp.where(positive & mine, loss, 0.0)
            part = loss[:, 0:256]
            for k in range(1, total // 256):
                part += loss[:, k * 256 : (k + 1) * 256]
            sums_ref[8:16, :] += part[0:8] + part[8:16]
            pull = jnp.minimum(jnp.maximum(differ / HUBER, -1.0), 1.0) * inv_norm
            pull = jnp.where(positive, pull, 0.0)
            gg_ref[pl.ds(pl.multiple_of(m * SLOT, 8), SLOT), :] = pull
            return carry

        lax.fori_loop(0, 4, guess, 0)

    def box_back(gg_ref, xg_ref):
        for t in range(9):
            moved = pltpu.roll(gg_ref[...], shift[t] % total, 1)
            xg_ref[t * BOX_ROWS : (t + 1) * BOX_ROWS, :] = (moved * mk_ref[0, 8 - t : 9 - t, :].astype(F32)).astype(BF)
        dwb_ref[...] += mm(xg_ref[:, edge : edge + own], bt_ref[edge : edge + own, :])

        def into(q, carry):
            row = pl.multiple_of(q * 256, 128)
            grad = mm(xg_ref[:, pl.ds(pl.multiple_of(first_g + row, 128), 256)], wb_ref[...], TN)
            pre = pre_ref[pl.ds(pl.multiple_of(first_g - first_tower + row, 16), 256), C:]
            g_ref[pl.ds(row, 256), C:] = (grad * gelu_slope(pre)).astype(BF)
            return carry

        lax.fori_loop(0, g_cells // 256, into, 0)

    def boxes(gg_ref):
        pl.run_scoped(functools.partial(box_forward, gg_ref), pltpu.VMEM((9 * BOX_ROWS, total), F32))
        pl.run_scoped(functools.partial(box_back, gg_ref), pltpu.VMEM((9 * BOX_ROWS, total), BF))

    pl.run_scoped(boxes, pltpu.VMEM((BOX_ROWS, total), F32))

    def class_back(z_ref):
        z_ref[:, 0:8, :] = jnp.zeros((3, 8, C), F32)
        z_ref[:, 8 + g_cells : 16 + g_cells, :] = jnp.zeros((3, 8, C), F32)
        piece = g_cells // 2

        def multiply(i, carry):
            row = pl.multiple_of(i * piece, 16)
            for k in range(3):
                acc = jnp.zeros((piece, C), F32)
                for r in range(3):
                    t = r * 3 + k
                    source = row + first_g - cols * (r - 1)
                    mask = mx_ref[t, pl.ds(pl.multiple_of(source, 16), piece), :]
                    value = lgs_ref[pl.ds(pl.multiple_of(source - first_logit, 16), piece), :]
                    value = value * jnp.concatenate([mask] * (WIDE // LANE), axis=1)
                    acc += mm(value, wct_ref[:, t * C : t * C + C])
                z_ref[k, pl.ds(pl.multiple_of(8 + row, 8), piece), :] = acc
            return carry

        lax.fori_loop(0, 2, multiply, 0)

        def collect(q, carry):
            row = pl.multiple_of(q * 256, 128)
            grad = z_ref[1, pl.ds(pl.multiple_of(8 + row, 8), 256), :]
            grad += z_ref[0, pl.ds(row, 272), :][9:265] + z_ref[2, pl.ds(row, 272), :][7:263]
            pre = pre_ref[pl.ds(pl.multiple_of(first_g - first_tower + row, 16), 256), :C]
            g_ref[pl.ds(row, 256), :C] = (grad * gelu_slope(pre)).astype(BF)
            return carry

        lax.fori_loop(0, g_cells // 256, collect, 0)

    pl.run_scoped(class_back, pltpu.VMEM((3, g_cells + 16, C), F32))

    def tower_back(z_ref, gt_ref):
        def flip(q, carry):
            row = pl.multiple_of(q * 256, 128)
            part = g_ref[pl.ds(pl.multiple_of(edge - first_g + row, 16), 256), :].astype(F32)
            gt_ref[:, pl.ds(row, 256)] = part.T.astype(BF)
            db_ref[...] += jnp.sum(part, axis=0, keepdims=True)
            return carry

        lax.fori_loop(0, own // 256, flip, 0)
        weight_sums(pl.program_id(0), cols, edge, own, lambda: gt_ref[...], f_ref.at[0], mx_ref, dwt_ref)
        first_z = edge - 16
        piece = (own + 32) // 2

        def multiply(i, carry):
            row = pl.multiple_of(i * piece, 16)
            for k in range(3):
                acc = jnp.zeros((piece, C), F32)
                for r in range(3):
                    t = r * 3 + k
                    source = row + first_z - cols * (r - 1)
                    mask = mx_ref[t, pl.ds(pl.multiple_of(source, 16), piece), :]
                    value = g_ref[pl.ds(pl.multiple_of(source - first_g, 16), piece), :]
                    value = value * jnp.concatenate([mask] * (2 * C // LANE), axis=1)
                    acc += mm(value, wt_ref[t * C : t * C + C, :], NT)
                z_ref[k, pl.ds(row, piece), :] = acc
            return carry

        lax.fori_loop(0, 2, multiply, 0)

        def collect(q, carry):
            row = pl.multiple_of(q * 256, 128)
            base = pl.multiple_of(row + 8, 8)
            grad = z_ref[1, pl.ds(pl.multiple_of(16 + row, 8), 256), :]
            grad += z_ref[0, pl.ds(base, 272), :][9:265] + z_ref[2, pl.ds(base, 272), :][7:263]
            grad = grad.astype(BF).astype(F32)
            for n in range(2):
                fg_ref[0, n, pl.ds(row, 256), :] = grad[:, n * LANE : n * LANE + LANE]
            return carry

        lax.fori_loop(0, own // 256, collect, 0)

    pl.run_scoped(
        tower_back,
        pltpu.VMEM((3, own + 32, C), F32),
        pltpu.VMEM((2 * C, own), BF),
    )

    @pl.when(pl.program_id(0) == pl.num_programs(0) - 1)
    def _():
        def deliver(class_held, tower_held):
            def turn(t, carry):
                at = pl.multiple_of(t * C, C)
                tower_held[pl.ds(at, C), :] = dwt_ref[0:C, pl.ds(at, C)].astype(BF).T
                tower_held[pl.ds(pl.multiple_of(9 * C + at, C), C), :] = dwt_ref[C:, pl.ds(at, C)].astype(BF).T
                class_held[pl.ds(at, C), :] = dwc_ref[:, pl.ds(at, C)].astype(BF).T
                return carry

            lax.fori_loop(0, 9, turn, 0)
            copies = [
                pltpu.make_async_copy(class_held, class_ref, copy_sems.at[0]),
                pltpu.make_async_copy(tower_held, tower_ref, copy_sems.at[1]),
            ]
            for copy in copies:
                copy.start()
            for copy in copies:
                copy.wait()

        pl.run_scoped(deliver, pltpu.VMEM((9 * C, WIDE), BF), pltpu.VMEM((18 * C, C), BF))


def whole(shape):
    return pl.BlockSpec(shape, lambda *_: (0,) * len(shape))


def shape_of(shape, dtype=F32):
    return jax.ShapeDtypeStruct(shape, dtype)


VM = pl.BlockSpec(memory_space=pltpu.VMEM)
VMEM_LIMIT = 63 * 1024 * 1024


def stem_forward(patches, rim, head):
    canvases, rows, width = patches.shape
    cols = width // PATCH
    pairs = 12
    steps = cols // (2 * pairs)
    chunk = 2 * pairs * PATCH
    count = pairs * canvases * rows
    total = (rows + 2 * HALO) * cols
    return pl.pallas_call(
        functools.partial(stem_kernel, pairs, cols, rows),
        grid=(steps,),
        in_specs=[
            pl.BlockSpec((canvases, rows, chunk), lambda s: (0, 0, s)),
            whole(rim.shape),
            whole(head.shape),
        ],
        out_specs=[
            pl.BlockSpec((count, 2 * C), lambda s: (s, 0)),
            pl.BlockSpec((count, 2 * C), lambda s: (s, 0)),
            whole((canvases, 3, total, C)),
            whole((C, C)),
        ],
        out_shape=[
            shape_of((steps * count, 2 * C)),
            shape_of((steps * count, 2 * C), BF),
            shape_of((canvases, 3, total, C), BF),
            shape_of((C, C), BF),
        ],
        scratch_shapes=[
            pltpu.VMEM((canvases, 2, total + 16, LANE), F32),
            pltpu.VMEM((2 * PATCH, 2 * C), BF),
            pltpu.VMEM((1, 2 * C), F32),
            pltpu.VMEM((1, C), F32),
        ],
        compiler_params=pltpu.CompilerParams(vmem_limit_bytes=VMEM_LIMIT),
        name="stem",
    )(patches, rim, head)


def stem_backward(patches, feature_grad, stem_out, stem_pre, lat_w):
    canvases, rows, width = patches.shape
    cols = width // PATCH
    pairs = 8
    steps = cols // (2 * pairs)
    chunk = 2 * pairs * PATCH
    count = pairs * canvases * rows
    return pl.pallas_call(
        functools.partial(stem_back_kernel, pairs, cols, rows),
        grid=(steps,),
        in_specs=[
            pl.BlockSpec((canvases, rows, chunk), lambda s: (0, 0, s)),
            whole((canvases, 2, rows * cols, LANE)),
            pl.BlockSpec((count, 2 * C), lambda s: (s, 0)),
            pl.BlockSpec((count, 2 * C), lambda s: (s, 0)),
            whole((C, C)),
        ],
        out_specs=whole((TOWER_ROW, C)),
        out_shape=shape_of((TOWER_ROW, C), BF),
        scratch_shapes=[
            pltpu.VMEM((PATCH, C), F32),
            pltpu.VMEM((1, C), F32),
            pltpu.VMEM((C, C), F32),
            pltpu.VMEM((1, C), F32),
            pltpu.VMEM((TOWER_ROW, C), F32),
        ],
        compiler_params=pltpu.CompilerParams(vmem_limit_bytes=VMEM_LIMIT),
        name="stem_back",
    )(patches, feature_grad, stem_out, stem_pre, lat_w)


BOX_CUTS = [(BOX_OUT * n // C, BOX_OUT * n % C) for n in range(64)]


def box_in_kernel(tail_ref, o_ref, t_ref, d_ref, u_ref):
    tail = tail_ref[...].astype(F32)
    count = tail.shape[0]
    lane = lax.broadcasted_iota(jnp.int32, (40, LANE), 1)
    for n in range(2):
        t_ref[n, 0:count, :] = tail[:, n * LANE : n * LANE + LANE]
        t_ref[n, count:, :] = jnp.zeros((t_ref.shape[1] - count, LANE), F32)
    lines = []
    for r in range(9):
        lines.append(jnp.concatenate([t_ref[n, pl.ds(2 + r, 40, stride=9), :] for n in range(2)], axis=1))
    for s, (r, at) in enumerate(BOX_CUTS):
        wide = jnp.concatenate([lines[r], lines[min(r + 1, 8)]], axis=1)
        d_ref[pl.ds(s, 40, stride=64), :] = jnp.where(lane < BOX_OUT, wide[:, at : at + LANE], 0.0)
    for t in range(9):
        turned = d_ref[t * C : t * C + C, :].T
        for n in range(2):
            u_ref[n] = turned[:, n * LANE : n * LANE + LANE]
        for m in range(4):
            here = t * BOX_ROWS + m * SLOT
            parts = [u_ref[n, pl.ds(m, SLOT, stride=4), :] for n in range(2)]
            o_ref[here : here + SLOT, :] = jnp.concatenate(parts, axis=1).astype(BF)


def box_out_kernel(w_ref, b_ref, o_ref, t_ref, d_ref, u_ref):
    u_ref[...] = jnp.zeros_like(u_ref)
    d_ref[9 * C :, :] = jnp.zeros((d_ref.shape[0] - 9 * C, LANE), F32)
    for t in range(9):
        for m in range(4):
            here = t * BOX_ROWS + m * SLOT
            for n in range(2):
                u_ref[n, pl.ds(m, SLOT, stride=4), :] = w_ref[here : here + SLOT, n * LANE : n * LANE + LANE]
        d_ref[t * C : t * C + C, :] = jnp.concatenate([u_ref[0], u_ref[1]], axis=1).T
    lines = [jnp.zeros((40, 2 * C), F32) for _ in range(9)]
    zero = jnp.zeros((40, 2 * C - LANE), F32)
    for s, (r, at) in enumerate(BOX_CUTS):
        wide = jnp.concatenate([d_ref[pl.ds(s, 40, stride=64), :], zero], axis=1)
        lines[r] = lines[r] + (pltpu.roll(wide, at, 1) if at else wide)
    t_ref[...] = jnp.zeros_like(t_ref)
    for r in range(9):
        line = lines[r][:, :C]
        if r:
            line = line + lines[r - 1][:, C:]
        for n in range(2):
            t_ref[n, pl.ds(2 + r, 40, stride=9), :] = line[:, n * LANE : n * LANE + LANE]
    for n in range(2):
        for k in range(2):
            at = k * C + n * LANE
            t_ref[n, k : k + 1, :] = b_ref[:, at : at + LANE]
    rows = o_ref.shape[0]
    o_ref[...] = jnp.concatenate([t_ref[0, 0:rows, :], t_ref[1, 0:rows, :]], axis=1).astype(BF)


def box_call(kernel, shape, kind, name, *args):
    return pl.pallas_call(
        kernel,
        in_specs=[VM] * len(args),
        out_specs=VM,
        out_shape=shape_of(shape, kind),
        scratch_shapes=[
            pltpu.VMEM((2, 368, LANE), F32),
            pltpu.VMEM((40 * 64, LANE), F32),
            pltpu.VMEM((2, LANE, LANE), F32),
        ],
        compiler_params=pltpu.CompilerParams(vmem_limit_bytes=VMEM_LIMIT),
        name=name,
    )(*args)


def heads_call(rows, cols, scal, feats, masks, labels, box_target, full, tb, head, wb):
    canvases = feats.shape[0]
    own = rows * cols
    total = own + 2 * HALO * cols
    spread = jnp.repeat(jnp.eye(SLOT, 9, dtype=BF), LANE, axis=1)

    def per(shape):
        return pl.BlockSpec((1,) + shape, lambda c: (c,) + (0,) * len(shape))

    return pl.pallas_call(
        functools.partial(head_kernel, cols, rows),
        grid=(canvases,),
        in_specs=[
            pl.BlockSpec(memory_space=pltpu.SMEM),
            per((3, total, C)),
            per((SLOT, total)),
            per((SLOT, total)),
            per((4, SLOT, total)),
            whole(spread.shape),
            pl.BlockSpec(memory_space=pl.ANY),
            whole(tb.shape),
            pl.BlockSpec(memory_space=pl.ANY),
            whole(wb.shape),
        ],
        out_specs=[
            pl.BlockSpec(memory_space=pl.ANY),
            pl.BlockSpec(memory_space=pl.ANY),
            whole((9 * BOX_ROWS, C)),
            whole((1, 2 * C)),
            per((2, own, LANE)),
            whole((16, 256)),
        ],
        out_shape=[
            shape_of((9 * C, WIDE), BF),
            shape_of((18 * C, C), BF),
            shape_of((9 * BOX_ROWS, C)),
            shape_of((1, 2 * C)),
            shape_of((canvases, 2, own, LANE)),
            shape_of((16, 256)),
        ],
        scratch_shapes=[
            pltpu.VMEM((9, total, LANE), BF),
            pltpu.VMEM((total - 2 * cols, 2 * C), F32),
            pltpu.VMEM((total, C), BF),
            pltpu.VMEM((WIDE, own + 512), BF),
            pltpu.VMEM((own + 512, WIDE), BF),
            pltpu.VMEM((own + 256, 2 * C), BF),
            pltpu.VMEM((9 * C, 2 * C), BF),
            pltpu.VMEM((WIDE, 9 * C), BF),
            pltpu.VMEM((WIDE, 9 * C), F32),
            pltpu.VMEM((2 * C, 9 * C), F32),
            pltpu.SemaphoreType.DMA((3,)),
        ],
        compiler_params=pltpu.CompilerParams(vmem_limit_bytes=VMEM_LIMIT),
        name="heads",
    )(scal, feats, masks, labels, box_target, spread, full, tb, head, wb)


def place():
    img = lax.axis_index("img")
    cls = lax.axis_index("cls")
    return img // 2, img % 2, cls // 2, cls % 2


def target(z, y, x, c):
    return (z * 2 + y, x * 2 + c)


def owner(z, y, x, c):
    return ((z * 2 + y) * 2 + x) * 2 + c


def enter(peers):
    barrier = pltpu.get_barrier_semaphore()
    for peer in peers:
        pl.semaphore_signal(barrier, inc=1, device_id=peer, device_id_type=MESH)
    pl.semaphore_wait(barrier, len(peers))


class Mail:
    def __init__(self, send_sems, recv_sems):
        self.send_sems, self.recv_sems, self.used, self.sent = send_sems, recv_sems, 0, []

    def push(self, source, landing, peer):
        copy = pltpu.make_async_remote_copy(
            src_ref=source,
            dst_ref=landing,
            send_sem=self.send_sems.at[self.used],
            recv_sem=self.recv_sems.at[self.used],
            device_id=peer,
            device_id_type=MESH,
        )
        self.used += 1
        copy.start()
        self.sent.append(copy)
        return copy

    def close(self):
        for copy in self.sent:
            copy.wait_send()


def window_row(index, shard):
    return pl.multiple_of((index * shard + LEAD * C) // (16 * C) * 16, 16)


def gather_kernel(shard, s_ref, k_ref, n_ref, r_ref, full_ref, head_ref, all_ref, first_ref, last_ref, rim_ref, count_ref, sh_ref, kx_ref, send_sems, recv_sems):
    z, y, x, c = place()
    block = k_ref.shape[0]
    win = s_ref.shape[0]
    others = [(k, j) for k in range(4) for j in range(2) if k or j]
    ring = [((z + k) % 4, (y + j) % 2) for k, j in others]
    line = [(z * 2 + y, (x * 2 + c + step) % 4) for step in (1, 3)]
    enter([target(zz, yy, x, c) for zz, yy in ring] + [target(z, y, 1 - x, c), target(z, y, x, 1 - c)] + line)
    mail = Mail(send_sems, recv_sems)
    me = owner(z, y, x, c)

    def rows(zz, yy):
        return pl.ds(pl.multiple_of((zz * 2 + yy) * block, 16), block)

    def lanes(cc):
        return pl.ds(pl.multiple_of(cc * HALF, LANE), HALF)

    got_kx = mail.push(k_ref, kx_ref, target(z, y, 1 - x, c))
    counts = [mail.push(n_ref, count_ref.at[z * 2 + y], target(zz, yy, x, c)) for zz, yy in ring]
    slot = sh_ref.at[me]
    got_z = [mail.push(s_ref, slot, target((z + k) % 4, y, x, c)) for k in range(1, 4)]
    got_y = [mail.push(s_ref, slot, target(z, 1 - y, x, c))]
    got_x = [mail.push(s_ref, slot, target(z, y, 1 - x, c))]
    got_c = [mail.push(s_ref, slot, target(z, y, x, 1 - c))]
    rims = [mail.push(r_ref.at[n], rim_ref.at[n], line[n]) for n in range(2)]
    count_ref[z * 2 + y] = n_ref[...]
    sh_ref[me] = s_ref[...]

    got_kx.wait_recv()
    mine = head_ref.at[rows(z, y), lanes(c)]
    head_ref[rows(z, y), lanes(c)] = k_ref[...] + kx_ref[...]
    got_kz = [mail.push(mine, mine, target((z + k) % 4, y, x, c)) for k in range(1, 4)]
    got_ky = [mail.push(mine, mine, target(z, 1 - y, x, c))]
    got_kc = [mail.push(mine, mine, target(z, y, x, 1 - c))]

    for k in range(1, 4):
        got_z[k - 1].wait_recv()
        slot = sh_ref.at[owner((z + 4 - k) % 4, y, x, c)]
        got_y.append(mail.push(slot, slot, target(z, 1 - y, x, c)))
        got_x.append(mail.push(slot, slot, target(z, y, 1 - x, c)))
        got_c.append(mail.push(slot, slot, target(z, y, x, 1 - c)))
    for k in range(1, 4):
        got_kz[k - 1].wait_recv()
        part = head_ref.at[rows((z + 4 - k) % 4, y), lanes(c)]
        got_ky.append(mail.push(part, part, target(z, 1 - y, x, c)))
        got_kc.append(mail.push(part, part, target(z, y, x, 1 - c)))
    for k in range(4):
        got_y[k].wait_recv()
        slot = sh_ref.at[owner((z + 4 - k) % 4, 1 - y, x, c)]
        got_x.append(mail.push(slot, slot, target(z, y, 1 - x, c)))
        got_c.append(mail.push(slot, slot, target(z, y, x, 1 - c)))
    for k in range(4):
        got_ky[k].wait_recv()
        part = head_ref.at[rows((z + 4 - k) % 4, 1 - y), lanes(c)]
        got_kc.append(mail.push(part, part, target(z, y, x, 1 - c)))
    for k in range(8):
        got_x[k].wait_recv()
        slot = sh_ref.at[owner((z + 4 - k % 4) % 4, (y + k // 4) % 2, 1 - x, c)]
        got_c.append(mail.push(slot, slot, target(z, y, x, 1 - c)))
    for copy in got_c + got_kc + counts + rims:
        copy.wait_recv()
    all_ref[...] = jnp.sum(count_ref[...], axis=0)
    full_ref[...] = jnp.zeros_like(full_ref)

    def merge(d, carry):
        full_ref[pl.ds(window_row(d, shard), win), :] += sh_ref[d]
        return carry

    lax.fori_loop(0, 32, merge, 0)
    first_ref[...] = full_ref[0:TOWER_ROW, :]
    last_ref[...] = full_ref[TAIL_ROW:FULL_ROWS, :]
    mail.close()


def scatter_kernel(
    shard, head_ref, tower_ref, tail_ref, k_ref, n_ref, s_out, k_out, n_out,
    full_ref, sc_ref, sx_ref, sy_ref, sz_ref, kc_ref, ky_ref, kz_ref, kx_ref, mine_ref, peer_ref, far_ref, nz_ref, send_sems, recv_sems,
):
    z, y, x, c = place()
    block = kx_ref.shape[1]
    win = s_out.shape[0]
    enter([target((z + k) % 4, y, x, c) for k in range(1, 4)] + [target(z, 1 - y, x, c), target(z, y, 1 - x, c), target(z, y, x, 1 - c)])
    mail = Mail(send_sems, recv_sems)

    def rows(zz, yy):
        return pl.ds(pl.multiple_of((zz * 2 + yy) * block, 16), block)

    def lanes(cc):
        return pl.ds(pl.multiple_of(cc * HALF, LANE), HALF)

    def window(zz, yy, xx, cc):
        return pl.ds(window_row(owner(zz, yy, xx, cc), shard), win)

    mine_ref[0] = n_ref[...]
    sum_c = mail.push(mine_ref.at[0], peer_ref.at[0], target(z, y, x, 1 - c))
    spots = [(j, k) for j in (1, 0) for k in (1, 2, 3, 0)]
    got_kc = []
    for n, (j, k) in enumerate(spots):
        part = k_ref.at[rows((z + k) % 4, (y + j) % 2), lanes(1 - c)]
        got_kc.append(mail.push(part, kc_ref.at[n], target(z, y, x, 1 - c)))
    full_ref[0:TOWER_ROW, :] = head_ref[...]
    full_ref[TOWER_ROW:TAIL_ROW, :] = tower_ref[...]
    full_ref[TAIL_ROW:FULL_ROWS, :] = tail_ref[...]
    got_c = []
    for i in (1, 0):
        for n, (j, k) in enumerate(spots):
            part = full_ref.at[window((z + k) % 4, (y + j) % 2, (x + i) % 2, 1 - c), :]
            got_c.append(mail.push(part, sc_ref.at[(1 - i) * 8 + n], target(z, y, x, 1 - c)))

    sum_c.wait_recv()
    mine_ref[1] = mine_ref[0] + peer_ref[0]
    sum_x = mail.push(mine_ref.at[1], peer_ref.at[1], target(z, y, 1 - x, c))

    got_ky = []
    for n, (j, k) in enumerate(spots):
        got_kc[n].wait_recv()
        kc_ref[n] = kc_ref[n] + k_ref[rows((z + k) % 4, (y + j) % 2), lanes(c)]
        if j == 1:
            got_ky.append(mail.push(kc_ref.at[n], ky_ref.at[n], target(z, 1 - y, x, c)))
    got_x = []
    for n, (j, k) in enumerate(spots):
        got_c[n].wait_recv()
        sc_ref[n] = sc_ref[n] + full_ref[window((z + k) % 4, (y + j) % 2, 1 - x, c), :]
        got_x.append(mail.push(sc_ref.at[n], sx_ref.at[n], target(z, y, 1 - x, c)))

    sum_x.wait_recv()
    mine_ref[2] = mine_ref[1] + peer_ref[1]
    sum_y = mail.push(mine_ref.at[2], peer_ref.at[2], target(z, 1 - y, x, c))

    got_kz = []
    for n in range(4):
        got_ky[n].wait_recv()
        kc_ref[4 + n] = kc_ref[4 + n] + ky_ref[n]
        if n < 3:
            got_kz.append(mail.push(kc_ref.at[4 + n], kz_ref.at[n], target((z + n + 1) % 4, y, x, c)))
    got_y = []
    for n, (j, k) in enumerate(spots):
        got_c[8 + n].wait_recv()
        got_x[n].wait_recv()
        total = sc_ref[8 + n].astype(F32) + full_ref[window((z + k) % 4, (y + j) % 2, x, c), :].astype(F32)
        sc_ref[8 + n] = (total + sx_ref[n].astype(F32)).astype(BF)
        if j == 1:
            got_y.append(mail.push(sc_ref.at[8 + n], sy_ref.at[n], target(z, 1 - y, x, c)))

    sum_y.wait_recv()
    mine_ref[3] = mine_ref[2] + peer_ref[2]
    nz_ref[z] = mine_ref[3]
    sum_z = [mail.push(mine_ref.at[3], nz_ref.at[z], target((z + k) % 4, y, x, c)) for k in range(1, 4)]

    total = kc_ref[7].astype(F32)
    for n in range(3):
        got_kz[n].wait_recv()
        total += kz_ref[n].astype(F32)
    kx_ref[0] = total.astype(BF)
    got_kx = mail.push(kx_ref.at[0], kx_ref.at[1], target(z, y, 1 - x, c))
    got_z = []
    for n in range(4):
        got_y[n].wait_recv()
        sc_ref[12 + n] = sc_ref[12 + n] + sy_ref[n]
        if n < 3:
            got_z.append(mail.push(sc_ref.at[12 + n], sz_ref.at[n], target((z + n + 1) % 4, y, x, c)))
    total = sc_ref[15].astype(F32)
    for n in range(3):
        got_z[n].wait_recv()
        total += sz_ref[n].astype(F32)
    s_out[...] = total
    for copy in sum_z:
        copy.wait_recv()
    n_out[...] = (nz_ref[0] + nz_ref[1]) + (nz_ref[2] + nz_ref[3])
    got_kx.wait_recv()
    k_out[...] = kx_ref[0].astype(F32) + kx_ref[1].astype(F32)
    mail.close()


def fast_mesh(img_parts, cls_parts, class_rows):
    return img_parts == 8 and cls_parts == 4 and class_rows % 16 == 0


def flat_place(index, shard):
    return (index * shard + LEAD * C) % (16 * C)


def gather_all(shared_params, class_params, count, edges):
    img, cls = lax.axis_index("img"), lax.axis_index("cls")
    img_parts, cls_parts = lax.axis_size("img"), lax.axis_size("cls")
    shard = shared_params.shape[0]
    block, part = class_params.shape
    if not fast_mesh(img_parts, cls_parts, block):
        flat = lax.all_gather(shared_params.astype(BF), ("img", "cls"), axis=0, tiled=True)
        full = jnp.pad(flat, (LEAD * C, FULL_ROWS * C - LEAD * C - flat.shape[0])).reshape(FULL_ROWS, C)
        head = lax.all_gather(class_params.astype(BF), ("img", "cls"), axis=0)
        head = head.reshape(img_parts, cls_parts, block, part).transpose(0, 2, 1, 3).reshape(-1, CLS_OUT)
        pieces = []
        for half in range(2):
            pieces += [head[:, 180 * half : 180 * half + 180], head[:, 360 + 180 * half : 540 + 180 * half]]
            pieces.append(jnp.zeros((head.shape[0], HALF - 360), BF))
        ways = [[(i, (i + step) % cls_parts) for i in range(cls_parts)] for step in (1, cls_parts - 1)]
        rim = jnp.stack([lax.ppermute(edges[n], "cls", ways[n]) for n in range(2)])
        return full, full[:TOWER_ROW], full[TAIL_ROW:], jnp.concatenate(pieces, axis=1), lax.psum(count, "img"), rim
    rows = -(-(shard + 16 * C) // (16 * C)) * 16
    window = lax.dynamic_update_slice(
        jnp.zeros((rows * C,), BF), shared_params.astype(BF), (flat_place(img * cls_parts + cls, shard),)
    ).reshape(rows, C)
    wide = jnp.pad(class_params.astype(BF), ((0, 0), (part, HALF - part)))
    wide = lax.dynamic_slice_in_dim(
        jnp.pad(wide, ((0, 0), (0, part))), jnp.where(cls // 2 == 0, part, 0), HALF, 1
    )
    number = jnp.broadcast_to(count, (8, LANE))
    full, head, counts, first, last, rim = pl.pallas_call(
        functools.partial(gather_kernel, shard),
        in_specs=[VM] * 4,
        out_specs=[VM] * 6,
        out_shape=[
            shape_of((FULL_ROWS, C), BF),
            shape_of((img_parts * block, 2 * HALF), BF),
            shape_of((8, LANE)),
            shape_of((TOWER_ROW, C), BF),
            shape_of((FULL_ROWS - TAIL_ROW, C), BF),
            shape_of(edges.shape, BF),
        ],
        scratch_shapes=[
            pltpu.VMEM((img_parts, 8, LANE), F32),
            pltpu.VMEM((img_parts * cls_parts, rows, C), BF),
            pltpu.VMEM((block, HALF), BF),
            pltpu.SemaphoreType.DMA((56,)),
            pltpu.SemaphoreType.DMA((56,)),
        ],
        compiler_params=pltpu.CompilerParams(collective_id=0, has_side_effects=True, vmem_limit_bytes=VMEM_LIMIT),
        name="gather",
    )(window, wide, number, edges)
    return full, first, last, head, counts[0, 0], rim


def scatter_all(head, tower, tail, class_grad, sums, shard, block, part):
    img, cls = lax.axis_index("img"), lax.axis_index("cls")
    img_parts, cls_parts = lax.axis_size("img"), lax.axis_size("cls")
    if not fast_mesh(img_parts, cls_parts, block):
        flat = jnp.concatenate([head, tower, tail], axis=0).reshape(-1)
        flat = flat[LEAD * C : LEAD * C + shard * img_parts * cls_parts].astype(F32)
        shared = lax.psum_scatter(flat, ("img", "cls"), scatter_dimension=0, tiled=True)
        pieces = [class_grad[:, at : at + 180] for at in (0, HALF, 180, HALF + 180)]
        whole_grad = lax.psum_scatter(
            jnp.concatenate(pieces, axis=1).astype(F32), "img", scatter_dimension=0, tiled=True
        )
        return shared, lax.psum_scatter(whole_grad, "cls", scatter_dimension=1, tiled=True), lax.psum(sums, ("img", "cls"))
    rows = -(-(shard + 16 * C) // (16 * C)) * 16
    window, wide, sums = pl.pallas_call(
        functools.partial(scatter_kernel, shard),
        in_specs=[VM] * 5,
        out_specs=[VM] * 3,
        out_shape=[shape_of((rows, C)), shape_of((block, HALF)), shape_of(sums.shape)],
        scratch_shapes=[
            pltpu.VMEM((FULL_ROWS, C), BF),
            pltpu.VMEM((16, rows, C), BF),
            pltpu.VMEM((8, rows, C), BF),
            pltpu.VMEM((4, rows, C), BF),
            pltpu.VMEM((3, rows, C), BF),
            pltpu.VMEM((8, block, HALF), BF),
            pltpu.VMEM((4, block, HALF), BF),
            pltpu.VMEM((3, block, HALF), BF),
            pltpu.VMEM((2, block, HALF), BF),
            pltpu.VMEM((4,) + sums.shape, F32),
            pltpu.VMEM((3,) + sums.shape, F32),
            pltpu.VMEM((8, LANE), F32),
            pltpu.VMEM((4,) + sums.shape, F32),
            pltpu.SemaphoreType.DMA((53,)),
            pltpu.SemaphoreType.DMA((53,)),
        ],
        compiler_params=pltpu.CompilerParams(collective_id=1, has_side_effects=True, vmem_limit_bytes=VMEM_LIMIT),
        name="scatter",
    )(head, tower, tail, class_grad, sums)
    flat = lax.dynamic_slice_in_dim(window.reshape(-1), flat_place(img * cls_parts + cls, shard), shard)
    grad = lax.dynamic_slice_in_dim(wide, jnp.where(cls // 2 == 0, 0, part), part, 1)
    grad = lax.optimization_barrier(grad.T).T
    return flat, grad, sums


def column_plan():
    plan = []
    for half in range(2):
        for group in range(2):
            column, row, end = 360 * group + 180 * half, HALF * half + 180 * group, 360 * group + 180 * half + 180
            while column < end:
                count = min(end, (column // CLASSES + 1) * CLASSES) - column
                plan.append((row, count, column // CLASSES, column % CLASSES))
                column, row = column + count, row + count
        plan.append((HALF * half + 360, HALF - 360, -1, 0))
    return plan


def adamw_update(weight, first, second, grad):
    first_new = MOMENT_ONE * first + (1.0 - MOMENT_ONE) * grad
    second_new = MOMENT_TWO * second + (1.0 - MOMENT_TWO) * grad * grad
    first_hat = first_new / (1.0 - MOMENT_ONE**STEP)
    second_hat = second_new / (1.0 - MOMENT_TWO**STEP)
    weight_new = weight - RATE * (first_hat / (jnp.sqrt(second_hat) + EPSILON) + DECAY * weight)
    return (weight_new, first_new, second_new)


def valid_positives(boxes, match, full_rows, cols):
    place = jnp.arange(full_rows * cols, dtype=jnp.int32)
    row, col = place // cols, place % cols
    inside = jnp.zeros((boxes.shape[0], full_rows * cols), bool)
    for k in range(boxes.shape[1]):
        edge = boxes[:, k, :, None]
        inside |= (row >= edge[:, 0]) & (row < edge[:, 2]) & (col >= edge[:, 1]) & (col < edge[:, 3])
    return ((match >= 0) & inside[:, None]).astype(F32)


def cell_data(boxes, match, gt_labels, gt_deltas, first_row, rows, cols):
    full_rows = match.shape[2] // cols
    total = (rows + 2 * HALO) * cols
    place = jnp.arange(total, dtype=jnp.int32)[None]
    row = place // cols + (first_row - HALO)
    col = place % cols

    def crop(r, j):
        found = jnp.full((boxes.shape[0], total), -1, jnp.int32)
        for k in range(boxes.shape[1]):
            edge = boxes[:, k, :, None]
            inside = (r >= edge[:, 0]) & (r < edge[:, 2]) & (j >= edge[:, 1]) & (j < edge[:, 3])
            found = jnp.where(inside, k, found)
        return jnp.where((r >= 0) & (r < full_rows) & (j >= 0) & (j < cols), found, -1)

    centre = crop(row, col)
    valid = centre >= 0
    masks = jnp.stack([(crop(row + di, col + dj) == centre) & valid for di, dj in TAPS], axis=1)
    masks = jnp.pad(masks.astype(BF), ((0, 0), (0, SLOT - 9), (0, 0)))
    edge = HALO * cols
    near = jnp.pad(match, ((0, 0), (0, 0), (edge, edge)), constant_values=-2)
    near = lax.dynamic_slice_in_dim(near, first_row * cols, total, 2)
    near = jnp.where(valid[:, None], near, -2)
    near = jnp.pad(near, ((0, 0), (0, SLOT - 9), (0, 0)), constant_values=-2)
    labels = near
    targets = jnp.zeros((near.shape[0], 4) + near.shape[1:], F32)
    for g in range(gt_labels.shape[1]):
        labels = jnp.where(near == g, gt_labels[:, g, None, None], labels)
        targets = jnp.where((near == g)[:, None], gt_deltas[:, g, :, None, None], targets)
    return masks, labels.astype(F32), targets


def local(patches, boxes, match, gt_labels, gt_deltas, ema_old, shared_params, shared_m, shared_v, class_params, class_m, class_v):
    cls_rank = lax.axis_index("cls")
    canvases, rows, width = patches.shape
    cols = width // PATCH
    masks, labels, targets = cell_data(boxes, match, gt_labels, gt_deltas, cls_rank * rows, rows, cols)
    full_rows = match.shape[2] // cols
    count = jnp.sum(valid_positives(boxes, match, full_rows, cols))
    edges = jnp.stack([patches[:, rows - HALO :], patches[:, :HALO]]).reshape(2, canvases * HALO, width)
    edges = jnp.concatenate([edges[..., : width // 2], edges[..., width // 2 :]], axis=1)
    full, first, last, head, positives, rim = gather_all(shared_params, class_params, count, edges)
    norm = jnp.maximum(positives, 1.0)
    ema_new = EMA_KEEP * ema_old + (1.0 - EMA_KEEP) * norm
    tb = last[0:2].reshape(1, 2 * C).astype(F32)
    wb = box_call(box_in_kernel, (9 * BOX_ROWS, C), BF, "box_in", last)
    stem_pre, stem_out, feats, lat_w = stem_forward(patches, rim, first)
    scal = jnp.stack([1.0 / ema_new, 1.0 / norm])
    class_grad, tower_grad, dwb, db, feature_grad, sums = heads_call(
        rows, cols, scal, feats, masks, labels, targets, full, tb, head, wb
    )
    first_grad = stem_backward(patches, feature_grad, stem_out, stem_pre, lat_w)
    last_grad = box_call(box_out_kernel, last.shape, BF, "box_out", dwb, db)
    shared_grad, class_grad, sums = scatter_all(
        first_grad, tower_grad, last_grad, class_grad, sums, shared_params.shape[0], *class_params.shape
    )
    loss = jnp.sum(sums[0:8]) / ema_new + jnp.sum(sums[8:16]) / norm
    return (
        loss,
        ema_new,
        *adamw_update(shared_params, shared_m, shared_v, shared_grad),
        *adamw_update(class_params, class_m, class_v, class_grad),
    )


def solution(mesh):
    spread = P(("img", "cls"))
    block = P("img", "cls")
    return jax.shard_map(
        local,
        mesh=mesh,
        in_specs=(
            P("img", "cls", None),
            P("img", None, None),
            P("img", None, None),
            P("img", None),
            P("img", None, None),
            P(),
            spread,
            spread,
            spread,
            block,
            block,
            block,
        ),
        out_specs=(P(), P(), spread, spread, spread, block, block, block),
        check_vma=False,
    )
```

```python
import functools

import jax
import jax.numpy as jnp
from jax import lax
from jax.experimental import pallas as pl
from jax.experimental.pallas import tpu as pltpu
from jax.sharding import PartitionSpec as P

C = 256
CLASSES = 80
ANCH = 9
PATCH = 192
BOX_OUT = 36
CLS_OUT = ANCH * CLASSES
STEP = 5
GT = 16
HALO = 4
SLOT = 16
BOX_ROWS = 4 * SLOT
LANE = 128
WIDE = 768
GROUP = 16

PRIOR = -4.59511985013459
ALPHA = 0.25
HUBER = 1.0 / 9.0
EMA_KEEP = 0.9
RATE = 0.01
MOMENT_ONE = 0.5
MOMENT_TWO = 0.5
DECAY = 0.05
EPSILON = 1e-08

LENGTHS = [PATCH * C, C, C * C, C, 18 * C * C, 2 * C, 9 * C * BOX_OUT]
TOWER_AT = sum(LENGTHS[:4]) // C
LEAD = -TOWER_AT % 16
TOWER_ROW = TOWER_AT + LEAD
TAIL_ROW = TOWER_ROW + 18 * C
FULL_ROWS = -(-(LEAD + sum(LENGTHS) // C) // 16) * 16
HALF = 384
MESH = pl.DeviceIdType.MESH

BF = jnp.bfloat16
F32 = jnp.float32
TAPS = [(di, dj) for di in (-1, 0, 1) for dj in (-1, 0, 1)]
NN = (((1,), (0,)), ((), ()))
NT = (((1,), (1,)), ((), ()))
TN = (((0,), (0,)), ((), ()))
K0 = 0.7978845608028654
K1 = 0.044715


def mm(a, b, dims=NN):
    return lax.dot_general(a, b, dims, preferred_element_type=F32)


def gelu(x):
    return 0.5 * x * (1.0 + jnp.tanh(K0 * (x + K1 * x * x * x)))


def gelu_slope(x):
    square = x * x
    th = jnp.tanh(K0 * (x + K1 * x * square))
    return 0.5 * (1.0 + th) + (0.5 * K0) * x * (1.0 - th * th) * (1.0 + 3.0 * K1 * square)


def columns_of(x, pairs, width):
    return [x[:, width * k : width * (k + 1)] for k in range(pairs)]


def stem_kernel(pairs, cols, rows, x_ref, h_ref, head_ref, pre_ref, so_ref, f_ref, lw_ref, t_ref, w_ref, b_ref, lb_ref):
    step = pl.program_id(0)
    canvases = x_ref.shape[0]
    own_rows = canvases * rows
    total = (rows + 2 * HALO) * cols

    @pl.when(step == 0)
    def _():
        head = head_ref[...].astype(F32)
        w_ref[...] = jnp.zeros_like(w_ref)
        stem_w = head[LEAD : LEAD + PATCH].astype(BF)
        w_ref[:PATCH, :C] = stem_w
        w_ref[PATCH:, C:] = stem_w
        bias = head[LEAD + PATCH : LEAD + PATCH + 1]
        b_ref[...] = jnp.concatenate([bias, bias], axis=1)
        lw_ref[...] = head[LEAD + PATCH + 1 : TOWER_ROW - 1].astype(BF)
        lb_ref[...] = head[TOWER_ROW - 1 : TOWER_ROW]
        for c in range(canvases):
            for n in range(2):
                t_ref[c, n, 0:8, :] = jnp.zeros((8, LANE), F32)
                t_ref[c, n, 8 + total : 16 + total, :] = jnp.zeros((8, LANE), F32)

    x = x_ref[...].reshape(own_rows, x_ref.shape[2])
    own = columns_of(x, pairs, 2 * PATCH)
    half = pl.num_programs(0) // 2
    lanes = pl.ds(pl.multiple_of(step % half * x.shape[1], LANE), x.shape[1])
    many_rows = h_ref.shape[1] // 2
    near = [h_ref[n, :, lanes].astype(F32) for n in range(2)]
    near = [jnp.where(step < half, one[:many_rows], one[many_rows:]) for one in near]
    rim = columns_of(jnp.concatenate(near, axis=0).astype(BF), pairs, 2 * PATCH)
    pre = mm(jnp.concatenate(own + rim, axis=0), w_ref[...]) + b_ref[...]
    count = pairs * own_rows
    pre_ref[...] = pre[:count]
    out = gelu(pre).astype(BF)
    so_ref[...] = out[:count]
    for half in range(2):
        feat = mm(out[:, half * C : half * C + C], lw_ref[...]) + lb_ref[...]
        for k in range(pairs):
            j = step * 2 * pairs + 2 * k + half
            for c in range(canvases):
                at = k * own_rows + c * rows
                up_at = count + k * 2 * HALO * canvases + c * HALO
                down_at = up_at + HALO * canvases
                for n in range(2):
                    side = slice(n * LANE, n * LANE + LANE)
                    place = pl.ds(8 + HALO * cols + j, rows, stride=cols)
                    t_ref[c, n, place, :] = feat[at : at + rows, side]
                    place = pl.ds(8 + j, HALO, stride=cols)
                    t_ref[c, n, place, :] = feat[up_at : up_at + HALO, side]
                    place = pl.ds(8 + (HALO + rows) * cols + j, HALO, stride=cols)
                    t_ref[c, n, place, :] = feat[down_at : down_at + HALO, side]

    @pl.when(step == pl.num_programs(0) - 1)
    def _():
        piece = 4 * cols

        def move(i, carry):
            base = pl.multiple_of(i * piece, 16)
            for c in range(canvases):
                for n in range(2):
                    value = t_ref[c, n, pl.ds(base, piece + 16), :]
                    for k in range(3):
                        moved = value[7 + k : 7 + k + piece].astype(BF)
                        f_ref[c, k, pl.ds(base, piece), n * LANE : n * LANE + LANE] = moved
            return carry

        lax.fori_loop(0, total // piece, move, 0)


def stem_back_kernel(pairs, cols, rows, x_ref, fg_ref, so_ref, pre_ref, lw_ref, head_ref, sw_out, sb_out, lw_out, lb_out, h_ref):
    step = pl.program_id(0)
    canvases = x_ref.shape[0]

    @pl.when(step == 0)
    def _():
        sw_out[...] = jnp.zeros_like(sw_out)
        sb_out[...] = jnp.zeros_like(sb_out)
        lw_out[...] = jnp.zeros_like(lw_out)
        lb_out[...] = jnp.zeros_like(lb_out)

    x = x_ref[...].reshape(canvases * rows, x_ref.shape[2])
    own = jnp.concatenate(columns_of(x, pairs, 2 * PATCH), axis=0)
    low = []
    for half in range(2):
        parts = []
        for k in range(pairs):
            j = step * 2 * pairs + 2 * k + half
            for c in range(canvases):
                place = pl.ds(j, rows, stride=cols)
                parts.append(jnp.concatenate([fg_ref[c, n, place, :] for n in range(2)], axis=1))
        grad32 = jnp.concatenate(parts, axis=0)
        grad = grad32.astype(BF)
        cut = slice(half * C, half * C + C)
        lw_out[...] += mm(so_ref[:, cut], grad, TN)
        lb_out[...] += jnp.sum(grad32, axis=0, keepdims=True)
        back = mm(grad, lw_ref[...], NT) * gelu_slope(pre_ref[:, cut])
        back = back.astype(BF)
        sb_out[...] += jnp.sum(back.astype(F32), axis=0, keepdims=True)
        low.append(back)
    both = mm(own, jnp.concatenate(low, axis=1), TN)
    sw_out[...] += both[:PATCH, :C] + both[PATCH:, C:]

    @pl.when(step == pl.num_programs(0) - 1)
    def _():
        at = LEAD + PATCH
        h_ref[0:LEAD, :] = jnp.zeros((LEAD, C), F32)
        h_ref[LEAD:at, :] = sw_out[...]
        h_ref[at : at + 1, :] = sb_out[...]
        h_ref[at + 1 : TOWER_ROW - 1, :] = lw_out[...]
        h_ref[TOWER_ROW - 1 :, :] = lb_out[...]
        head_ref[...] = h_ref[...].astype(BF)


def aligned(value, multiple):
    return value if isinstance(value, int) else pl.multiple_of(value, multiple)


def many(mask, count):
    return jnp.concatenate([mask] * count, axis=1)


def weight_sums(canvas, cols, edge, own, grad, source, mx_ref, sum_ref):
    def go(x_ref):
        def triple(n, carry):
            at = pl.multiple_of(edge + cols * (n - 1), 16)
            for k in range(3):
                mask = mx_ref[n * 3 + k, edge : edge + own, :]
                x_ref[:, k * C : k * C + C] = source[k, pl.ds(at, own), :] * many(mask, 2)
            side = pl.ds(pl.multiple_of(n * 3 * C, C), 3 * C)
            sum_ref[:, side] = jnp.where(canvas > 0, sum_ref[:, side], 0.0) + mm(grad(), x_ref[...])
            return carry

        lax.fori_loop(0, 3, triple, 0)

    pl.run_scoped(go, pltpu.VMEM((own, 3 * C), BF))


def head_kernel(
    cols, rows, scal_ref, f_ref, mk_ref, lab_ref, btt_ref, e_ref, full_ref, tb_ref, head_ref, wb_ref,
    class_ref, tower_ref, dwb_ref, db_ref, fg_ref, sums_ref,
    mx_ref, pre_ref, bt_ref, lgt_ref, lgs_ref, g_ref, wt_ref, wct_ref, dwc_ref, dwt_ref, copy_sems,
):
    own = rows * cols
    edge = HALO * cols
    total = own + 2 * edge
    shift = [cols * di + dj for di, dj in TAPS]

    @pl.when(pl.program_id(0) == 0)
    def _():
        dwb_ref[...] = jnp.zeros_like(dwb_ref)
        db_ref[...] = jnp.zeros_like(db_ref)
        sums_ref[...] = jnp.zeros_like(sums_ref)
        def fetch(held_ref):
            copies = [pltpu.make_async_copy(head_ref, held_ref, copy_sems.at[2])]
            for n in range(2):
                rows_of = full_ref.at[TOWER_ROW + n * 9 * C : TOWER_ROW + (n + 1) * 9 * C, :]
                copies.append(pltpu.make_async_copy(rows_of, wt_ref.at[:, n * C : n * C + C], copy_sems.at[n]))
            for copy in copies:
                copy.start()
            copies[0].wait()

            def turn(t, carry):
                at = pl.multiple_of(t * C, C)
                wct_ref[:, pl.ds(at, C)] = held_ref[pl.ds(at, C), :].T
                return carry

            lax.fori_loop(0, 9, turn, 0)
            for copy in copies[1:]:
                copy.wait()

        pl.run_scoped(fetch, pltpu.VMEM((9 * C, WIDE), BF))

    def spread(i, carry):
        at = pl.multiple_of(i * 384, 128)
        wide = mm(mk_ref[0, :, pl.ds(at, 384)], e_ref[...], TN).astype(BF)
        for t in range(9):
            mx_ref[t, pl.ds(at, 384), :] = wide[:, t * LANE : (t + 1) * LANE]
        return carry

    lax.fori_loop(0, total // 384, spread, 0)

    def twice(mask):
        return jnp.concatenate([mask, mask], axis=1)

    def build(source, at, count, x_ref):
        for t, (di, dj) in enumerate(TAPS):
            value = source[dj + 1, pl.ds(pl.multiple_of(at + cols * di, 16), count), :]
            x_ref[:, t * C : (t + 1) * C] = value * twice(mx_ref[t, pl.ds(at, count), :])

    first_tower = cols
    tower_rows = total - 2 * cols
    first_logit = edge - 256
    logit_cells = own + 512
    first_g = edge - 128
    g_cells = own + 256

    def heads(ct32_ref, ct_ref):
        zero = jnp.zeros((cols + 8, C), F32)
        ct32_ref[0 : cols + 8, :] = zero
        ct32_ref[8 + total - cols : 16 + total, :] = zero
        zero = jnp.zeros((cols, C), BF)
        bt_ref[0:cols, :] = zero
        bt_ref[total - cols : total, :] = zero
        piece = tower_rows // 2

        def towers(x_ref):
            def tower(i, carry):
                row = pl.multiple_of(i * piece, 16)
                at = pl.multiple_of(first_tower + i * piece, 16)
                build(f_ref.at[0], at, piece, x_ref)
                pre = mm(x_ref[...], wt_ref[...]) + tb_ref[...]
                pre_ref[pl.ds(row, piece), :] = pre
                out = gelu(pre)
                ct32_ref[pl.ds(pl.multiple_of(8 + at, 8), piece), :] = out[:, :C]
                bt_ref[pl.ds(at, piece), :] = out[:, C:].astype(BF)
                return carry

            lax.fori_loop(0, 2, tower, 0)

        pl.run_scoped(towers, pltpu.VMEM((piece, 9 * C), BF))

        def move(i, carry):
            base = pl.multiple_of(i * edge, 16)
            value = ct32_ref[pl.ds(base, edge + 16), :]
            for k in range(3):
                ct_ref[k, pl.ds(base, edge), :] = value[7 + k : 7 + k + edge].astype(BF)
            return carry

        lax.fori_loop(0, total // edge, move, 0)
        def logits(xa_ref, la_ref):
            inv_ema = scal_ref[0]
            number = lax.broadcasted_iota(jnp.int32, (GROUP, 256), 0).astype(F32)
            lane = lax.broadcasted_iota(jnp.int32, (8, 256), 1)
            plan = column_plan()

            def ready(q, x_ref):
                build(ct_ref, pl.multiple_of(first_logit + q * 256, 128), 256, x_ref)

            def work(q, x_ref, l_ref):
                l_ref[...] = mm(wct_ref[...], x_ref[...], NT)

            def focal(q, l_ref):
                row = pl.multiple_of(q * 256, 128)
                at = pl.multiple_of(first_logit + row, 128)
                spot = lane + at
                mine = (spot >= edge) & (spot < edge + own)
                lines = [lab_ref[0, a : a + 1, pl.ds(at, 256)] for a in range(ANCH)]
                rest = [jnp.where(line > -1.5, 1.0 - ALPHA, 0.0) for line in lines]
                pulls = [line * inv_ema for line in rest]
                total_focal = jnp.zeros((8, 256), F32)
                for first in range(0, WIDE, GROUP):
                    value = l_ref[first : first + GROUP, :] + PRIOR
                    key = None
                    for begin, count, anchor, klass in plan:
                        if begin >= first + GROUP or begin + count <= first:
                            continue
                        if anchor < 0:
                            parts = [jnp.full((GROUP, 256), n, F32) for n in (-2.0, 0.0, 0.0)]
                        else:
                            parts = [lines[anchor] - float(klass - (begin - first)), rest[anchor], pulls[anchor]]
                            parts = [jnp.broadcast_to(part, (GROUP, 256)) for part in parts]
                        if key is None:
                            key, other, pull_other = parts
                        else:
                            later = number >= float(begin - first)
                            key = jnp.where(later, parts[0], key)
                            other = jnp.where(later, parts[1], other)
                            pull_other = jnp.where(later, parts[2], pull_other)
                    hit = key == number
                    side = jnp.where(hit, -value, value)
                    small = jnp.exp(-jnp.abs(side))
                    whole_one = 1.0 + small
                    ratio = pltpu.reciprocal(whole_one, approx=True)
                    ratio = ratio * (2.0 - whole_one * ratio)
                    part = small * ratio
                    up = side >= 0.0
                    prob = jnp.where(up, ratio, part)
                    miss = jnp.where(up, part, ratio)
                    tiny = small * (1.0 - 0.5 * small)
                    cross = jnp.maximum(side, 0.0) + jnp.where(small < 0.001, tiny, jnp.log(whole_one))
                    square = prob * prob
                    value = square * cross * jnp.where(hit, ALPHA, other)
                    pull = square * (2.0 * miss * cross + prob) * jnp.where(hit, -ALPHA * inv_ema, pull_other)
                    l_ref[first : first + GROUP, :] = pull
                    lgt_ref[first : first + GROUP, pl.ds(row, 256)] = pull.astype(BF)
                    total_focal += jnp.sum(value.reshape(GROUP // 8, 8, 256), axis=0)
                sums_ref[0:8, :] += jnp.where(mine, total_focal, 0.0)
                lgs_ref[pl.ds(row, 256), :] = l_ref[...].T.astype(BF)

            def logits_of(q, carry):
                ready(q, xa_ref)
                work(q, xa_ref, la_ref)
                focal(q, la_ref)
                return carry

            lax.fori_loop(0, logit_cells // 256, logits_of, 0)

        pl.run_scoped(logits, pltpu.VMEM((256, 9 * C), BF), pltpu.VMEM((WIDE, 256), F32))
        weight_sums(pl.program_id(0), cols, edge, own, lambda: lgt_ref[:, 256 : 256 + own], ct_ref, mx_ref, dwc_ref)

    pl.run_scoped(heads, pltpu.VMEM((total + 16, C), F32), pltpu.VMEM((3, total, C), BF))

    def box_forward(gg_ref, y_ref):
        inv_norm = scal_ref[1]

        def outer(i, carry):
            at = pl.multiple_of(i * 768, 128)
            y_ref[:, pl.ds(at, 768)] = mm(wb_ref[...], bt_ref[pl.ds(at, 768), :], NT)
            return carry

        lax.fori_loop(0, total // 768, outer, 0)
        lane = lax.broadcasted_iota(jnp.int32, (SLOT, total), 1)
        mine = (lane >= edge) & (lane < edge + own)

        def guess(m, carry):
            acc = jnp.zeros((SLOT, total), F32)
            for t in range(9):
                value = y_ref[pl.ds(pl.multiple_of(t * BOX_ROWS + m * SLOT, 8), SLOT), :]
                moved = pltpu.roll(value, (-shift[t]) % total, 1)
                acc += moved * mk_ref[0, t : t + 1, :].astype(F32)
            differ = acc - btt_ref[0, m]
            positive = lab_ref[0] >= 0.0
            size = jnp.abs(differ)
            loss = jnp.where(size < HUBER, 0.5 * differ * differ / HUBER, size - 0.5 * HUBER)
            loss = jnp.where(positive & mine, loss, 0.0)
            part = loss[:, 0:256]
            for k in range(1, total // 256):
                part += loss[:, k * 256 : (k + 1) * 256]
            sums_ref[8:16, :] += part[0:8] + part[8:16]
            pull = jnp.minimum(jnp.maximum(differ / HUBER, -1.0), 1.0) * inv_norm
            pull = jnp.where(positive, pull, 0.0)
            gg_ref[pl.ds(pl.multiple_of(m * SLOT, 8), SLOT), :] = pull
            return carry

        lax.fori_loop(0, 4, guess, 0)

    def box_back(gg_ref, xg_ref):
        for t in range(9):
            moved = pltpu.roll(gg_ref[...], shift[t] % total, 1)
            xg_ref[t * BOX_ROWS : (t + 1) * BOX_ROWS, :] = (moved * mk_ref[0, 8 - t : 9 - t, :].astype(F32)).astype(BF)
        dwb_ref[...] += mm(xg_ref[:, edge : edge + own], bt_ref[edge : edge + own, :])

        def into(q, carry):
            row = pl.multiple_of(q * 256, 128)
            grad = mm(xg_ref[:, pl.ds(pl.multiple_of(first_g + row, 128), 256)], wb_ref[...], TN)
            pre = pre_ref[pl.ds(pl.multiple_of(first_g - first_tower + row, 16), 256), C:]
            g_ref[pl.ds(row, 256), C:] = (grad * gelu_slope(pre)).astype(BF)
            return carry

        lax.fori_loop(0, g_cells // 256, into, 0)

    def boxes(gg_ref):
        pl.run_scoped(functools.partial(box_forward, gg_ref), pltpu.VMEM((9 * BOX_ROWS, total), F32))
        pl.run_scoped(functools.partial(box_back, gg_ref), pltpu.VMEM((9 * BOX_ROWS, total), BF))

    pl.run_scoped(boxes, pltpu.VMEM((BOX_ROWS, total), F32))

    def class_back(z_ref):
        z_ref[:, 0:8, :] = jnp.zeros((3, 8, C), F32)
        z_ref[:, 8 + g_cells : 16 + g_cells, :] = jnp.zeros((3, 8, C), F32)
        piece = g_cells // 2

        def multiply(i, carry):
            row = pl.multiple_of(i * piece, 16)
            for k in range(3):
                acc = jnp.zeros((piece, C), F32)
                for r in range(3):
                    t = r * 3 + k
                    source = row + first_g - cols * (r - 1)
                    mask = mx_ref[t, pl.ds(pl.multiple_of(source, 16), piece), :]
                    value = lgs_ref[pl.ds(pl.multiple_of(source - first_logit, 16), piece), :]
                    value = value * jnp.concatenate([mask] * (WIDE // LANE), axis=1)
                    acc += mm(value, wct_ref[:, t * C : t * C + C])
                z_ref[k, pl.ds(pl.multiple_of(8 + row, 8), piece), :] = acc
            return carry

        lax.fori_loop(0, 2, multiply, 0)

        def collect(q, carry):
            row = pl.multiple_of(q * 256, 128)
            grad = z_ref[1, pl.ds(pl.multiple_of(8 + row, 8), 256), :]
            grad += z_ref[0, pl.ds(row, 272), :][9:265] + z_ref[2, pl.ds(row, 272), :][7:263]
            pre = pre_ref[pl.ds(pl.multiple_of(first_g - first_tower + row, 16), 256), :C]
            g_ref[pl.ds(row, 256), :C] = (grad * gelu_slope(pre)).astype(BF)
            return carry

        lax.fori_loop(0, g_cells // 256, collect, 0)

    pl.run_scoped(class_back, pltpu.VMEM((3, g_cells + 16, C), F32))

    def tower_back(z_ref, gt_ref):
        def flip(q, carry):
            row = pl.multiple_of(q * 256, 128)
            part = g_ref[pl.ds(pl.multiple_of(edge - first_g + row, 16), 256), :].astype(F32)
            gt_ref[:, pl.ds(row, 256)] = part.T.astype(BF)
            db_ref[...] += jnp.sum(part, axis=0, keepdims=True)
            return carry

        lax.fori_loop(0, own // 256, flip, 0)
        weight_sums(pl.program_id(0), cols, edge, own, lambda: gt_ref[...], f_ref.at[0], mx_ref, dwt_ref)
        first_z = edge - 16
        piece = own + 32

        def multiply(i, carry):
            row = pl.multiple_of(i * piece, 16)
            for k in range(3):
                acc = jnp.zeros((piece, C), F32)
                for r in range(3):
                    t = r * 3 + k
                    source = row + first_z - cols * (r - 1)
                    mask = mx_ref[t, pl.ds(pl.multiple_of(source, 16), piece), :]
                    value = g_ref[pl.ds(pl.multiple_of(source - first_g, 16), piece), :]
                    value = value * jnp.concatenate([mask] * (2 * C // LANE), axis=1)
                    acc += mm(value, wt_ref[t * C : t * C + C, :], NT)
                z_ref[k, pl.ds(row, piece), :] = acc
            return carry

        lax.fori_loop(0, 1, multiply, 0)

        def collect(q, carry):
            row = pl.multiple_of(q * 256, 128)
            base = pl.multiple_of(row + 8, 8)
            grad = z_ref[1, pl.ds(pl.multiple_of(16 + row, 8), 256), :]
            grad += z_ref[0, pl.ds(base, 272), :][9:265] + z_ref[2, pl.ds(base, 272), :][7:263]
            grad = grad.astype(BF).astype(F32)
            for n in range(2):
                fg_ref[0, n, pl.ds(row, 256), :] = grad[:, n * LANE : n * LANE + LANE]
            return carry

        lax.fori_loop(0, own // 256, collect, 0)

    pl.run_scoped(
        tower_back,
        pltpu.VMEM((3, own + 32, C), F32),
        pltpu.VMEM((2 * C, own), BF),
    )

    @pl.when(pl.program_id(0) == pl.num_programs(0) - 1)
    def _():
        def deliver(class_held, tower_held):
            def turn(t, carry):
                at = pl.multiple_of(t * C, C)
                tower_held[pl.ds(at, C), :] = dwt_ref[0:C, pl.ds(at, C)].astype(BF).T
                tower_held[pl.ds(pl.multiple_of(9 * C + at, C), C), :] = dwt_ref[C:, pl.ds(at, C)].astype(BF).T
                class_held[pl.ds(at, C), :] = dwc_ref[:, pl.ds(at, C)].astype(BF).T
                return carry

            lax.fori_loop(0, 9, turn, 0)
            copies = [
                pltpu.make_async_copy(class_held, class_ref, copy_sems.at[0]),
                pltpu.make_async_copy(tower_held, tower_ref, copy_sems.at[1]),
            ]
            for copy in copies:
                copy.start()
            for copy in copies:
                copy.wait()

        pl.run_scoped(deliver, pltpu.VMEM((9 * C, WIDE), BF), pltpu.VMEM((18 * C, C), BF))


def whole(shape):
    return pl.BlockSpec(shape, lambda *_: (0,) * len(shape))


def shape_of(shape, dtype=F32):
    return jax.ShapeDtypeStruct(shape, dtype)


VM = pl.BlockSpec(memory_space=pltpu.VMEM)
VMEM_LIMIT = 63 * 1024 * 1024


def stem_forward(patches, rim, head):
    canvases, rows, width = patches.shape
    cols = width // PATCH
    pairs = 12
    steps = cols // (2 * pairs)
    chunk = 2 * pairs * PATCH
    count = pairs * canvases * rows
    total = (rows + 2 * HALO) * cols
    return pl.pallas_call(
        functools.partial(stem_kernel, pairs, cols, rows),
        grid=(steps,),
        in_specs=[
            pl.BlockSpec((canvases, rows, chunk), lambda s: (0, 0, s)),
            whole(rim.shape),
            whole(head.shape),
        ],
        out_specs=[
            pl.BlockSpec((count, 2 * C), lambda s: (s, 0)),
            pl.BlockSpec((count, 2 * C), lambda s: (s, 0)),
            whole((canvases, 3, total, C)),
            whole((C, C)),
        ],
        out_shape=[
            shape_of((steps * count, 2 * C)),
            shape_of((steps * count, 2 * C), BF),
            shape_of((canvases, 3, total, C), BF),
            shape_of((C, C), BF),
        ],
        scratch_shapes=[
            pltpu.VMEM((canvases, 2, total + 16, LANE), F32),
            pltpu.VMEM((2 * PATCH, 2 * C), BF),
            pltpu.VMEM((1, 2 * C), F32),
            pltpu.VMEM((1, C), F32),
        ],
        compiler_params=pltpu.CompilerParams(vmem_limit_bytes=VMEM_LIMIT),
        name="stem",
    )(patches, rim, head)


def stem_backward(patches, feature_grad, stem_out, stem_pre, lat_w):
    canvases, rows, width = patches.shape
    cols = width // PATCH
    pairs = 8
    steps = cols // (2 * pairs)
    chunk = 2 * pairs * PATCH
    count = pairs * canvases * rows
    return pl.pallas_call(
        functools.partial(stem_back_kernel, pairs, cols, rows),
        grid=(steps,),
        in_specs=[
            pl.BlockSpec((canvases, rows, chunk), lambda s: (0, 0, s)),
            whole((canvases, 2, rows * cols, LANE)),
            pl.BlockSpec((count, 2 * C), lambda s: (s, 0)),
            pl.BlockSpec((count, 2 * C), lambda s: (s, 0)),
            whole((C, C)),
        ],
        out_specs=whole((TOWER_ROW, C)),
        out_shape=shape_of((TOWER_ROW, C), BF),
        scratch_shapes=[
            pltpu.VMEM((PATCH, C), F32),
            pltpu.VMEM((1, C), F32),
            pltpu.VMEM((C, C), F32),
            pltpu.VMEM((1, C), F32),
            pltpu.VMEM((TOWER_ROW, C), F32),
        ],
        compiler_params=pltpu.CompilerParams(vmem_limit_bytes=VMEM_LIMIT),
        name="stem_back",
    )(patches, feature_grad, stem_out, stem_pre, lat_w)


BOX_CUTS = [(BOX_OUT * n // C, BOX_OUT * n % C) for n in range(64)]


def box_in_kernel(tail_ref, o_ref, t_ref, d_ref, u_ref):
    tail = tail_ref[...].astype(F32)
    count = tail.shape[0]
    lane = lax.broadcasted_iota(jnp.int32, (40, LANE), 1)
    for n in range(2):
        t_ref[n, 0:count, :] = tail[:, n * LANE : n * LANE + LANE]
        t_ref[n, count:, :] = jnp.zeros((t_ref.shape[1] - count, LANE), F32)
    lines = []
    for r in range(9):
        lines.append(jnp.concatenate([t_ref[n, pl.ds(2 + r, 40, stride=9), :] for n in range(2)], axis=1))
    for s, (r, at) in enumerate(BOX_CUTS):
        wide = jnp.concatenate([lines[r], lines[min(r + 1, 8)]], axis=1)
        d_ref[pl.ds(s, 40, stride=64), :] = jnp.where(lane < BOX_OUT, wide[:, at : at + LANE], 0.0)
    for t in range(9):
        turned = d_ref[t * C : t * C + C, :].T
        for n in range(2):
            u_ref[n] = turned[:, n * LANE : n * LANE + LANE]
        for m in range(4):
            here = t * BOX_ROWS + m * SLOT
            parts = [u_ref[n, pl.ds(m, SLOT, stride=4), :] for n in range(2)]
            o_ref[here : here + SLOT, :] = jnp.concatenate(parts, axis=1).astype(BF)


def box_out_kernel(w_ref, b_ref, o_ref, t_ref, d_ref, u_ref):
    u_ref[...] = jnp.zeros_like(u_ref)
    d_ref[9 * C :, :] = jnp.zeros((d_ref.shape[0] - 9 * C, LANE), F32)
    for t in range(9):
        for m in range(4):
            here = t * BOX_ROWS + m * SLOT
            for n in range(2):
                u_ref[n, pl.ds(m, SLOT, stride=4), :] = w_ref[here : here + SLOT, n * LANE : n * LANE + LANE]
        d_ref[t * C : t * C + C, :] = jnp.concatenate([u_ref[0], u_ref[1]], axis=1).T
    lines = [jnp.zeros((40, 2 * C), F32) for _ in range(9)]
    zero = jnp.zeros((40, 2 * C - LANE), F32)
    for s, (r, at) in enumerate(BOX_CUTS):
        wide = jnp.concatenate([d_ref[pl.ds(s, 40, stride=64), :], zero], axis=1)
        lines[r] = lines[r] + (pltpu.roll(wide, at, 1) if at else wide)
    t_ref[...] = jnp.zeros_like(t_ref)
    for r in range(9):
        line = lines[r][:, :C]
        if r:
            line = line + lines[r - 1][:, C:]
        for n in range(2):
            t_ref[n, pl.ds(2 + r, 40, stride=9), :] = line[:, n * LANE : n * LANE + LANE]
    for n in range(2):
        for k in range(2):
            at = k * C + n * LANE
            t_ref[n, k : k + 1, :] = b_ref[:, at : at + LANE]
    rows = o_ref.shape[0]
    o_ref[...] = jnp.concatenate([t_ref[0, 0:rows, :], t_ref[1, 0:rows, :]], axis=1).astype(BF)


def box_call(kernel, shape, kind, name, *args):
    return pl.pallas_call(
        kernel,
        in_specs=[VM] * len(args),
        out_specs=VM,
        out_shape=shape_of(shape, kind),
        scratch_shapes=[
            pltpu.VMEM((2, 368, LANE), F32),
            pltpu.VMEM((40 * 64, LANE), F32),
            pltpu.VMEM((2, LANE, LANE), F32),
        ],
        compiler_params=pltpu.CompilerParams(vmem_limit_bytes=VMEM_LIMIT),
        name=name,
    )(*args)


def heads_call(rows, cols, scal, feats, masks, labels, box_target, full, tb, head, wb):
    canvases = feats.shape[0]
    own = rows * cols
    total = own + 2 * HALO * cols
    spread = jnp.repeat(jnp.eye(SLOT, 9, dtype=BF), LANE, axis=1)

    def per(shape):
        return pl.BlockSpec((1,) + shape, lambda c: (c,) + (0,) * len(shape))

    return pl.pallas_call(
        functools.partial(head_kernel, cols, rows),
        grid=(canvases,),
        in_specs=[
            pl.BlockSpec(memory_space=pltpu.SMEM),
            per((3, total, C)),
            per((SLOT, total)),
            per((SLOT, total)),
            per((4, SLOT, total)),
            whole(spread.shape),
            pl.BlockSpec(memory_space=pl.ANY),
            whole(tb.shape),
            pl.BlockSpec(memory_space=pl.ANY),
            whole(wb.shape),
        ],
        out_specs=[
            pl.BlockSpec(memory_space=pl.ANY),
            pl.BlockSpec(memory_space=pl.ANY),
            whole((9 * BOX_ROWS, C)),
            whole((1, 2 * C)),
            per((2, own, LANE)),
            whole((16, 256)),
        ],
        out_shape=[
            shape_of((9 * C, WIDE), BF),
            shape_of((18 * C, C), BF),
            shape_of((9 * BOX_ROWS, C)),
            shape_of((1, 2 * C)),
            shape_of((canvases, 2, own, LANE)),
            shape_of((16, 256)),
        ],
        scratch_shapes=[
            pltpu.VMEM((9, total, LANE), BF),
            pltpu.VMEM((total - 2 * cols, 2 * C), F32),
            pltpu.VMEM((total, C), BF),
            pltpu.VMEM((WIDE, own + 512), BF),
            pltpu.VMEM((own + 512, WIDE), BF),
            pltpu.VMEM((own + 256, 2 * C), BF),
            pltpu.VMEM((9 * C, 2 * C), BF),
            pltpu.VMEM((WIDE, 9 * C), BF),
            pltpu.VMEM((WIDE, 9 * C), F32),
            pltpu.VMEM((2 * C, 9 * C), F32),
            pltpu.SemaphoreType.DMA((3,)),
        ],
        compiler_params=pltpu.CompilerParams(vmem_limit_bytes=VMEM_LIMIT),
        name="heads",
    )(scal, feats, masks, labels, box_target, spread, full, tb, head, wb)


def place():
    img = lax.axis_index("img")
    cls = lax.axis_index("cls")
    return img // 2, img % 2, cls // 2, cls % 2


def target(z, y, x, c):
    return (z * 2 + y, x * 2 + c)


def owner(z, y, x, c):
    return ((z * 2 + y) * 2 + x) * 2 + c


def enter(peers):
    barrier = pltpu.get_barrier_semaphore()
    for peer in peers:
        pl.semaphore_signal(barrier, inc=1, device_id=peer, device_id_type=MESH)
    pl.semaphore_wait(barrier, len(peers))


class Mail:
    def __init__(self, send_sems, recv_sems):
        self.send_sems, self.recv_sems, self.used, self.sent = send_sems, recv_sems, 0, []

    def push(self, source, landing, peer):
        copy = pltpu.make_async_remote_copy(
            src_ref=source,
            dst_ref=landing,
            send_sem=self.send_sems.at[self.used],
            recv_sem=self.recv_sems.at[self.used],
            device_id=peer,
            device_id_type=MESH,
        )
        self.used += 1
        copy.start()
        self.sent.append(copy)
        return copy

    def close(self):
        for copy in self.sent:
            copy.wait_send()


def window_row(index, shard):
    return pl.multiple_of((index * shard + LEAD * C) // (16 * C) * 16, 16)


def gather_kernel(shard, s_ref, k_ref, n_ref, r_ref, full_ref, head_ref, all_ref, first_ref, last_ref, rim_ref, count_ref, sh_ref, kx_ref, send_sems, recv_sems):
    z, y, x, c = place()
    block = k_ref.shape[0]
    win = s_ref.shape[0]
    others = [(k, j) for k in range(4) for j in range(2) if k or j]
    ring = [((z + k) % 4, (y + j) % 2) for k, j in others]
    line = [(z * 2 + y, (x * 2 + c + step) % 4) for step in (1, 3)]
    enter([target(zz, yy, x, c) for zz, yy in ring] + [target(z, y, 1 - x, c), target(z, y, x, 1 - c)] + line)
    mail = Mail(send_sems, recv_sems)
    me = owner(z, y, x, c)

    def rows(zz, yy):
        return pl.ds(pl.multiple_of((zz * 2 + yy) * block, 16), block)

    def lanes(cc):
        return pl.ds(pl.multiple_of(cc * HALF, LANE), HALF)

    got_kx = mail.push(k_ref, kx_ref, target(z, y, 1 - x, c))
    counts = [mail.push(n_ref, count_ref.at[z * 2 + y], target(zz, yy, x, c)) for zz, yy in ring]
    slot = sh_ref.at[me]
    got_z = [mail.push(s_ref, slot, target((z + k) % 4, y, x, c)) for k in range(1, 4)]
    got_y = [mail.push(s_ref, slot, target(z, 1 - y, x, c))]
    got_x = [mail.push(s_ref, slot, target(z, y, 1 - x, c))]
    got_c = [mail.push(s_ref, slot, target(z, y, x, 1 - c))]
    rims = [mail.push(r_ref.at[n], rim_ref.at[n], line[n]) for n in range(2)]
    count_ref[z * 2 + y] = n_ref[...]
    sh_ref[me] = s_ref[...]

    got_kx.wait_recv()
    mine = head_ref.at[rows(z, y), lanes(c)]
    head_ref[rows(z, y), lanes(c)] = k_ref[...] + kx_ref[...]
    got_kz = [mail.push(mine, mine, target((z + k) % 4, y, x, c)) for k in range(1, 4)]
    got_ky = [mail.push(mine, mine, target(z, 1 - y, x, c))]
    got_kc = [mail.push(mine, mine, target(z, y, x, 1 - c))]

    for k in range(1, 4):
        got_z[k - 1].wait_recv()
        slot = sh_ref.at[owner((z + 4 - k) % 4, y, x, c)]
        got_y.append(mail.push(slot, slot, target(z, 1 - y, x, c)))
        got_x.append(mail.push(slot, slot, target(z, y, 1 - x, c)))
        got_c.append(mail.push(slot, slot, target(z, y, x, 1 - c)))
    for k in range(1, 4):
        got_kz[k - 1].wait_recv()
        part = head_ref.at[rows((z + 4 - k) % 4, y), lanes(c)]
        got_ky.append(mail.push(part, part, target(z, 1 - y, x, c)))
        got_kc.append(mail.push(part, part, target(z, y, x, 1 - c)))
    for k in range(4):
        got_y[k].wait_recv()
        slot = sh_ref.at[owner((z + 4 - k) % 4, 1 - y, x, c)]
        got_x.append(mail.push(slot, slot, target(z, y, 1 - x, c)))
        got_c.append(mail.push(slot, slot, target(z, y, x, 1 - c)))
    for k in range(4):
        got_ky[k].wait_recv()
        part = head_ref.at[rows((z + 4 - k) % 4, 1 - y), lanes(c)]
        got_kc.append(mail.push(part, part, target(z, y, x, 1 - c)))
    for k in range(8):
        got_x[k].wait_recv()
        slot = sh_ref.at[owner((z + 4 - k % 4) % 4, (y + k // 4) % 2, 1 - x, c)]
        got_c.append(mail.push(slot, slot, target(z, y, x, 1 - c)))
    for copy in got_c + got_kc + counts + rims:
        copy.wait_recv()
    all_ref[...] = jnp.sum(count_ref[...], axis=0)
    full_ref[...] = jnp.zeros_like(full_ref)

    def merge(d, carry):
        full_ref[pl.ds(window_row(d, shard), win), :] += sh_ref[d]
        return carry

    lax.fori_loop(0, 32, merge, 0)
    first_ref[...] = full_ref[0:TOWER_ROW, :]
    last_ref[...] = full_ref[TAIL_ROW:FULL_ROWS, :]
    mail.close()


def scatter_kernel(
    shard, head_ref, tower_ref, tail_ref, k_ref, n_ref, s_out, k_out, n_out,
    full_ref, sc_ref, sx_ref, sy_ref, sz_ref, kc_ref, ky_ref, kz_ref, kx_ref, mine_ref, peer_ref, far_ref, nz_ref, send_sems, recv_sems,
):
    z, y, x, c = place()
    block = kx_ref.shape[1]
    win = s_out.shape[0]
    enter([target((z + k) % 4, y, x, c) for k in range(1, 4)] + [target(z, 1 - y, x, c), target(z, y, 1 - x, c), target(z, y, x, 1 - c)])
    mail = Mail(send_sems, recv_sems)

    def rows(zz, yy):
        return pl.ds(pl.multiple_of((zz * 2 + yy) * block, 16), block)

    def lanes(cc):
        return pl.ds(pl.multiple_of(cc * HALF, LANE), HALF)

    def window(zz, yy, xx, cc):
        return pl.ds(window_row(owner(zz, yy, xx, cc), shard), win)

    mine_ref[0] = n_ref[...]
    sum_c = mail.push(mine_ref.at[0], peer_ref.at[0], target(z, y, x, 1 - c))
    spots = [(j, k) for j in (1, 0) for k in (1, 2, 3, 0)]
    got_kc = []
    for n, (j, k) in enumerate(spots):
        part = k_ref.at[rows((z + k) % 4, (y + j) % 2), lanes(1 - c)]
        got_kc.append(mail.push(part, kc_ref.at[n], target(z, y, x, 1 - c)))
    full_ref[0:TOWER_ROW, :] = head_ref[...]
    full_ref[TOWER_ROW:TAIL_ROW, :] = tower_ref[...]
    full_ref[TAIL_ROW:FULL_ROWS, :] = tail_ref[...]
    got_c = []
    for i in (1, 0):
        for n, (j, k) in enumerate(spots):
            part = full_ref.at[window((z + k) % 4, (y + j) % 2, (x + i) % 2, 1 - c), :]
            got_c.append(mail.push(part, sc_ref.at[(1 - i) * 8 + n], target(z, y, x, 1 - c)))

    sum_c.wait_recv()
    mine_ref[1] = mine_ref[0] + peer_ref[0]
    sum_x = mail.push(mine_ref.at[1], peer_ref.at[1], target(z, y, 1 - x, c))

    got_ky = []
    for n, (j, k) in enumerate(spots):
        got_kc[n].wait_recv()
        kc_ref[n] = kc_ref[n] + k_ref[rows((z + k) % 4, (y + j) % 2), lanes(c)]
        if j == 1:
            got_ky.append(mail.push(kc_ref.at[n], ky_ref.at[n], target(z, 1 - y, x, c)))
    got_x = []
    for n, (j, k) in enumerate(spots):
        got_c[n].wait_recv()
        sc_ref[n] = sc_ref[n] + full_ref[window((z + k) % 4, (y + j) % 2, 1 - x, c), :]
        got_x.append(mail.push(sc_ref.at[n], sx_ref.at[n], target(z, y, 1 - x, c)))

    sum_x.wait_recv()
    mine_ref[2] = mine_ref[1] + peer_ref[1]
    sum_y = mail.push(mine_ref.at[2], peer_ref.at[2], target(z, 1 - y, x, c))

    got_kz = []
    for n in range(4):
        got_ky[n].wait_recv()
        kc_ref[4 + n] = kc_ref[4 + n] + ky_ref[n]
        if n < 3:
            got_kz.append(mail.push(kc_ref.at[4 + n], kz_ref.at[n], target((z + n + 1) % 4, y, x, c)))
    got_y = []
    for n, (j, k) in enumerate(spots):
        got_c[8 + n].wait_recv()
        got_x[n].wait_recv()
        total = sc_ref[8 + n].astype(F32) + full_ref[window((z + k) % 4, (y + j) % 2, x, c), :].astype(F32)
        sc_ref[8 + n] = (total + sx_ref[n].astype(F32)).astype(BF)
        if j == 1:
            got_y.append(mail.push(sc_ref.at[8 + n], sy_ref.at[n], target(z, 1 - y, x, c)))

    sum_y.wait_recv()
    mine_ref[3] = mine_ref[2] + peer_ref[2]
    nz_ref[z] = mine_ref[3]
    sum_z = [mail.push(mine_ref.at[3], nz_ref.at[z], target((z + k) % 4, y, x, c)) for k in range(1, 4)]

    total = kc_ref[7].astype(F32)
    for n in range(3):
        got_kz[n].wait_recv()
        total += kz_ref[n].astype(F32)
    kx_ref[0] = total.astype(BF)
    got_kx = mail.push(kx_ref.at[0], kx_ref.at[1], target(z, y, 1 - x, c))
    got_z = []
    for n in range(4):
        got_y[n].wait_recv()
        sc_ref[12 + n] = sc_ref[12 + n] + sy_ref[n]
        if n < 3:
            got_z.append(mail.push(sc_ref.at[12 + n], sz_ref.at[n], target((z + n + 1) % 4, y, x, c)))
    total = sc_ref[15].astype(F32)
    for n in range(3):
        got_z[n].wait_recv()
        total += sz_ref[n].astype(F32)
    s_out[...] = total
    for copy in sum_z:
        copy.wait_recv()
    n_out[...] = (nz_ref[0] + nz_ref[1]) + (nz_ref[2] + nz_ref[3])
    got_kx.wait_recv()
    k_out[...] = kx_ref[0].astype(F32) + kx_ref[1].astype(F32)
    mail.close()


def fast_mesh(img_parts, cls_parts, class_rows):
    return img_parts == 8 and cls_parts == 4 and class_rows % 16 == 0


def flat_place(index, shard):
    return (index * shard + LEAD * C) % (16 * C)


def gather_all(shared_params, class_params, count, edges):
    img, cls = lax.axis_index("img"), lax.axis_index("cls")
    img_parts, cls_parts = lax.axis_size("img"), lax.axis_size("cls")
    shard = shared_params.shape[0]
    block, part = class_params.shape
    if not fast_mesh(img_parts, cls_parts, block):
        flat = lax.all_gather(shared_params.astype(BF), ("img", "cls"), axis=0, tiled=True)
        full = jnp.pad(flat, (LEAD * C, FULL_ROWS * C - LEAD * C - flat.shape[0])).reshape(FULL_ROWS, C)
        head = lax.all_gather(class_params.astype(BF), ("img", "cls"), axis=0)
        head = head.reshape(img_parts, cls_parts, block, part).transpose(0, 2, 1, 3).reshape(-1, CLS_OUT)
        pieces = []
        for half in range(2):
            pieces += [head[:, 180 * half : 180 * half + 180], head[:, 360 + 180 * half : 540 + 180 * half]]
            pieces.append(jnp.zeros((head.shape[0], HALF - 360), BF))
        ways = [[(i, (i + step) % cls_parts) for i in range(cls_parts)] for step in (1, cls_parts - 1)]
        rim = jnp.stack([lax.ppermute(edges[n], "cls", ways[n]) for n in range(2)])
        return full, full[:TOWER_ROW], full[TAIL_ROW:], jnp.concatenate(pieces, axis=1), lax.psum(count, "img"), rim
    rows = -(-(shard + 16 * C) // (16 * C)) * 16
    window = lax.dynamic_update_slice(
        jnp.zeros((rows * C,), BF), shared_params.astype(BF), (flat_place(img * cls_parts + cls, shard),)
    ).reshape(rows, C)
    wide = jnp.pad(class_params.astype(BF), ((0, 0), (part, HALF - part)))
    wide = lax.dynamic_slice_in_dim(
        jnp.pad(wide, ((0, 0), (0, part))), jnp.where(cls // 2 == 0, part, 0), HALF, 1
    )
    number = jnp.broadcast_to(count, (8, LANE))
    full, head, counts, first, last, rim = pl.pallas_call(
        functools.partial(gather_kernel, shard),
        in_specs=[VM] * 4,
        out_specs=[VM] * 6,
        out_shape=[
            shape_of((FULL_ROWS, C), BF),
            shape_of((img_parts * block, 2 * HALF), BF),
            shape_of((8, LANE)),
            shape_of((TOWER_ROW, C), BF),
            shape_of((FULL_ROWS - TAIL_ROW, C), BF),
            shape_of(edges.shape, BF),
        ],
        scratch_shapes=[
            pltpu.VMEM((img_parts, 8, LANE), F32),
            pltpu.VMEM((img_parts * cls_parts, rows, C), BF),
            pltpu.VMEM((block, HALF), BF),
            pltpu.SemaphoreType.DMA((56,)),
            pltpu.SemaphoreType.DMA((56,)),
        ],
        compiler_params=pltpu.CompilerParams(collective_id=0, has_side_effects=True, vmem_limit_bytes=VMEM_LIMIT),
        name="gather",
    )(window, wide, number, edges)
    return full, first, last, head, counts[0, 0], rim


def scatter_all(head, tower, tail, class_grad, sums, shard, block, part):
    img, cls = lax.axis_index("img"), lax.axis_index("cls")
    img_parts, cls_parts = lax.axis_size("img"), lax.axis_size("cls")
    if not fast_mesh(img_parts, cls_parts, block):
        flat = jnp.concatenate([head, tower, tail], axis=0).reshape(-1)
        flat = flat[LEAD * C : LEAD * C + shard * img_parts * cls_parts].astype(F32)
        shared = lax.psum_scatter(flat, ("img", "cls"), scatter_dimension=0, tiled=True)
        pieces = [class_grad[:, at : at + 180] for at in (0, HALF, 180, HALF + 180)]
        whole_grad = lax.psum_scatter(
            jnp.concatenate(pieces, axis=1).astype(F32), "img", scatter_dimension=0, tiled=True
        )
        return shared, lax.psum_scatter(whole_grad, "cls", scatter_dimension=1, tiled=True), lax.psum(sums, ("img", "cls"))
    rows = -(-(shard + 16 * C) // (16 * C)) * 16
    window, wide, sums = pl.pallas_call(
        functools.partial(scatter_kernel, shard),
        in_specs=[VM] * 5,
        out_specs=[VM] * 3,
        out_shape=[shape_of((rows, C)), shape_of((block, HALF)), shape_of(sums.shape)],
        scratch_shapes=[
            pltpu.VMEM((FULL_ROWS, C), BF),
            pltpu.VMEM((16, rows, C), BF),
            pltpu.VMEM((8, rows, C), BF),
            pltpu.VMEM((4, rows, C), BF),
            pltpu.VMEM((3, rows, C), BF),
            pltpu.VMEM((8, block, HALF), BF),
            pltpu.VMEM((4, block, HALF), BF),
            pltpu.VMEM((3, block, HALF), BF),
            pltpu.VMEM((2, block, HALF), BF),
            pltpu.VMEM((4,) + sums.shape, F32),
            pltpu.VMEM((3,) + sums.shape, F32),
            pltpu.VMEM((8, LANE), F32),
            pltpu.VMEM((4,) + sums.shape, F32),
            pltpu.SemaphoreType.DMA((53,)),
            pltpu.SemaphoreType.DMA((53,)),
        ],
        compiler_params=pltpu.CompilerParams(collective_id=1, has_side_effects=True, vmem_limit_bytes=VMEM_LIMIT),
        name="scatter",
    )(head, tower, tail, class_grad, sums)
    flat = lax.dynamic_slice_in_dim(window.reshape(-1), flat_place(img * cls_parts + cls, shard), shard)
    grad = lax.dynamic_slice_in_dim(wide, jnp.where(cls // 2 == 0, 0, part), part, 1)
    grad = lax.optimization_barrier(grad.T).T
    return flat, grad, sums


def column_plan():
    plan = []
    for half in range(2):
        for group in range(2):
            column, row, end = 360 * group + 180 * half, HALF * half + 180 * group, 360 * group + 180 * half + 180
            while column < end:
                count = min(end, (column // CLASSES + 1) * CLASSES) - column
                plan.append((row, count, column // CLASSES, column % CLASSES))
                column, row = column + count, row + count
        plan.append((HALF * half + 360, HALF - 360, -1, 0))
    return plan


def adamw_update(weight, first, second, grad):
    first_new = MOMENT_ONE * first + (1.0 - MOMENT_ONE) * grad
    second_new = MOMENT_TWO * second + (1.0 - MOMENT_TWO) * grad * grad
    first_hat = first_new / (1.0 - MOMENT_ONE**STEP)
    second_hat = second_new / (1.0 - MOMENT_TWO**STEP)
    weight_new = weight - RATE * (first_hat / (jnp.sqrt(second_hat) + EPSILON) + DECAY * weight)
    return (weight_new, first_new, second_new)


def valid_positives(boxes, match, full_rows, cols):
    place = jnp.arange(full_rows * cols, dtype=jnp.int32)
    row, col = place // cols, place % cols
    inside = jnp.zeros((boxes.shape[0], full_rows * cols), bool)
    for k in range(boxes.shape[1]):
        edge = boxes[:, k, :, None]
        inside |= (row >= edge[:, 0]) & (row < edge[:, 2]) & (col >= edge[:, 1]) & (col < edge[:, 3])
    return ((match >= 0) & inside[:, None]).astype(F32)


def cell_data(boxes, match, gt_labels, gt_deltas, first_row, rows, cols):
    full_rows = match.shape[2] // cols
    total = (rows + 2 * HALO) * cols
    place = jnp.arange(total, dtype=jnp.int32)[None]
    row = place // cols + (first_row - HALO)
    col = place % cols

    def crop(r, j):
        found = jnp.full((boxes.shape[0], total), -1, jnp.int32)
        for k in range(boxes.shape[1]):
            edge = boxes[:, k, :, None]
            inside = (r >= edge[:, 0]) & (r < edge[:, 2]) & (j >= edge[:, 1]) & (j < edge[:, 3])
            found = jnp.where(inside, k, found)
        return jnp.where((r >= 0) & (r < full_rows) & (j >= 0) & (j < cols), found, -1)

    centre = crop(row, col)
    valid = centre >= 0
    masks = jnp.stack([(crop(row + di, col + dj) == centre) & valid for di, dj in TAPS], axis=1)
    masks = jnp.pad(masks.astype(BF), ((0, 0), (0, SLOT - 9), (0, 0)))
    edge = HALO * cols
    near = jnp.pad(match, ((0, 0), (0, 0), (edge, edge)), constant_values=-2)
    near = lax.dynamic_slice_in_dim(near, first_row * cols, total, 2)
    near = jnp.where(valid[:, None], near, -2)
    near = jnp.pad(near, ((0, 0), (0, SLOT - 9), (0, 0)), constant_values=-2)
    labels = near
    targets = jnp.zeros((near.shape[0], 4) + near.shape[1:], F32)
    for g in range(gt_labels.shape[1]):
        labels = jnp.where(near == g, gt_labels[:, g, None, None], labels)
        targets = jnp.where((near == g)[:, None], gt_deltas[:, g, :, None, None], targets)
    return masks, labels.astype(F32), targets


def local(patches, boxes, match, gt_labels, gt_deltas, ema_old, shared_params, shared_m, shared_v, class_params, class_m, class_v):
    cls_rank = lax.axis_index("cls")
    canvases, rows, width = patches.shape
    cols = width // PATCH
    masks, labels, targets = cell_data(boxes, match, gt_labels, gt_deltas, cls_rank * rows, rows, cols)
    full_rows = match.shape[2] // cols
    count = jnp.sum(valid_positives(boxes, match, full_rows, cols))
    edges = jnp.stack([patches[:, rows - HALO :], patches[:, :HALO]]).reshape(2, canvases * HALO, width)
    edges = jnp.concatenate([edges[..., : width // 2], edges[..., width // 2 :]], axis=1)
    full, first, last, head, positives, rim = gather_all(shared_params, class_params, count, edges)
    norm = jnp.maximum(positives, 1.0)
    ema_new = EMA_KEEP * ema_old + (1.0 - EMA_KEEP) * norm
    tb = last[0:2].reshape(1, 2 * C).astype(F32)
    wb = box_call(box_in_kernel, (9 * BOX_ROWS, C), BF, "box_in", last)
    stem_pre, stem_out, feats, lat_w = stem_forward(patches, rim, first)
    scal = jnp.stack([1.0 / ema_new, 1.0 / norm])
    class_grad, tower_grad, dwb, db, feature_grad, sums = heads_call(
        rows, cols, scal, feats, masks, labels, targets, full, tb, head, wb
    )
    first_grad = stem_backward(patches, feature_grad, stem_out, stem_pre, lat_w)
    last_grad = box_call(box_out_kernel, last.shape, BF, "box_out", dwb, db)
    shared_grad, class_grad, sums = scatter_all(
        first_grad, tower_grad, last_grad, class_grad, sums, shared_params.shape[0], *class_params.shape
    )
    loss = jnp.sum(sums[0:8]) / ema_new + jnp.sum(sums[8:16]) / norm
    return (
        loss,
        ema_new,
        *adamw_update(shared_params, shared_m, shared_v, shared_grad),
        *adamw_update(class_params, class_m, class_v, class_grad),
    )


def solution(mesh):
    spread = P(("img", "cls"))
    block = P("img", "cls")
    return jax.shard_map(
        local,
        mesh=mesh,
        in_specs=(
            P("img", "cls", None),
            P("img", None, None),
            P("img", None, None),
            P("img", None),
            P("img", None, None),
            P(),
            spread,
            spread,
            spread,
            block,
            block,
            block,
        ),
        out_specs=(P(), P(), spread, spread, spread, block, block, block),
        check_vma=False,
    )
```
